128 devices in a mesh: gx: 8 (over z, core), gy: 16 (over y, x).
Axes of the slice: x: 4, y: 4, z: 4, core: 2. Of those that a mesh axis runs over, the one named last changes fastest.
Arguments:
- e_adjoint: float32 [3, 256, 640, 128], P(None, 'gx', 'gy'), may hold values from -6 to 6
- h_adjoint: float32 [3, 256, 640, 128], P(None, 'gx', 'gy'), may hold values from -6 to 6
- conductivity: float32 [256, 640, 128], P('gx', 'gy'), may hold values from 0.05 to 2
- permittivity: float32 [256, 640, 128], P('gx', 'gy'), may hold values from 1 to 4
- forward_e: bfloat16 [3, 3, 256, 640, 128], P(None, None, 'gx', 'gy'), may hold values from -6 to 6
- receiver_data: float32 [131072, 128], P(('gx', 'gy')), may hold values from -6 to 6
- receiver_tile: int32 [131072, 1], P(('gx', 'gy')), may hold values from 0 to 127; in each aligned block of 1024 rows (0 to 1023, 1024 to 2047, ...) at most 24 rows name the same one
- receiver_cell: int32 [131072], P(('gx', 'gy')), may hold values from 0 to 163839
- receiver_comp: int32 [131072], P(('gx', 'gy')), may hold values from 0 to 2
Outputs:
- e_final: float32 [3, 256, 640, 128], P(None, 'gx', 'gy')
- h_final: float32 [3, 256, 640, 128], P(None, 'gx', 'gy')
- grad_sigma: float32 [256, 640, 128], P('gx', 'gy')
The draws below stay inside these ranges and needn't reach their ends.
Inputs may be any that keep to these rules, and one draw needn't show every extreme that they name: `receiver_tile`: among the rows of one device, no tile is named by more than 24 rows.
All inputs are finite; a program needn't handle non-finite values.
Results may differ from the reference program's by a relative error of at most 0.0003.
Values sent between devices are 32-bit elements; how exact they have to be, the bound alone decides.
A program may use at most 128 MiB of HBM per device.

```python
import math
import jax
import jax.numpy as jnp
import numpy as np
from jax import lax

CX = 32
CY = 40
NZ = 128
STEPS = 3
SAMPLES = 128
REC_DEV = 1024
NX = 256
NY = 640
RECEIVERS = 131072
CAP = 24
N_GY = 16
DEVICES = 128


def plant(values, key, least, high):
    longest = values.shape.index(max(values.shape))
    spots = []
    for shift in (0, 1):
        where = [jax.random.randint(jax.random.fold_in(key, axis), (), 0, length) for axis, length in enumerate(values.shape)]
        where[longest] = (where[longest] + shift) % values.shape[longest]
        spots.append(tuple(where))
    return values.at[spots[0]].set(least).at[spots[1]].set(high)


def block_levels(own_key, shape, cuts, least, top_value):
    def one(axis_at, blocks):
        draws = jax.random.uniform(jax.random.fold_in(jax.random.fold_in(own_key, 6), axis_at), (blocks,), jnp.float32, least / len(cuts), top_value / len(cuts))
        return jnp.repeat(jnp.exp(draws), shape[axis_at] // blocks).reshape((-1,) + (1,) * (len(shape) - axis_at - 1))

    loudness = one(*cuts[0])
    for cut in cuts[1:]:
        loudness = loudness * one(*cut)
    return loudness


def deal_out(key, own, number, rows, count, top, limit, lean):
    sequence = jax.random.permutation(key, count)
    packed, ordinary = shares(count, rows * top, limit, lean, True), shares(count, rows * top, limit, lean, False)
    places = jnp.arange(count)

    def named(lengths, offset_by):
        used = int((lengths > 0).sum())
        fixed = max(1, used // 4)
        passed = fixed + (places - fixed + offset_by * (used - fixed)) % max(1, count - fixed)
        return jnp.zeros((count,), jnp.int32).at[sequence[jnp.where(places < fixed, places, passed)]].set(jnp.asarray(lengths, jnp.int32))

    lengths = jnp.where(number % 4 == 0, named(packed, number // 4), named(ordinary, number - number // 4 - 1))
    mixed = jax.random.permutation(jax.random.fold_in(own, 3), count)
    giver, taker = mixed[0:count // 2 * 2:2], mixed[1:count // 2 * 2:2]
    margin = jnp.minimum(lengths[giver] - 1, limit - lengths[taker]) // 2
    margin = jnp.where((giver == sequence[0]) | (taker == sequence[0]) | (lengths[taker] == 0), 0, jnp.maximum(margin, 0))
    passed = jax.random.randint(jax.random.fold_in(own, 4), (count // 2,), 0, 1 << 20) % (margin + 1)
    lengths = lengths.at[giver].add(-passed).at[taker].add(passed)
    labels = jnp.searchsorted(jnp.cumsum(lengths), jnp.arange(rows * top), side="right").astype(jnp.int32)
    grid = labels.reshape(top, rows).T
    grid = grid[jax.random.permutation(jax.random.fold_in(own, 1), rows)]
    offset_by = jax.random.randint(jax.random.fold_in(own, 2), (rows, 1), 0, top)
    return jnp.take_along_axis(grid, (jnp.arange(top)[None, :] + offset_by) % top, axis=1)


def shares(count, total, limit, lean, full):
    portions = [(1 << 20) // math.isqrt(grade ** lean) + 1 for grade in range(1, count + 1)]
    largest = limit if full else min(limit, max(-(-total // count), total * portions[0] // sum(portions)))
    least = 1 if total - largest >= count - 1 else 0
    counts, surplus = [largest] + [least] * (count - 1), total - largest - least * (count - 1)
    while surplus > 0:
        free = [i for i in range(1, count) if counts[i] < largest] or [i for i in range(1, count) if counts[i] < limit]
        pool, left = sum([portions[i] for i in free]), surplus
        for i in free:
            more = min(limit - counts[i], max(1, left * portions[i] // pool), surplus)
            counts[i] = counts[i] + more
            surplus = surplus - more
    return np.array(counts)


def centred(stream_key, shape, scale, most, shards=(), held_as=jnp.bfloat16):
    factor_of = block_levels(stream_key, shape, shards, -0.22, 0.18) if shards else 1.0
    array = jax.random.normal(stream_key, shape, jnp.float32) * scale * factor_of
    return jnp.minimum(jnp.maximum(array, -most), most).astype(held_as)


def setup_inputs(seed: int = 0) -> dict:
    streams_of = jax.random.split(jax.random.key(seed), 10)
    e_adjoint = centred(streams_of[0], (3, NX, NY, NZ), 1.0, 6.0, ((1, 8), (2, 16)), jnp.float32)
    h_adjoint = centred(streams_of[1], (3, NX, NY, NZ), 1.0, 6.0, ((1, 8), (2, 16)), jnp.float32)
    conductivity = jnp.clip(jnp.exp(math.log(2.0) - 3.6888794 * jax.random.uniform(streams_of[2], (NX, NY, NZ), jnp.float32) ** block_levels(streams_of[2], (NX, NY, NZ), ((0, 8), (1, 16)), -0.2, 0.2)), 0.05, 2.0)
    permittivity = jnp.clip(jnp.exp(math.log(4.0) - 1.3862944 * jax.random.uniform(streams_of[3], (NX, NY, NZ), jnp.float32) ** block_levels(streams_of[3], (NX, NY, NZ), ((0, 8), (1, 16)), -0.2, 0.2)), 1.0, 4.0)
    forward_e = centred(streams_of[4], (STEPS, 3, NX, NY, NZ), 1.0, 6.0, ((2, 8), (3, 16)))
    receiver_data = centred(streams_of[5], (RECEIVERS, SAMPLES), 1.0, 6.0, ((0, 128),), jnp.float32)
    receiver_tile_keys = jax.random.split(jax.random.fold_in(streams_of[6], 1), RECEIVERS // REC_DEV)
    receiver_tile_turns = jax.random.permutation(jax.random.fold_in(streams_of[6], 3), RECEIVERS // REC_DEV)
    receiver_tile = jax.vmap(lambda own, number: deal_out(jax.random.fold_in(streams_of[6], 2), own, number, REC_DEV, DEVICES, 1, CAP, 2))(receiver_tile_keys, receiver_tile_turns).reshape((RECEIVERS, 1))
    receiver_cell = plant(jax.random.randint(streams_of[7], (RECEIVERS,), 0, CX * CY * NZ), jax.random.fold_in(streams_of[7], 1), 0, (CX * CY * NZ) - 1).astype(jnp.int32)
    receiver_comp = plant(jax.random.randint(streams_of[8], (RECEIVERS,), 0, 3), jax.random.fold_in(streams_of[8], 1), 0, 2).astype(jnp.int32)
    return {"e_adjoint": e_adjoint, "h_adjoint": h_adjoint, "conductivity": conductivity, "permittivity": permittivity, "forward_e": forward_e, "receiver_data": receiver_data, "receiver_tile": receiver_tile, "receiver_cell": receiver_cell, "receiver_comp": receiver_comp}


time_step = 0.55

def time_kernel():
    sample = jnp.arange(SAMPLES).astype(jnp.float32)
    centre = (jnp.arange(STEPS).astype(jnp.float32)[:, None] + 0.5) * (SAMPLES / STEPS)
    spread = SAMPLES / (4.0 * STEPS)
    kernel = jnp.exp(-jnp.square((sample[None, :] - centre) / spread))
    return kernel / jnp.sqrt(lax.optimization_barrier(jnp.sum(kernel * kernel, axis=1, keepdims=True)))

def forward_diff(field, after, axis):
    joined = jnp.concatenate([field, after], axis=axis)
    return lax.slice_in_dim(joined, 1, joined.shape[axis], axis=axis) - field

def backward_diff(field, before, axis):
    joined = jnp.concatenate([before, lax.slice_in_dim(field, 0, field.shape[axis] - 1, axis=axis)], axis=axis)
    return field - joined

def curl_e(field, after_x, after_y):
    zplane = jnp.zeros_like(field[0][:, :, :1])
    cx = forward_diff(field[2], after_y[1], 1) - forward_diff(field[1], zplane, 2)
    cy = forward_diff(field[0], zplane, 2) - forward_diff(field[2], after_x[1], 0)
    cz = forward_diff(field[1], after_x[0], 0) - forward_diff(field[0], after_y[0], 1)
    return jnp.stack([cx, cy, cz])

def curl_h(field, before_x, before_y):
    zplane = jnp.zeros_like(field[0][:, :, :1])
    cx = backward_diff(field[2], before_y[1], 1) - backward_diff(field[1], zplane, 2)
    cy = backward_diff(field[0], zplane, 2) - backward_diff(field[2], before_x[1], 0)
    cz = backward_diff(field[1], before_x[0], 0) - backward_diff(field[0], before_y[0], 1)
    return jnp.stack([cx, cy, cz])

def reference(e_adjoint, h_adjoint, conductivity, permittivity, forward_e, receiver_data, receiver_tile, receiver_cell, receiver_comp):
    loss = conductivity * time_step / (2.0 * permittivity)
    decay = (1.0 - loss) / (1.0 + loss)
    gain = time_step / permittivity / (1.0 + loss)
    amplitudes = jnp.dot(receiver_data, time_kernel().T, precision=lax.Precision.HIGHEST)
    tile = receiver_tile[:, 0]
    tile_x = tile // N_GY
    tile_y = tile % N_GY
    local_i = receiver_cell // (CY * NZ)
    local_j = receiver_cell // NZ % CY
    local_k = receiver_cell % NZ
    total_cells = NX * NY * NZ
    flat = receiver_comp * total_cells + ((tile_x * CX + local_i) * NY + tile_y * CY + local_j) * NZ + local_k
    flat = flat.astype(jnp.int32)
    e_field = e_adjoint
    h_field = h_adjoint
    after_x = jnp.zeros((2, 1, NY, NZ), e_adjoint.dtype)
    after_y = jnp.zeros((2, NX, 1, NZ), e_adjoint.dtype)
    gradient = jnp.zeros((NX, NY, NZ), jnp.float32)
    for moment in range(STEPS):
        h_field = h_field - time_step * curl_e(e_field, after_x, after_y)
        source = jnp.zeros((3 * total_cells,), jnp.float32).at[flat].add(amplitudes[:, moment]).reshape(3, NX, NY, NZ)
        e_field = decay * e_field + gain * (curl_h(h_field, after_x, after_y) - source)
        gradient = gradient + lax.optimization_barrier(jnp.sum(forward_e[moment].astype(jnp.float32) * e_field, axis=0))
    return (e_field, h_field, gradient)
```

```python
import functools

import jax
import jax.numpy as jnp
from jax import lax
from jax.experimental import pallas as pl
from jax.experimental.pallas import tpu as pltpu
from jax.sharding import PartitionSpec as P

STEPS = 3
SAMPLES = 128
LANES = 128
FIELDS = 4
SPAN = LANES // FIELDS
MESH = pl.DeviceIdType.MESH
MIB = 1 << 20

time_step = 0.55


def split3(x):
    a = x.astype(jnp.bfloat16)
    rest = x - a.astype(jnp.float32)
    b = rest.astype(jnp.bfloat16)
    c = (rest - b.astype(jnp.float32)).astype(jnp.bfloat16)
    return a, b, c


def mm(a, b, contract=((1,), (0,))):
    return lax.dot_general(a, b, (contract, ((), ())), preferred_element_type=jnp.float32)


def time_kernel():
    rows = 8
    sample = lax.broadcasted_iota(jnp.int32, (rows, SAMPLES), 1).astype(jnp.float32)
    step = lax.broadcasted_iota(jnp.int32, (rows, SAMPLES), 0).astype(jnp.float32)
    centre = (step + 0.5) * (SAMPLES / STEPS)
    spread = SAMPLES / (4.0 * STEPS)
    kernel = jnp.exp(-jnp.square((sample - centre) / spread))
    kernel = jnp.where(step < STEPS - 0.5, kernel, 0.0)
    norm = jnp.sum(kernel * kernel, axis=1, keepdims=True)
    return kernel / jnp.sqrt(jnp.where(norm > 0.0, norm, 1.0))


def pack(devices, cells, data_ref, tile_ref, cell_ref, comp_ref):
    blocks, width = tile_ref.shape
    kernel = time_kernel()
    before = (
        lax.broadcasted_iota(jnp.int32, (width, width), 0)
        < lax.broadcasted_iota(jnp.int32, (width, width), 1)
    ).astype(jnp.bfloat16)
    every = jnp.ones((width, width), jnp.bfloat16)
    destination = lax.broadcasted_iota(jnp.int32, (devices, width), 0)
    slot = lax.broadcasted_iota(jnp.int32, (SPAN, width), 0).astype(jnp.float32)
    seen = jnp.zeros((devices, width), jnp.float32)
    packed = jnp.zeros((devices, LANES), jnp.float32)
    for b in range(blocks):
        onehot = (destination == tile_ref[b : b + 1, :]).astype(jnp.float32)
        hot = onehot.astype(jnp.bfloat16)
        rank = jnp.sum(onehot * (seen + mm(hot, before)), axis=0, keepdims=True)
        seen = seen + mm(hot, every)
        amplitude = lax.dot_general(
            kernel,
            data_ref[b * width : (b + 1) * width, :],
            (((1,), (1,)), ((), ())),
            precision=lax.Precision.HIGHEST,
            preferred_element_type=jnp.float32,
        )
        code = (comp_ref[b : b + 1, :] * cells + cell_ref[b : b + 1, :]).astype(jnp.float32)
        here = slot == rank
        fields = [amplitude[t : t + 1, :] for t in range(STEPS)] + [code]
        spread = jnp.concatenate([jnp.where(here, f, 0.0) for f in fields], axis=0)
        for term in split3(spread):
            packed = packed + mm(hot, term, ((1,), (1,)))
    return packed


def route_kernel(
    nx,
    ny,
    cells,
    data_ref,
    tile_ref,
    cell_ref,
    comp_ref,
    got_ref,
    code_ref,
    first,
    mid,
    second,
    last,
    send_y,
    recv_y,
    send_x,
    recv_x,
):
    ix, iy = lax.axis_index("gx"), lax.axis_index("gy")
    barrier = pltpu.get_barrier_semaphore()
    for k in range(1, nx):
        pl.semaphore_signal(barrier, inc=1, device_id=(lax.rem(ix + k, nx), iy), device_id_type=MESH)
    for k in range(1, ny):
        pl.semaphore_signal(barrier, inc=1, device_id=(ix, lax.rem(iy + k, ny)), device_id_type=MESH)

    first[...] = pack(nx * ny, cells, data_ref, tile_ref, cell_ref, comp_ref)
    pl.semaphore_wait(barrier, nx + ny - 2)

    copies = []
    for k in range(1, nx):
        to = lax.rem(ix + k, nx)
        copy = pltpu.make_async_remote_copy(
            src_ref=first.at[pl.ds(pl.multiple_of(to * ny, ny), ny), :],
            dst_ref=mid.at[pl.ds(pl.multiple_of(ix * ny, ny), ny), :],
            send_sem=send_x.at[k - 1],
            recv_sem=recv_x.at[k - 1],
            device_id=(to, iy),
            device_id_type=MESH,
        )
        copy.start()
        copies.append(copy)
    own = pl.ds(pl.multiple_of(ix * ny, ny), ny)
    mid[own, :] = first[own, :]
    for copy in copies:
        copy.wait_recv()
    for j in range(ny):
        second[j * nx : (j + 1) * nx, :] = mid[pl.ds(j, nx, stride=ny), :]
    later = []
    for k in range(1, ny):
        to = lax.rem(iy + k, ny)
        copy = pltpu.make_async_remote_copy(
            src_ref=second.at[pl.ds(pl.multiple_of(to * nx, nx), nx), :],
            dst_ref=last.at[pl.ds(pl.multiple_of(iy * nx, nx), nx), :],
            send_sem=send_y.at[k - 1],
            recv_sem=recv_y.at[k - 1],
            device_id=(ix, to),
            device_id_type=MESH,
        )
        copy.start()
        later.append(copy)
    own = pl.ds(pl.multiple_of(iy * nx, nx), nx)
    last[own, :] = second[own, :]
    for copy in copies:
        copy.wait_send()
    for copy in later:
        copy.wait()
    got = last[...]
    got_ref[...] = got
    code_ref[...] = got.astype(jnp.int32)


def route(nx, ny, cells, data, tile, cell, comp):
    devices = nx * ny
    rows = lambda: pltpu.VMEM((devices, LANES), jnp.float32)
    return pl.pallas_call(
        functools.partial(route_kernel, nx, ny, cells),
        out_shape=[
            jax.ShapeDtypeStruct((devices, LANES), jnp.float32),
            jax.ShapeDtypeStruct((devices, LANES), jnp.int32),
        ],
        in_specs=[pl.BlockSpec(memory_space=pltpu.VMEM)] * 4,
        out_specs=[pl.BlockSpec(memory_space=pltpu.VMEM)] * 2,
        scratch_shapes=[
            rows(),
            rows(),
            rows(),
            rows(),
            pltpu.SemaphoreType.DMA((ny - 1,)),
            pltpu.SemaphoreType.DMA((ny - 1,)),
            pltpu.SemaphoreType.DMA((nx - 1,)),
            pltpu.SemaphoreType.DMA((nx - 1,)),
        ],
        compiler_params=pltpu.CompilerParams(
            collective_id=0, has_side_effects=True, vmem_limit_bytes=16 * MIB
        ),
        name="route",
    )(data, tile, cell, comp)


def scatter_kernel(cap, code_ref, got_ref, out_ref, quad, wide):
    devices = got_ref.shape[0]
    got = got_ref[...]
    lane = lax.broadcasted_iota(jnp.int32, (devices, LANES), 1)
    slot = jnp.bitwise_and(lane, SPAN - 1)
    codes = jnp.where(lane >= (FIELDS - 1) * SPAN, got, 0.0)
    codes = codes + pltpu.roll(codes, SPAN, 1)
    codes = codes + pltpu.roll(codes, 2 * SPAN, 1)
    total = got
    for d in range(1, cap):
        same = (codes == pltpu.roll(codes, d, 1)) & (slot >= d)
        total = total + jnp.where(same, pltpu.roll(got, d, 1), 0.0)
    for t in range(FIELDS):
        quad[pl.ds(t, devices, stride=FIELDS), :] = jnp.where(
            (lane >= t * SPAN) & (lane < (t + 1) * SPAN), total, 0.0
        )
    values = quad[...]
    high = values.astype(jnp.bfloat16)
    low = (values - high.astype(jnp.float32)).astype(jnp.bfloat16)
    terms = jnp.concatenate([high, low], axis=1)
    row_slot = jnp.bitwise_and(lax.broadcasted_iota(jnp.int32, (2 * LANES, 2 * LANES), 0), SPAN - 1)
    column = lax.broadcasted_iota(jnp.int32, (2 * LANES, 2 * LANES), 1) // LANES
    for i in range(0, cap, 2):
        pick = (row_slot == column + i).astype(jnp.bfloat16)
        both = mm(terms, pick)
        wide[i] = both[:, :LANES]
        wide[i + 1] = both[:, LANES:]

    rows = out_ref.shape[0]
    step = 128

    def clear(n, _):
        out_ref[pl.ds(pl.multiple_of(n * step, step), step), :] = jnp.zeros((step, LANES), jnp.float32)
        return 0

    lax.fori_loop(0, rows // step, clear, 0)
    depth = lax.broadcasted_iota(jnp.int32, (FIELDS, LANES), 1)

    def place(s, _):
        where, news = [], []
        for i in range(cap):
            code = code_ref[s, (FIELDS - 1) * SPAN + i]
            row = pl.ds(pl.multiple_of(lax.shift_right_logical(code, 7) * FIELDS, FIELDS), FIELDS)
            news.append(out_ref[row, :] + wide[i, pl.ds(pl.multiple_of(s * FIELDS, FIELDS), FIELDS), :])
            where.append((row, depth == jnp.bitwise_and(code, LANES - 1)))
        for (row, mask), new in zip(where, news):
            pltpu.store(out_ref.at[row, :], new, mask=mask)
        return 0

    lax.fori_loop(0, devices, place, 0)


def scatter(cap, rows, codes, got):
    devices = got.shape[0]
    return pl.pallas_call(
        functools.partial(scatter_kernel, cap),
        out_shape=jax.ShapeDtypeStruct((rows * FIELDS, LANES), jnp.float32),
        in_specs=[pl.BlockSpec(memory_space=pltpu.SMEM), pl.BlockSpec(memory_space=pltpu.VMEM)],
        out_specs=pl.BlockSpec(memory_space=pltpu.VMEM),
        scratch_shapes=[
            pltpu.VMEM((devices * FIELDS, LANES), jnp.float32),
            pltpu.VMEM((cap, devices * FIELDS, LANES), jnp.float32),
        ],
        compiler_params=pltpu.CompilerParams(vmem_limit_bytes=32 * MIB),
        name="scatter",
    )(codes, got)


def steps_kernel(
    nx,
    ny,
    e_in,
    h_in,
    cond_in,
    perm_in,
    fwd_in,
    src_in,
    e,
    h,
    grad,
    decay,
    gain,
    fwd,
    src,
    ex_got,
    ey_got,
    hx_got,
    hy_got,
    ex_put,
    ey_put,
    hx_put,
    hy_put,
    load,
    send,
    recv,
):
    ix, iy = lax.axis_index("gx"), lax.axis_index("gy")
    below_x = (lax.rem(ix + nx - 1, nx), iy)
    above_x = (lax.rem(ix + 1, nx), iy)
    below_y = (ix, lax.rem(iy + ny - 1, ny))
    above_y = (ix, lax.rem(iy + 1, ny))
    barrier = pltpu.get_barrier_semaphore()
    for other in (below_x, above_x, below_y, above_y):
        pl.semaphore_signal(barrier, inc=1, device_id=other, device_id_type=MESH)

    loads = [
        pltpu.make_async_copy(a, b, load.at[n])
        for n, (a, b) in enumerate(
            (
                (e_in, e),
                (h_in, h),
                (cond_in, decay),
                (perm_in, gain),
                (src_in, src),
                (fwd_in, fwd),
            )
        )
    ]
    for copy in loads:
        copy.start()

    size_x, size_y, depth = e.shape[1:]
    shape = (size_y, depth)
    row = lax.broadcasted_iota(jnp.int32, shape, 0)
    lane = lax.broadcasted_iota(jnp.int32, shape, 1)
    one = jnp.float32(1.0)
    zero = jnp.float32(0.0)
    keep_ex = jnp.where(ix == nx - 1, zero, one)
    keep_ey = jnp.where(iy == ny - 1, zero, one)
    keep_hx = jnp.where(ix == 0, zero, one)
    keep_hy = jnp.where(iy == 0, zero, one)

    def up_z(f):
        return jnp.where(lane == depth - 1, 0.0, pltpu.roll(f, depth - 1, 1))

    def down_z(f):
        return jnp.where(lane == 0, 0.0, pltpu.roll(f, 1, 1))

    def up_y(f, after):
        return jnp.where(row == size_y - 1, after, pltpu.roll(f, size_y - 1, 0))

    def down_y(f, before):
        return jnp.where(row == 0, before, pltpu.roll(f, 1, 0))

    def e_rows(x, p, t, ex, ez):
        ey_put[t, 0, pl.ds(p, 1), :] = ex[:1]
        ey_put[t, 1, pl.ds(p, 1), :] = ez[:1]

    def h_plane(x, p, t, next_y, next_z):
        ex, ey, ez = e[0, x], e[1, x], e[2, x]
        after_x = ey_got[t, 0, pl.ds(p, 1), :] * keep_ey
        after_z = ey_got[t, 1, pl.ds(p, 1), :] * keep_ey
        curl_x = (up_y(ez, after_z) - ez) - (up_z(ey) - ey)
        curl_y = (up_z(ex) - ex) - (next_z - ez)
        curl_z = (next_y - ey) - (up_y(ex, after_x) - ex)
        hx = h[0, x] - time_step * curl_x
        hy = h[1, x] - time_step * curl_y
        hz = h[2, x] - time_step * curl_z
        h[0, x] = hx
        h[1, x] = hy
        h[2, x] = hz
        hy_put[t, 0, pl.ds(p, 1), :] = hx[size_y - 1 :]
        hy_put[t, 1, pl.ds(p, 1), :] = hz[size_y - 1 :]

    def e_plane(x, p, t, last_y, last_z):
        hx, hy, hz = h[0, x], h[1, x], h[2, x]
        before_x = hy_got[t, 0, pl.ds(p, 1), :] * keep_hy
        before_z = hy_got[t, 1, pl.ds(p, 1), :] * keep_hy
        curl_x = (hz - down_y(hz, before_z)) - (hy - down_z(hy))
        curl_y = (hx - down_z(hx)) - (hz - last_z)
        curl_z = (hy - last_y) - (hx - down_y(hx, before_x))
        if t == 0:
            half_loss = decay[x] * (0.5 * time_step)
            eps = gain[x]
            inverse = 1.0 / (eps + half_loss)
            fade = (eps - half_loss) * inverse
            rise = time_step * inverse
            decay[x] = fade
            gain[x] = rise
        else:
            fade, rise = decay[x], gain[x]
        total = None
        for c, curl in enumerate((curl_x, curl_y, curl_z)):
            source = src[c, x, pl.ds(t, size_y, stride=FIELDS), :]
            new = fade * e[c, x] + rise * (curl - source)
            e[c, x] = new
            term = fwd[t, c, x].astype(jnp.float32) * new
            total = term if total is None else total + term
            if t < STEPS - 1 and c != 1:
                ey_put[t + 1, c // 2, pl.ds(p, 1), :] = new[:1]
        grad[x] = total if t == 0 else grad[x] + total

    def remote(a, b, n, device):
        return pltpu.make_async_remote_copy(
            src_ref=a,
            dst_ref=b,
            send_sem=send.at[n],
            recv_sem=recv.at[n],
            device_id=device,
            device_id_type=MESH,
        )

    def e_copies(t):
        return (
            remote(ey_put.at[t], ey_got.at[t], 4 * t, below_y),
            remote(ex_put.at[t], ex_got.at[t], 4 * t + 1, below_x),
        )

    def h_copies(t):
        return (
            remote(hy_put.at[t], hy_got.at[t], 4 * t + 2, above_y),
            remote(hx_put.at[t], hx_got.at[t], 4 * t + 3, above_x),
        )

    loads[0].wait()

    def first_rows(p, _):
        x = lax.rem(p + 1, size_x)
        e_rows(x, p, 0, e[0, x], e[2, x])
        return 0

    lax.fori_loop(0, size_x, first_rows, 0)
    pl.semaphore_wait(barrier, 4)
    pending = []
    for t in range(STEPS):
        ex_put[t, 0] = e[1, 0]
        ex_put[t, 1] = e[2, 0]
        across, along = e_copies(t)
        across.start()
        along.start()
        if t == 0:
            loads[1].wait()
        across.wait_recv()

        def h_inner(p, _):
            x = p + 1
            h_plane(x, p, t, e[1, x + 1], e[2, x + 1])
            return 0

        lax.fori_loop(0, size_x - 2, h_inner, 0)
        along.wait_recv()
        h_plane(size_x - 1, size_x - 2, t, ex_got[t, 0] * keep_ex, ex_got[t, 1] * keep_ex)
        h_plane(0, size_x - 1, t, e[1, 1], e[2, 1])
        pending += [across, along]
        hx_put[t, 0] = h[1, size_x - 1]
        hx_put[t, 1] = h[2, size_x - 1]
        across, along = h_copies(t)
        across.start()
        along.start()
        if t == 0:
            for n in (2, 3, 4, 5):
                loads[n].wait()
        across.wait_recv()

        def e_inner(p, _):
            x = p + 1
            e_plane(x, p, t, h[1, x - 1], h[2, x - 1])
            return 0

        lax.fori_loop(0, size_x - 1, e_inner, 0)
        along.wait_recv()
        e_plane(0, size_x - 1, t, hx_got[t, 0] * keep_hx, hx_got[t, 1] * keep_hx)
        pending += [across, along]
    for copy in pending:
        copy.wait_send()


def steps(nx, ny, e, h, cond, perm, fwd, src):
    size_x, size_y, depth = e.shape[1:]
    field = jax.ShapeDtypeStruct(e.shape, jnp.float32)
    single = jax.ShapeDtypeStruct(cond.shape, jnp.float32)
    x_halo = lambda: pltpu.VMEM((STEPS, 2, size_y, depth), jnp.float32)
    y_halo = lambda: pltpu.VMEM((STEPS, 2, size_x, depth), jnp.float32)
    whole = lambda a: pltpu.VMEM(a.shape, a.dtype)
    return pl.pallas_call(
        functools.partial(steps_kernel, nx, ny),
        out_shape=[field, field, single],
        in_specs=[pl.BlockSpec(memory_space=pl.ANY)] * 6,
        out_specs=[pl.BlockSpec(memory_space=pltpu.VMEM)] * 3,
        scratch_shapes=[
            whole(cond),
            whole(perm),
            whole(fwd),
            whole(src),
            x_halo(),
            y_halo(),
            x_halo(),
            y_halo(),
            x_halo(),
            y_halo(),
            x_halo(),
            y_halo(),
            pltpu.SemaphoreType.DMA((6,)),
            pltpu.SemaphoreType.DMA((4 * STEPS,)),
            pltpu.SemaphoreType.DMA((4 * STEPS,)),
        ],
        compiler_params=pltpu.CompilerParams(
            collective_id=1, has_side_effects=True, vmem_limit_bytes=40 * MIB
        ),
        name="steps",
    )(e, h, cond, perm, fwd, src)


def per_device(
    e_adjoint,
    h_adjoint,
    conductivity,
    permittivity,
    forward_e,
    receiver_data,
    receiver_tile,
    receiver_cell,
    receiver_comp,
):
    _, size_x, size_y, depth = e_adjoint.shape
    nx, ny = lax.axis_size("gx"), lax.axis_size("gy")
    receivers = receiver_data.shape[0]
    cap = 3 * receivers // (nx * ny)
    by_lane = lambda a: a.reshape(receivers // LANES, LANES)
    got, codes = route(
        nx,
        ny,
        size_x * size_y * depth,
        receiver_data,
        by_lane(receiver_tile),
        by_lane(receiver_cell),
        by_lane(receiver_comp),
    )
    placed = scatter(cap, 3 * size_x * size_y, codes, got)
    placed = placed.reshape(3, size_x, size_y * FIELDS, depth)
    return tuple(steps(nx, ny, e_adjoint, h_adjoint, conductivity, permittivity, forward_e, placed))


def solution(mesh):
    placed = (
        P(None, "gx", "gy", None),
        P(None, "gx", "gy", None),
        P("gx", "gy", None),
        P("gx", "gy", None),
        P(None, None, "gx", "gy", None),
        P(("gx", "gy"), None),
        P(("gx", "gy"), None),
        P(("gx", "gy")),
        P(("gx", "gy")),
    )
    return jax.shard_map(
        per_device,
        mesh=mesh,
        in_specs=placed,
        out_specs=(P(None, "gx", "gy", None), P(None, "gx", "gy", None), P("gx", "gy", None)),
        check_vma=False,
    )
```

```python
import functools

import jax
import jax.numpy as jnp
from jax import lax
from jax.experimental import pallas as pl
from jax.experimental.pallas import tpu as pltpu
from jax.sharding import PartitionSpec as P

STEPS = 3
SAMPLES = 128
LANES = 128
FIELDS = 4
SPAN = LANES // FIELDS
MESH = pl.DeviceIdType.MESH
GROUP = 12
MIB = 1 << 20

time_step = 0.55


def split3(x):
    a = x.astype(jnp.bfloat16)
    rest = x - a.astype(jnp.float32)
    b = rest.astype(jnp.bfloat16)
    c = (rest - b.astype(jnp.float32)).astype(jnp.bfloat16)
    return a, b, c


def mm(a, b, contract=((1,), (0,))):
    return lax.dot_general(a, b, (contract, ((), ())), preferred_element_type=jnp.float32)


def time_kernel():
    rows = 8
    sample = lax.broadcasted_iota(jnp.int32, (rows, SAMPLES), 1).astype(jnp.float32)
    step = lax.broadcasted_iota(jnp.int32, (rows, SAMPLES), 0).astype(jnp.float32)
    centre = (step + 0.5) * (SAMPLES / STEPS)
    spread = SAMPLES / (4.0 * STEPS)
    kernel = jnp.exp(-jnp.square((sample - centre) / spread))
    kernel = jnp.where(step < STEPS - 0.5, kernel, 0.0)
    norm = jnp.sum(kernel * kernel, axis=1, keepdims=True)
    return kernel / jnp.sqrt(jnp.where(norm > 0.0, norm, 1.0))


def pack(devices, cells, data_ref, tile_ref, cell_ref, comp_ref):
    blocks, width = tile_ref.shape
    kernel = time_kernel()
    before = (
        lax.broadcasted_iota(jnp.int32, (width, width), 0)
        < lax.broadcasted_iota(jnp.int32, (width, width), 1)
    ).astype(jnp.bfloat16)
    every = jnp.ones((width, width), jnp.bfloat16)
    destination = lax.broadcasted_iota(jnp.int32, (devices, width), 0)
    slot = lax.broadcasted_iota(jnp.int32, (SPAN, width), 0).astype(jnp.float32)
    seen = jnp.zeros((devices, width), jnp.float32)
    packed = jnp.zeros((devices, LANES), jnp.float32)
    for b in range(blocks):
        onehot = (destination == tile_ref[b : b + 1, :]).astype(jnp.float32)
        hot = onehot.astype(jnp.bfloat16)
        rank = jnp.sum(onehot * (seen + mm(hot, before)), axis=0, keepdims=True)
        seen = seen + mm(hot, every)
        amplitude = lax.dot_general(
            kernel,
            data_ref[b * width : (b + 1) * width, :],
            (((1,), (1,)), ((), ())),
            precision=lax.Precision.HIGHEST,
            preferred_element_type=jnp.float32,
        )
        code = (comp_ref[b : b + 1, :] * cells + cell_ref[b : b + 1, :]).astype(jnp.float32)
        here = slot == rank
        fields = [amplitude[t : t + 1, :] for t in range(STEPS)] + [code]
        spread = jnp.concatenate([jnp.where(here, f, 0.0) for f in fields], axis=0)
        for term in split3(spread):
            packed = packed + mm(hot, term, ((1,), (1,)))
    return packed


def route_kernel(
    nx,
    ny,
    cells,
    data_in,
    tile_in,
    cell_in,
    comp_in,
    got_ref,
    code_ref,
    data_ref,
    tile_ref,
    cell_ref,
    comp_ref,
    first,
    mid,
    second,
    last,
    load,
    send_y,
    recv_y,
    send_x,
    recv_x,
):
    ix, iy = lax.axis_index("gx"), lax.axis_index("gy")
    pairs = ((tile_in, tile_ref), (cell_in, cell_ref), (comp_in, comp_ref), (data_in, data_ref))
    loads = [pltpu.make_async_copy(a, b, load.at[n]) for n, (a, b) in enumerate(pairs)]
    for copy in loads:
        copy.start()
    barrier = pltpu.get_barrier_semaphore()
    for k in range(1, nx):
        pl.semaphore_signal(barrier, inc=1, device_id=(lax.rem(ix + k, nx), iy), device_id_type=MESH)
    for k in range(1, ny):
        pl.semaphore_signal(barrier, inc=1, device_id=(ix, lax.rem(iy + k, ny)), device_id_type=MESH)

    for copy in loads:
        copy.wait()
    first[...] = pack(nx * ny, cells, data_ref, tile_ref, cell_ref, comp_ref)
    pl.semaphore_wait(barrier, nx + ny - 2)

    copies = []
    for k in range(1, nx):
        to = lax.rem(ix + k, nx)
        copy = pltpu.make_async_remote_copy(
            src_ref=first.at[pl.ds(pl.multiple_of(to * ny, ny), ny), :],
            dst_ref=mid.at[pl.ds(pl.multiple_of(ix * ny, ny), ny), :],
            send_sem=send_x.at[k - 1],
            recv_sem=recv_x.at[k - 1],
            device_id=(to, iy),
            device_id_type=MESH,
        )
        copy.start()
        copies.append(copy)
    own = pl.ds(pl.multiple_of(ix * ny, ny), ny)
    mid[own, :] = first[own, :]
    for copy in copies:
        copy.wait_recv()
    for j in range(ny):
        second[j * nx : (j + 1) * nx, :] = mid[pl.ds(j, nx, stride=ny), :]
    later = []
    for k in range(1, ny):
        to = lax.rem(iy + k, ny)
        copy = pltpu.make_async_remote_copy(
            src_ref=second.at[pl.ds(pl.multiple_of(to * nx, nx), nx), :],
            dst_ref=last.at[pl.ds(pl.multiple_of(iy * nx, nx), nx), :],
            send_sem=send_y.at[k - 1],
            recv_sem=recv_y.at[k - 1],
            device_id=(ix, to),
            device_id_type=MESH,
        )
        copy.start()
        later.append(copy)
    own = pl.ds(pl.multiple_of(iy * nx, nx), nx)
    last[own, :] = second[own, :]
    for copy in copies:
        copy.wait_send()
    for copy in later:
        copy.wait()
    got_ref[...] = last[...]
    quarter = nx * ny // FIELDS
    lane = lax.broadcasted_iota(jnp.int32, (quarter, LANES), 1) // SPAN
    codes = jnp.zeros((quarter, LANES), jnp.int32)
    for p in range(FIELDS):
        code = last[pl.ds(p, quarter, stride=FIELDS), :].astype(jnp.int32)
        word = jnp.bitwise_and(code, LANES - 1) + jnp.bitwise_and(code, -LANES) * FIELDS
        codes = jnp.where(lane == p, pltpu.roll(word, (p + 1) * SPAN % LANES, 1), codes)
    code_ref[...] = codes


def route(nx, ny, cells, data, tile, cell, comp):
    devices = nx * ny
    rows = lambda: pltpu.VMEM((devices, LANES), jnp.float32)
    return pl.pallas_call(
        functools.partial(route_kernel, nx, ny, cells),
        out_shape=[
            jax.ShapeDtypeStruct((devices, LANES), jnp.float32),
            jax.ShapeDtypeStruct((devices // FIELDS, LANES), jnp.int32),
        ],
        in_specs=[pl.BlockSpec(memory_space=pltpu.HBM)] * 4,
        out_specs=[pl.BlockSpec(memory_space=pltpu.VMEM)] * 2,
        scratch_shapes=[
            *(pltpu.VMEM(a.shape, a.dtype) for a in (data, tile, cell, comp)),
            rows(),
            rows(),
            rows(),
            rows(),
            pltpu.SemaphoreType.DMA((4,)),
            pltpu.SemaphoreType.DMA((ny - 1,)),
            pltpu.SemaphoreType.DMA((ny - 1,)),
            pltpu.SemaphoreType.DMA((nx - 1,)),
            pltpu.SemaphoreType.DMA((nx - 1,)),
        ],
        compiler_params=pltpu.CompilerParams(
            collective_id=0, has_side_effects=True, vmem_limit_bytes=16 * MIB
        ),
        name="route",
    )(*(pltpu.with_memory_space_constraint(a, pltpu.HBM) for a in (data, tile, cell, comp)))


def scatter_kernel(cap, code_ref, got_ref, out_ref, quad, wide):
    devices = got_ref.shape[0]
    got = got_ref[...]
    lane = lax.broadcasted_iota(jnp.int32, (devices, LANES), 1)
    slot = jnp.bitwise_and(lane, SPAN - 1)
    codes = jnp.where(lane >= (FIELDS - 1) * SPAN, got, 0.0)
    codes = codes + pltpu.roll(codes, SPAN, 1)
    codes = codes + pltpu.roll(codes, 2 * SPAN, 1)
    total = got
    place_in_group = slot - slot // GROUP * GROUP
    for d in range(1, GROUP):
        same = (codes == pltpu.roll(codes, d, 1)) & (place_in_group >= d)
        total = total + jnp.where(same, pltpu.roll(got, d, 1), 0.0)
    for t in range(FIELDS):
        quad[pl.ds(t, devices, stride=FIELDS), :] = jnp.where(
            (lane >= t * SPAN) & (lane < (t + 1) * SPAN), total, 0.0
        )
    values = quad[...]
    high = values.astype(jnp.bfloat16)
    low = (values - high.astype(jnp.float32)).astype(jnp.bfloat16)
    terms = jnp.concatenate([high, low], axis=1)
    row_slot = jnp.bitwise_and(lax.broadcasted_iota(jnp.int32, (2 * LANES, 2 * LANES), 0), SPAN - 1)
    column = lax.broadcasted_iota(jnp.int32, (2 * LANES, 2 * LANES), 1) // LANES
    for i in range(0, cap, 2):
        pick = (row_slot == column + i).astype(jnp.bfloat16)
        both = mm(terms, pick)
        wide[i] = both[:, :LANES]
        wide[i + 1] = both[:, LANES:]

    rows = out_ref.shape[0]
    step = 128

    def clear(n, _):
        out_ref[pl.ds(pl.multiple_of(n * step, step), step), :] = jnp.zeros((step, LANES), jnp.float32)
        return 0

    lax.fori_loop(0, rows // step, clear, 0)
    depth = lax.broadcasted_iota(jnp.int32, (FIELDS, LANES), 1)

    def place(q, _):
        for p in range(FIELDS):
            s = q * FIELDS + p
            for start in range(0, cap, GROUP):
                where, news = [], []
                for i in range(start, min(cap, start + GROUP)):
                    word = code_ref[q, p * SPAN + i]
                    row = pl.ds(pl.multiple_of(lax.shift_right_logical(word, 7), FIELDS), FIELDS)
                    news.append(out_ref[row, :] + wide[i, pl.ds(pl.multiple_of(s * FIELDS, FIELDS), FIELDS), :])
                    column = jnp.bitwise_and(jnp.full((FIELDS, LANES), word, jnp.int32), LANES - 1)
                    where.append((row, depth == column))
                for (row, mask), new in zip(where, news):
                    pltpu.store(out_ref.at[row, :], new, mask=mask)
        return 0

    lax.fori_loop(0, devices // FIELDS, place, 0)


def scatter(cap, rows, codes, got):
    devices = got.shape[0]
    return pl.pallas_call(
        functools.partial(scatter_kernel, cap),
        out_shape=jax.ShapeDtypeStruct((rows * FIELDS, LANES), jnp.float32),
        in_specs=[pl.BlockSpec(memory_space=pltpu.SMEM), pl.BlockSpec(memory_space=pltpu.VMEM)],
        out_specs=pl.BlockSpec(memory_space=pltpu.VMEM),
        scratch_shapes=[
            pltpu.VMEM((devices * FIELDS, LANES), jnp.float32),
            pltpu.VMEM((cap, devices * FIELDS, LANES), jnp.float32),
        ],
        compiler_params=pltpu.CompilerParams(vmem_limit_bytes=24 * MIB),
        name="scatter",
    )(codes, got)


def steps_kernel(
    nx,
    ny,
    e_in,
    h_in,
    cond_in,
    perm_in,
    fwd,
    src,
    e,
    h,
    grad,
    decay,
    gain,
    ex_got,
    ey_got,
    hx_got,
    hy_got,
    ex_put,
    ey_put,
    hx_put,
    hy_put,
    send,
    recv,
):
    ix, iy = lax.axis_index("gx"), lax.axis_index("gy")
    below_x = (lax.rem(ix + nx - 1, nx), iy)
    above_x = (lax.rem(ix + 1, nx), iy)
    below_y = (ix, lax.rem(iy + ny - 1, ny))
    above_y = (ix, lax.rem(iy + 1, ny))
    barrier = pltpu.get_barrier_semaphore()
    for other in (below_x, above_x, below_y, above_y):
        pl.semaphore_signal(barrier, inc=1, device_id=other, device_id_type=MESH)

    size_x, size_y, depth = e.shape[1:]
    shape = (size_y, depth)
    row = lax.broadcasted_iota(jnp.int32, shape, 0)
    lane = lax.broadcasted_iota(jnp.int32, shape, 1)
    one = jnp.float32(1.0)
    zero = jnp.float32(0.0)
    keep_ex = jnp.where(ix == nx - 1, zero, one)
    keep_ey = jnp.where(iy == ny - 1, zero, one)
    keep_hx = jnp.where(ix == 0, zero, one)
    keep_hy = jnp.where(iy == 0, zero, one)

    def up_z(f):
        return jnp.where(lane == depth - 1, 0.0, pltpu.roll(f, depth - 1, 1))

    def down_z(f):
        return jnp.where(lane == 0, 0.0, pltpu.roll(f, 1, 1))

    def up_y(f, after):
        return jnp.where(row == size_y - 1, after, pltpu.roll(f, size_y - 1, 0))

    def down_y(f, before):
        return jnp.where(row == 0, before, pltpu.roll(f, 1, 0))

    def e_rows(x, p, t, ex, ez):
        ey_put[t, 0, pl.ds(p, 1), :] = ex[:1]
        ey_put[t, 1, pl.ds(p, 1), :] = ez[:1]

    def h_plane(x, p, t, next_y, next_z):
        es, hs = (e_in, h_in) if t == 0 else (e, h)
        ex, ey, ez = es[0, x], es[1, x], es[2, x]
        after_x = ey_got[t, 0, pl.ds(p, 1), :] * keep_ey
        after_z = ey_got[t, 1, pl.ds(p, 1), :] * keep_ey
        curl_x = (up_y(ez, after_z) - ez) - (up_z(ey) - ey)
        curl_y = (up_z(ex) - ex) - (next_z - ez)
        curl_z = (next_y - ey) - (up_y(ex, after_x) - ex)
        hx = hs[0, x] - time_step * curl_x
        hy = hs[1, x] - time_step * curl_y
        hz = hs[2, x] - time_step * curl_z
        h[0, x] = hx
        h[1, x] = hy
        h[2, x] = hz
        hy_put[t, 0, pl.ds(p, 1), :] = hx[size_y - 1 :]
        hy_put[t, 1, pl.ds(p, 1), :] = hz[size_y - 1 :]

    def e_plane(x, p, t, last_y, last_z):
        hx, hy, hz = h[0, x], h[1, x], h[2, x]
        before_x = hy_got[t, 0, pl.ds(p, 1), :] * keep_hy
        before_z = hy_got[t, 1, pl.ds(p, 1), :] * keep_hy
        curl_x = (hz - down_y(hz, before_z)) - (hy - down_z(hy))
        curl_y = (hx - down_z(hx)) - (hz - last_z)
        curl_z = (hy - last_y) - (hx - down_y(hx, before_x))
        if t == 0:
            half_loss = cond_in[x] * (0.5 * time_step)
            eps = perm_in[x]
            inverse = 1.0 / (eps + half_loss)
            fade = (eps - half_loss) * inverse
            rise = time_step * inverse
            decay[x] = fade
            gain[x] = rise
        else:
            fade, rise = decay[x], gain[x]
        es = e_in if t == 0 else e
        total = None
        for c, curl in enumerate((curl_x, curl_y, curl_z)):
            source = src[c, x, pl.ds(t, size_y, stride=FIELDS), :]
            new = fade * es[c, x] + rise * (curl - source)
            e[c, x] = new
            term = fwd[t, c, x].astype(jnp.float32) * new
            total = term if total is None else total + term
            if t < STEPS - 1 and c != 1:
                ey_put[t + 1, c // 2, pl.ds(p, 1), :] = new[:1]
        grad[x] = total if t == 0 else grad[x] + total

    def remote(a, b, n, device):
        return pltpu.make_async_remote_copy(
            src_ref=a,
            dst_ref=b,
            send_sem=send.at[n],
            recv_sem=recv.at[n],
            device_id=device,
            device_id_type=MESH,
        )

    def e_copies(t):
        return (
            remote(ey_put.at[t], ey_got.at[t], 4 * t, below_y),
            remote(ex_put.at[t], ex_got.at[t], 4 * t + 1, below_x),
        )

    def h_copies(t):
        return (
            remote(hy_put.at[t], hy_got.at[t], 4 * t + 2, above_y),
            remote(hx_put.at[t], hx_got.at[t], 4 * t + 3, above_x),
        )

    def first_rows(p, _):
        x = lax.rem(p + 1, size_x)
        e_rows(x, p, 0, e_in[0, x], e_in[2, x])
        return 0

    lax.fori_loop(0, size_x, first_rows, 0)
    pl.semaphore_wait(barrier, 4)
    pending = []
    for t in range(STEPS):
        es = e_in if t == 0 else e
        ex_put[t, 0] = es[1, 0]
        ex_put[t, 1] = es[2, 0]
        across, along = e_copies(t)
        across.start()
        along.start()
        across.wait_recv()

        def h_inner(p, _):
            x = p + 1
            h_plane(x, p, t, es[1, x + 1], es[2, x + 1])
            return 0

        lax.fori_loop(0, size_x - 2, h_inner, 0)
        along.wait_recv()
        h_plane(size_x - 1, size_x - 2, t, ex_got[t, 0] * keep_ex, ex_got[t, 1] * keep_ex)
        h_plane(0, size_x - 1, t, es[1, 1], es[2, 1])
        pending += [across, along]
        hx_put[t, 0] = h[1, size_x - 1]
        hx_put[t, 1] = h[2, size_x - 1]
        across, along = h_copies(t)
        across.start()
        along.start()
        across.wait_recv()

        def e_inner(p, _):
            x = p + 1
            e_plane(x, p, t, h[1, x - 1], h[2, x - 1])
            return 0

        lax.fori_loop(0, size_x - 1, e_inner, 0)
        along.wait_recv()
        e_plane(0, size_x - 1, t, hx_got[t, 0] * keep_hx, hx_got[t, 1] * keep_hx)
        pending += [across, along]
    for copy in pending:
        copy.wait_send()


def steps(nx, ny, e, h, cond, perm, fwd, src):
    size_x, size_y, depth = e.shape[1:]
    field = jax.ShapeDtypeStruct(e.shape, jnp.float32)
    single = jax.ShapeDtypeStruct(cond.shape, jnp.float32)
    x_halo = lambda: pltpu.VMEM((STEPS, 2, size_y, depth), jnp.float32)
    y_halo = lambda: pltpu.VMEM((STEPS, 2, size_x, depth), jnp.float32)
    whole = lambda a: pltpu.VMEM(a.shape, a.dtype)
    return pl.pallas_call(
        functools.partial(steps_kernel, nx, ny),
        out_shape=[field, field, single],
        in_specs=[pl.BlockSpec(memory_space=pltpu.VMEM)] * 6,
        out_specs=[pl.BlockSpec(memory_space=pltpu.VMEM)] * 3,
        scratch_shapes=[
            whole(cond),
            whole(perm),
            x_halo(),
            y_halo(),
            x_halo(),
            y_halo(),
            x_halo(),
            y_halo(),
            x_halo(),
            y_halo(),
            pltpu.SemaphoreType.DMA((4 * STEPS,)),
            pltpu.SemaphoreType.DMA((4 * STEPS,)),
        ],
        compiler_params=pltpu.CompilerParams(
            collective_id=1, has_side_effects=True, vmem_limit_bytes=8 * MIB
        ),
        name="steps",
    )(e, h, cond, perm, fwd, src)


def per_device(
    e_adjoint,
    h_adjoint,
    conductivity,
    permittivity,
    forward_e,
    receiver_data,
    receiver_tile,
    receiver_cell,
    receiver_comp,
):
    _, size_x, size_y, depth = e_adjoint.shape
    nx, ny = lax.axis_size("gx"), lax.axis_size("gy")
    receivers = receiver_data.shape[0]
    cap = 3 * receivers // (nx * ny)
    by_lane = lambda a: a.reshape(receivers // LANES, LANES)
    got, codes = route(
        nx,
        ny,
        size_x * size_y * depth,
        receiver_data,
        by_lane(receiver_tile),
        by_lane(receiver_cell),
        by_lane(receiver_comp),
    )
    placed = scatter(cap, 3 * size_x * size_y, codes, got)
    placed = placed.reshape(3, size_x, size_y * FIELDS, depth)
    return tuple(steps(nx, ny, e_adjoint, h_adjoint, conductivity, permittivity, forward_e, placed))


def solution(mesh):
    placed = (
        P(None, "gx", "gy", None),
        P(None, "gx", "gy", None),
        P("gx", "gy", None),
        P("gx", "gy", None),
        P(None, None, "gx", "gy", None),
        P(("gx", "gy"), None),
        P(("gx", "gy"), None),
        P(("gx", "gy")),
        P(("gx", "gy")),
    )
    return jax.shard_map(
        per_device,
        mesh=mesh,
        in_specs=placed,
        out_specs=(P(None, "gx", "gy", None), P(None, "gx", "gy", None), P("gx", "gy", None)),
        check_vma=False,
    )
```

```python
import functools

import jax
import jax.numpy as jnp
from jax import lax
from jax.experimental import pallas as pl
from jax.experimental.pallas import tpu as pltpu
from jax.sharding import PartitionSpec as P

STEPS = 3
SAMPLES = 128
LANES = 128
FIELDS = 4
SPAN = LANES // FIELDS
MESH = pl.DeviceIdType.MESH
GROUP = 12
MIB = 1 << 20

time_step = 0.55


def split3(x):
    a = x.astype(jnp.bfloat16)
    rest = x - a.astype(jnp.float32)
    b = rest.astype(jnp.bfloat16)
    c = (rest - b.astype(jnp.float32)).astype(jnp.bfloat16)
    return a, b, c


def mm(a, b, contract=((1,), (0,))):
    return lax.dot_general(a, b, (contract, ((), ())), preferred_element_type=jnp.float32)


def time_kernel():
    rows = 8
    sample = lax.broadcasted_iota(jnp.int32, (rows, SAMPLES), 1).astype(jnp.float32)
    step = lax.broadcasted_iota(jnp.int32, (rows, SAMPLES), 0).astype(jnp.float32)
    centre = (step + 0.5) * (SAMPLES / STEPS)
    spread = SAMPLES / (4.0 * STEPS)
    kernel = jnp.exp(-jnp.square((sample - centre) / spread))
    kernel = jnp.where(step < STEPS - 0.5, kernel, 0.0)
    norm = jnp.sum(kernel * kernel, axis=1, keepdims=True)
    return kernel / jnp.sqrt(jnp.where(norm > 0.0, norm, 1.0))


def pack(devices, cells, data_ref, tile_ref, cell_ref, comp_ref):
    blocks, width = tile_ref.shape
    kernel = time_kernel()
    before = (
        lax.broadcasted_iota(jnp.int32, (width, width), 0)
        < lax.broadcasted_iota(jnp.int32, (width, width), 1)
    ).astype(jnp.bfloat16)
    every = jnp.ones((width, width), jnp.bfloat16)
    destination = lax.broadcasted_iota(jnp.int32, (devices, width), 0)
    slot = lax.broadcasted_iota(jnp.int32, (SPAN, width), 0).astype(jnp.float32)
    seen = jnp.zeros((devices, width), jnp.float32)
    packed = jnp.zeros((devices, LANES), jnp.float32)
    for b in range(blocks):
        onehot = (destination == tile_ref[b : b + 1, :]).astype(jnp.float32)
        hot = onehot.astype(jnp.bfloat16)
        rank = jnp.sum(onehot * (seen + mm(hot, before)), axis=0, keepdims=True)
        seen = seen + mm(hot, every)
        amplitude = lax.dot_general(
            kernel,
            data_ref[b * width : (b + 1) * width, :],
            (((1,), (1,)), ((), ())),
            precision=lax.Precision.HIGHEST,
            preferred_element_type=jnp.float32,
        )
        code = (comp_ref[b : b + 1, :] * cells + cell_ref[b : b + 1, :]).astype(jnp.float32)
        here = slot == rank
        fields = [amplitude[t : t + 1, :] for t in range(STEPS)] + [code]
        spread = jnp.concatenate([jnp.where(here, f, 0.0) for f in fields], axis=0)
        for term in split3(spread):
            packed = packed + mm(hot, term, ((1,), (1,)))
    return packed


class Place:
    def __init__(self, nx, ny):
        self.nx, self.ny = nx, ny
        self.ix, self.iy = lax.axis_index("gx"), lax.axis_index("gy")
        self.lo_x, self.hi_x = lax.rem(self.ix + nx - 1, nx), lax.rem(self.ix + 1, nx)
        self.lo_y, self.hi_y = lax.rem(self.iy + ny - 1, ny), lax.rem(self.iy + 1, ny)
        one, zero = jnp.float32(1.0), jnp.float32(0.0)
        self.keep_lo_x = jnp.where(self.ix == 0, zero, one)
        self.keep_hi_x = jnp.where(self.ix == nx - 1, zero, one)
        self.keep_lo_y = jnp.where(self.iy == 0, zero, one)
        self.keep_hi_y = jnp.where(self.iy == ny - 1, zero, one)

    def corners(self):
        return [(x, y) for x in (self.lo_x, self.hi_x) for y in (self.lo_y, self.hi_y)]

    def sides(self):
        return [(self.lo_x, self.iy), (self.hi_x, self.iy), (self.ix, self.lo_y), (self.ix, self.hi_y)]

    def plane(self, p, size_x):
        return jnp.where(p < 2, self.keep_lo_x, jnp.where(p >= size_x + 2, self.keep_hi_x, 1.0))


def shifts(rows, depth):
    lane = lax.broadcasted_iota(jnp.int32, (rows, depth), 1)

    def up_z(f):
        return jnp.where(lane == depth - 1, 0.0, pltpu.roll(f, depth - 1, 1))

    def down_z(f):
        return jnp.where(lane == 0, 0.0, pltpu.roll(f, 1, 1))

    def up_y(f):
        return pltpu.roll(f, rows - 1, 0)

    def down_y(f):
        return pltpu.roll(f, 1, 0)

    return up_z, down_z, up_y, down_y


def h_plane(e, h_from, h_to, p, factor, moves):
    up_z, _, up_y, _ = moves
    ex, ey, ez = e[0, p], e[1, p], e[2, p]
    curl_x = (up_y(ez) - ez) - (up_z(ey) - ey)
    curl_y = (up_z(ex) - ex) - (e[2, p + 1] - ez)
    curl_z = (e[1, p + 1] - ey) - (up_y(ex) - ex)
    for c, curl in enumerate((curl_x, curl_y, curl_z)):
        h_to[c, p] = h_from[c, p] - factor * curl


def curl_h(h, p, moves):
    _, down_z, _, down_y = moves
    hx, hy, hz = h[0, p], h[1, p], h[2, p]
    curl_x = (hz - down_y(hz)) - (hy - down_z(hy))
    curl_y = (hx - down_z(hx)) - (hz - h[2, p - 1])
    curl_z = (hy - h[1, p - 1]) - (hx - down_y(hx))
    return curl_x, curl_y, curl_z


def h_factor(place, size_y, rows, depth):
    row = lax.broadcasted_iota(jnp.int32, (rows, depth), 0)
    beyond = jnp.where(row < size_y + 4, place.keep_hi_y, place.keep_lo_y)
    return time_step * jnp.where(row < size_y, 1.0, beyond)


def row_copies(dn_put, up_put, up_got, lo_got, size_x, place):
    first, last, low, high = pl.ds(0, 2), pl.ds(size_x - 2, 2), pl.ds(0, 2), pl.ds(size_x + 2, 2)
    whole = pl.ds(2, size_x)
    return [
        (dn_put, up_got.at[:, whole], (place.ix, place.lo_y)),
        (up_put, lo_got.at[:, whole], (place.ix, place.hi_y)),
        (dn_put.at[:, first], up_got.at[:, high], (place.lo_x, place.lo_y)),
        (dn_put.at[:, last], up_got.at[:, low], (place.hi_x, place.lo_y)),
        (up_put.at[:, first], lo_got.at[:, high], (place.lo_x, place.hi_y)),
        (up_put.at[:, last], lo_got.at[:, low], (place.hi_x, place.hi_y)),
    ]


def plane_copies(array, count, size_x, size_y, place):
    lead = (slice(None),) * (len(array.shape) - 3)
    rows = pl.ds(0, size_y)

    def part(start):
        return array.at[(*lead, pl.ds(start, count), rows)]

    return [
        (part(2), part(size_x + 2), (place.lo_x, place.iy)),
        (part(size_x + 2 - count), part(2 - count), (place.hi_x, place.iy)),
    ]


def start_copies(parts, send, recv):
    copies = [
        pltpu.make_async_remote_copy(
            src_ref=a,
            dst_ref=b,
            send_sem=send.at[n],
            recv_sem=recv.at[n],
            device_id=device,
            device_id_type=MESH,
        )
        for n, (a, b, device) in enumerate(parts)
    ]
    for copy in copies:
        copy.start()
    return copies


def route_kernel(
    nx,
    ny,
    cells,
    data_in,
    tile_in,
    cell_in,
    comp_in,
    e_in,
    h_in,
    cond_in,
    perm_in,
    got_ref,
    code_ref,
    h,
    base,
    decay,
    gain,
    data_ref,
    tile_ref,
    cell_ref,
    comp_ref,
    e,
    first,
    mid,
    second,
    last,
    dn_put,
    up_put,
    up_got,
    lo_got,
    load,
    send_y,
    recv_y,
    send_x,
    recv_x,
    send,
    recv,
):
    place = Place(nx, ny)
    ix, iy = place.ix, place.iy
    size_x, size_y, depth = base.shape[1:]
    rows = size_y + 8
    inner = (pl.ds(2, size_x), pl.ds(0, size_y))
    pairs = (
        (tile_in, tile_ref),
        (cell_in, cell_ref),
        (comp_in, comp_ref),
        (data_in, data_ref),
        (e_in, e.at[:, inner[0], inner[1]]),
        (h_in, h.at[:, inner[0], inner[1]]),
        (cond_in, decay.at[inner[0], inner[1]]),
        (perm_in, gain.at[inner[0], inner[1]]),
    )
    loads = [pltpu.make_async_copy(a, b, load.at[n]) for n, (a, b) in enumerate(pairs)]
    for copy in loads:
        copy.start()
    barrier = pltpu.get_barrier_semaphore()
    for k in range(1, nx):
        pl.semaphore_signal(barrier, inc=1, device_id=(lax.rem(ix + k, nx), iy), device_id_type=MESH)
    for k in range(1, ny):
        pl.semaphore_signal(barrier, inc=1, device_id=(ix, lax.rem(iy + k, ny)), device_id_type=MESH)
    for other in place.corners():
        pl.semaphore_signal(barrier, inc=1, device_id=other, device_id_type=MESH)
    for copy in loads:
        copy.wait()

    def stage(x, _):
        p = x + 2
        n = 0
        for array in (e, h):
            for c in range(3):
                for r in range(2):
                    dn_put[n, x] = array[c, p, r : r + 1, :]
                    up_put[n, x] = array[c, p, size_y - 2 + r : size_y - 1 + r, :]
                    n += 1
        for array in (decay, gain):
            dn_put[n, x] = array[p, 0:1, :]
            up_put[n, x] = array[p, size_y - 1 : size_y, :]
            n += 1
        return 0

    lax.fori_loop(0, size_x, stage, 0)
    pl.semaphore_wait(barrier, nx + ny + 2)
    halos = start_copies(
        row_copies(dn_put, up_put, up_got, lo_got, size_x, place)
        + plane_copies(e, 2, size_x, size_y, place)
        + plane_copies(h, 2, size_x, size_y, place)
        + plane_copies(decay, 1, size_x, size_y, place)
        + plane_copies(gain, 1, size_x, size_y, place),
        send,
        recv,
    )
    first[...] = pack(nx * ny, cells, data_ref, tile_ref, cell_ref, comp_ref)

    copies = []
    for k in range(1, nx):
        to = lax.rem(ix + k, nx)
        copy = pltpu.make_async_remote_copy(
            src_ref=first.at[pl.ds(pl.multiple_of(to * ny, ny), ny), :],
            dst_ref=mid.at[pl.ds(pl.multiple_of(ix * ny, ny), ny), :],
            send_sem=send_x.at[k - 1],
            recv_sem=recv_x.at[k - 1],
            device_id=(to, iy),
            device_id_type=MESH,
        )
        copy.start()
        copies.append(copy)
    own = pl.ds(pl.multiple_of(ix * ny, ny), ny)
    mid[own, :] = first[own, :]
    for copy in copies:
        copy.wait_recv()
    for j in range(ny):
        second[j * nx : (j + 1) * nx, :] = mid[pl.ds(j, nx, stride=ny), :]
    later = []
    for k in range(1, ny):
        to = lax.rem(iy + k, ny)
        copy = pltpu.make_async_remote_copy(
            src_ref=second.at[pl.ds(pl.multiple_of(to * nx, nx), nx), :],
            dst_ref=last.at[pl.ds(pl.multiple_of(iy * nx, nx), nx), :],
            send_sem=send_y.at[k - 1],
            recv_sem=recv_y.at[k - 1],
            device_id=(ix, to),
            device_id_type=MESH,
        )
        copy.start()
        later.append(copy)
    own = pl.ds(pl.multiple_of(iy * nx, nx), nx)
    last[own, :] = second[own, :]
    for copy in copies:
        copy.wait_send()

    for copy in halos:
        copy.wait()
    for p in (0, 1, size_x + 2, size_x + 3):
        keep = place.plane(p, size_x)
        for c in range(3):
            for array in (e, h):
                array[c, p, :size_y] = array[c, p, :size_y] * keep

    def unstage(p, _):
        keep = place.plane(p, size_x)
        above, below = keep * place.keep_hi_y, keep * place.keep_lo_y
        n = 0
        gap = jnp.zeros((4, depth), jnp.float32)
        for array in (e, h):
            for c in range(3):
                array[c, p, size_y:] = jnp.concatenate(
                    [up_got[n, p] * above, up_got[n + 1, p] * above, gap, lo_got[n, p] * below, lo_got[n + 1, p] * below],
                    axis=0,
                )
                n += 2
        return 0

    lax.fori_loop(0, size_x + 4, unstage, 0)
    row = lax.broadcasted_iota(jnp.int32, (rows, depth), 0)
    inside = jnp.where(
        row < size_y,
        1.0,
        jnp.where(row == size_y, place.keep_hi_y, jnp.where(row == rows - 1, place.keep_lo_y, 0.0)),
    )
    ones = jnp.ones((6, depth), jnp.float32)

    def coefficients(p, _):
        decay[p, size_y:] = jnp.concatenate([up_got[12, p], ones, lo_got[12, p]], axis=0)
        gain[p, size_y:] = jnp.concatenate([up_got[13, p], ones, lo_got[13, p]], axis=0)
        half_loss = decay[p] * (0.5 * time_step)
        eps = gain[p]
        inverse = 1.0 / (eps + half_loss)
        keep = inside * place.plane(p, size_x)
        decay[p] = (eps - half_loss) * inverse * keep
        gain[p] = time_step * inverse * keep
        return 0

    lax.fori_loop(1, size_x + 3, coefficients, 0)
    moves = shifts(rows, depth)
    factor = h_factor(place, size_y, rows, depth)

    def h_step(p, _):
        h_plane(e, h, h, p, factor * place.plane(p, size_x), moves)
        return 0

    lax.fori_loop(0, size_x + 3, h_step, 0)

    def e_step(x, _):
        p = x + 2
        for c, curl in enumerate(curl_h(h, p, moves)):
            new = decay[p] * e[c, p] + gain[p] * curl
            base[c, x] = new[:size_y]
        return 0

    lax.fori_loop(0, size_x, e_step, 0)

    for copy in later:
        copy.wait()
    got_ref[...] = last[...]
    quarter = nx * ny // FIELDS
    lane = lax.broadcasted_iota(jnp.int32, (quarter, LANES), 1) // SPAN
    codes = jnp.zeros((quarter, LANES), jnp.int32)
    for k in range(FIELDS):
        code = last[pl.ds(k, quarter, stride=FIELDS), :].astype(jnp.int32)
        word = jnp.bitwise_and(code, LANES - 1) + jnp.bitwise_and(code, -LANES) * FIELDS
        codes = jnp.where(lane == k, pltpu.roll(word, (k + 1) * SPAN % LANES, 1), codes)
    code_ref[...] = codes


def in_vmem(count):
    return [pl.BlockSpec(memory_space=pltpu.VMEM)] * count


def f32(*shape):
    return jax.ShapeDtypeStruct(shape, jnp.float32)


def route(nx, ny, data, tile, cell, comp, e, h, cond, perm):
    devices = nx * ny
    size_x, size_y, depth = cond.shape
    wide, tall = size_x + 4, size_y + 8
    inputs = (data, tile, cell, comp, e, h, cond, perm)
    rows = lambda: pltpu.VMEM((devices, LANES), jnp.float32)
    count = 14
    return pl.pallas_call(
        functools.partial(route_kernel, nx, ny, size_x * size_y * depth),
        out_shape=[
            f32(devices, LANES),
            jax.ShapeDtypeStruct((devices // FIELDS, LANES), jnp.int32),
            f32(3, wide, tall, depth),
            f32(3, size_x, size_y, depth),
            f32(wide, tall, depth),
            f32(wide, tall, depth),
        ],
        in_specs=[pl.BlockSpec(memory_space=pltpu.HBM)] * 8,
        out_specs=in_vmem(6),
        scratch_shapes=[
            *(pltpu.VMEM(a.shape, a.dtype) for a in (data, tile, cell, comp)),
            pltpu.VMEM((3, wide, tall, depth), jnp.float32),
            rows(),
            rows(),
            rows(),
            rows(),
            pltpu.VMEM((count, size_x, 1, depth), jnp.float32),
            pltpu.VMEM((count, size_x, 1, depth), jnp.float32),
            pltpu.VMEM((count, wide, 1, depth), jnp.float32),
            pltpu.VMEM((count, wide, 1, depth), jnp.float32),
            pltpu.SemaphoreType.DMA((8,)),
            pltpu.SemaphoreType.DMA((ny - 1,)),
            pltpu.SemaphoreType.DMA((ny - 1,)),
            pltpu.SemaphoreType.DMA((nx - 1,)),
            pltpu.SemaphoreType.DMA((nx - 1,)),
            pltpu.SemaphoreType.DMA((14,)),
            pltpu.SemaphoreType.DMA((14,)),
        ],
        compiler_params=pltpu.CompilerParams(
            collective_id=0, has_side_effects=True, vmem_limit_bytes=16 * MIB
        ),
        name="route",
    )(*(pltpu.with_memory_space_constraint(a, pltpu.HBM) for a in inputs))


def scatter_kernel(cap, code_ref, got_ref, out_ref, quad, wide):
    devices = got_ref.shape[0]
    got = got_ref[...]
    lane = lax.broadcasted_iota(jnp.int32, (devices, LANES), 1)
    slot = jnp.bitwise_and(lane, SPAN - 1)
    codes = jnp.where(lane >= (FIELDS - 1) * SPAN, got, 0.0)
    codes = codes + pltpu.roll(codes, SPAN, 1)
    codes = codes + pltpu.roll(codes, 2 * SPAN, 1)
    total = got
    place_in_group = slot - slot // GROUP * GROUP
    for d in range(1, GROUP):
        same = (codes == pltpu.roll(codes, d, 1)) & (place_in_group >= d)
        total = total + jnp.where(same, pltpu.roll(got, d, 1), 0.0)
    for t in range(FIELDS):
        quad[pl.ds(t, devices, stride=FIELDS), :] = jnp.where(
            (lane >= t * SPAN) & (lane < (t + 1) * SPAN), total, 0.0
        )
    values = quad[...]
    high = values.astype(jnp.bfloat16)
    low = (values - high.astype(jnp.float32)).astype(jnp.bfloat16)
    terms = jnp.concatenate([high, low], axis=1)
    row_slot = jnp.bitwise_and(lax.broadcasted_iota(jnp.int32, (2 * LANES, 2 * LANES), 0), SPAN - 1)
    column = lax.broadcasted_iota(jnp.int32, (2 * LANES, 2 * LANES), 1) // LANES
    for i in range(0, cap, 2):
        pick = (row_slot == column + i).astype(jnp.bfloat16)
        both = mm(terms, pick)
        wide[i] = both[:, :LANES]
        wide[i + 1] = both[:, LANES:]

    rows = out_ref.shape[0]
    step = 128

    def clear(n, _):
        out_ref[pl.ds(pl.multiple_of(n * step, step), step), :] = jnp.zeros((step, LANES), jnp.float32)
        return 0

    lax.fori_loop(0, rows // step, clear, 0)
    depth = lax.broadcasted_iota(jnp.int32, (FIELDS, LANES), 1)

    def place(q, _):
        for p in range(FIELDS):
            s = q * FIELDS + p
            for start in range(0, cap, GROUP):
                where, news = [], []
                for i in range(start, min(cap, start + GROUP)):
                    word = code_ref[q, p * SPAN + i]
                    row = pl.ds(pl.multiple_of(lax.shift_right_logical(word, 7), FIELDS), FIELDS)
                    news.append(out_ref[row, :] + wide[i, pl.ds(pl.multiple_of(s * FIELDS, FIELDS), FIELDS), :])
                    column = jnp.bitwise_and(jnp.full((FIELDS, LANES), word, jnp.int32), LANES - 1)
                    where.append((row, depth == column))
                for (row, mask), new in zip(where, news):
                    pltpu.store(out_ref.at[row, :], new, mask=mask)
        return 0

    lax.fori_loop(0, devices // FIELDS, place, 0)


def scatter(cap, rows, codes, got):
    devices = got.shape[0]
    return pl.pallas_call(
        functools.partial(scatter_kernel, cap),
        out_shape=jax.ShapeDtypeStruct((rows * FIELDS, LANES), jnp.float32),
        in_specs=[pl.BlockSpec(memory_space=pltpu.SMEM), pl.BlockSpec(memory_space=pltpu.VMEM)],
        out_specs=pl.BlockSpec(memory_space=pltpu.VMEM),
        scratch_shapes=[
            pltpu.VMEM((devices * FIELDS, LANES), jnp.float32),
            pltpu.VMEM((cap, devices * FIELDS, LANES), jnp.float32),
        ],
        compiler_params=pltpu.CompilerParams(vmem_limit_bytes=24 * MIB),
        name="scatter",
    )(codes, got)


def share_kernel(
    nx, ny, base, gain, src, fwd, e, src1, grad, dn_put, up_put, up_got, lo_got, send, recv
):
    place = Place(nx, ny)
    size_x, size_y, depth = base.shape[1:]
    barrier = pltpu.get_barrier_semaphore()
    others = place.sides() + place.corners()
    for other in others:
        pl.semaphore_signal(barrier, inc=1, device_id=other, device_id_type=MESH)

    def own(x, _):
        p = x + 2
        rise = gain[p, :size_y]
        for c in range(3):
            new = base[c, x] - rise * src[c, x, pl.ds(0, size_y, stride=FIELDS), :]
            e[c, p, :size_y] = new
            source = src[c, x, pl.ds(1, size_y, stride=FIELDS), :]
            src1[c, p, :size_y] = source
            for r in range(2):
                dn_put[2 * c + r, x] = new[r : r + 1]
                up_put[2 * c + r, x] = new[size_y - 2 + r : size_y - 1 + r]
            dn_put[6 + c, x] = source[:1]
            up_put[6 + c, x] = source[size_y - 1 :]
        return 0

    lax.fori_loop(0, size_x, own, 0)
    pl.semaphore_wait(barrier, len(others))
    copies = start_copies(
        row_copies(dn_put, up_put, up_got, lo_got, size_x, place)
        + plane_copies(e, 2, size_x, size_y, place)
        + plane_copies(src1, 1, size_x, size_y, place),
        send,
        recv,
    )

    def product(x, _):
        total = fwd[0, 0, x].astype(jnp.float32) * e[0, x + 2, :size_y]
        for c in (1, 2):
            total = total + fwd[0, c, x].astype(jnp.float32) * e[c, x + 2, :size_y]
        grad[x] = total
        return 0

    lax.fori_loop(0, size_x, product, 0)
    for copy in copies:
        copy.wait()
    for p in (0, 1, size_x + 2, size_x + 3):
        keep = place.plane(p, size_x)
        for c in range(3):
            e[c, p, :size_y] = e[c, p, :size_y] * keep

    def unstage(p, _):
        keep = place.plane(p, size_x)
        above, below = keep * place.keep_hi_y, keep * place.keep_lo_y
        gap = jnp.zeros((4, depth), jnp.float32)
        for c in range(3):
            n = 2 * c
            e[c, p, size_y:] = jnp.concatenate(
                [up_got[n, p] * above, up_got[n + 1, p] * above, gap, lo_got[n, p] * below, lo_got[n + 1, p] * below],
                axis=0,
            )
            src1[c, p, size_y:] = jnp.concatenate([up_got[6 + c, p], gap, gap[:2], lo_got[6 + c, p]], axis=0)
        return 0

    lax.fori_loop(0, size_x + 4, unstage, 0)


def share(nx, ny, base, gain, src, fwd):
    size_x, size_y, depth = base.shape[1:]
    wide, tall = size_x + 4, size_y + 8
    count = 9
    return pl.pallas_call(
        functools.partial(share_kernel, nx, ny),
        out_shape=[f32(3, wide, tall, depth), f32(3, wide, tall, depth), f32(size_x, size_y, depth)],
        in_specs=in_vmem(4),
        out_specs=in_vmem(3),
        scratch_shapes=[
            pltpu.VMEM((count, size_x, 1, depth), jnp.float32),
            pltpu.VMEM((count, size_x, 1, depth), jnp.float32),
            pltpu.VMEM((count, wide, 1, depth), jnp.float32),
            pltpu.VMEM((count, wide, 1, depth), jnp.float32),
            pltpu.SemaphoreType.DMA((10,)),
            pltpu.SemaphoreType.DMA((10,)),
        ],
        compiler_params=pltpu.CompilerParams(
            collective_id=1, has_side_effects=True, vmem_limit_bytes=6 * MIB
        ),
        name="share",
    )(base, gain, src, fwd)


def finish_kernel(
    nx, ny, e1, h1, decay, gain, src1, src, fwd, grad1, e_out, h_out, grad_out, e, h, grad, sem
):
    place = Place(nx, ny)
    size_x, size_y, depth = grad1.shape
    rows = size_y + 8
    moves = shifts(rows, depth)
    factor = h_factor(place, size_y, rows, depth)

    def h_second(p, _):
        h_plane(e1, h1, h, p, factor * place.plane(p, size_x), moves)
        return 0

    lax.fori_loop(0, size_x + 3, h_second, 0)

    def e_second(p, inner):
        fade, rise = decay[p], gain[p]
        total = None
        for c, curl in enumerate(curl_h(h, p, moves)):
            new = fade * e1[c, p] + rise * (curl - src1[c, p])
            e[c, p] = new
            if inner:
                term = fwd[1, c, p - 2].astype(jnp.float32) * new[:size_y]
                total = term if total is None else total + term
        if inner:
            grad[p - 2] = grad1[p - 2] + total

    e_second(1, False)

    def e_inner(x, _):
        e_second(x + 2, True)
        return 0

    lax.fori_loop(0, size_x, e_inner, 0)
    e_second(size_x + 2, False)

    def h_third(p, _):
        h_plane(e, h, h, p, factor * place.plane(p, size_x), moves)
        return 0

    lax.fori_loop(1, size_x + 2, h_third, 0)
    inside = pl.ds(0, size_y)
    outs = [pltpu.make_async_copy(h.at[:, pl.ds(2, size_x), inside], h_out, sem.at[0])]
    outs[0].start()

    def e_third(x, _):
        p = x + 2
        fade, rise = decay[p, :size_y], gain[p, :size_y]
        total = grad[x]
        for c, curl in enumerate(curl_h(h, p, moves)):
            source = src[c, x, pl.ds(2, size_y, stride=FIELDS), :]
            new = fade * e[c, p, :size_y] + rise * (curl[:size_y] - source)
            e[c, p, :size_y] = new
            total = total + fwd[2, c, x].astype(jnp.float32) * new
        grad[x] = total
        return 0

    parts = 4
    each = size_x // parts
    for k in range(parts):
        lax.fori_loop(k * each, (k + 1) * each, e_third, 0)
        here = pl.ds(k * each, each)
        outs.append(
            pltpu.make_async_copy(
                e.at[:, pl.ds(2 + k * each, each), inside], e_out.at[:, here], sem.at[1 + 2 * k]
            )
        )
        outs.append(pltpu.make_async_copy(grad.at[here], grad_out.at[here], sem.at[2 + 2 * k]))
        outs[-2].start()
        outs[-1].start()
    for copy in outs:
        copy.wait()


def finish(nx, ny, e1, h1, decay, gain, src1, src, fwd, grad1):
    size_x, size_y, depth = grad1.shape
    field = f32(3, size_x, size_y, depth)
    return pl.pallas_call(
        functools.partial(finish_kernel, nx, ny),
        out_shape=[field, field, f32(size_x, size_y, depth)],
        in_specs=in_vmem(8),
        out_specs=[pl.BlockSpec(memory_space=pltpu.HBM)] * 3,
        scratch_shapes=[
            pltpu.VMEM(e1.shape, jnp.float32),
            pltpu.VMEM(h1.shape, jnp.float32),
            pltpu.VMEM(grad1.shape, jnp.float32),
            pltpu.SemaphoreType.DMA((9,)),
        ],
        compiler_params=pltpu.CompilerParams(vmem_limit_bytes=10 * MIB),
        name="finish",
    )(e1, h1, decay, gain, src1, src, fwd, grad1)


def per_device(
    e_adjoint,
    h_adjoint,
    conductivity,
    permittivity,
    forward_e,
    receiver_data,
    receiver_tile,
    receiver_cell,
    receiver_comp,
):
    _, size_x, size_y, depth = e_adjoint.shape
    nx, ny = lax.axis_size("gx"), lax.axis_size("gy")
    receivers = receiver_data.shape[0]
    cap = 3 * receivers // (nx * ny)
    by_lane = lambda a: a.reshape(receivers // LANES, LANES)
    got, codes, h1, base, decay, gain = route(
        nx,
        ny,
        receiver_data,
        by_lane(receiver_tile),
        by_lane(receiver_cell),
        by_lane(receiver_comp),
        e_adjoint,
        h_adjoint,
        conductivity,
        permittivity,
    )
    placed = scatter(cap, 3 * size_x * size_y, codes, got)
    placed = placed.reshape(3, size_x, size_y * FIELDS, depth)
    e1, src1, grad1 = share(nx, ny, base, gain, placed, forward_e)
    return tuple(finish(nx, ny, e1, h1, decay, gain, src1, placed, forward_e, grad1))


def solution(mesh):
    placed = (
        P(None, "gx", "gy", None),
        P(None, "gx", "gy", None),
        P("gx", "gy", None),
        P("gx", "gy", None),
        P(None, None, "gx", "gy", None),
        P(("gx", "gy"), None),
        P(("gx", "gy"), None),
        P(("gx", "gy")),
        P(("gx", "gy")),
    )
    return jax.shard_map(
        per_device,
        mesh=mesh,
        in_specs=placed,
        out_specs=(P(None, "gx", "gy", None), P(None, "gx", "gy", None), P("gx", "gy", None)),
        check_vma=False,
    )
```

```python
import functools

import jax
import jax.numpy as jnp
from jax import lax
from jax.experimental import pallas as pl
from jax.experimental.pallas import tpu as pltpu
from jax.sharding import PartitionSpec as P

STEPS = 3
SAMPLES = 128
LANES = 128
FIELDS = 4
SPAN = LANES // FIELDS
MESH = pl.DeviceIdType.MESH
GROUP = 12
PARTS = 4
MIB = 1 << 20

time_step = 0.55


def split3(x):
    a = x.astype(jnp.bfloat16)
    rest = x - a.astype(jnp.float32)
    b = rest.astype(jnp.bfloat16)
    c = (rest - b.astype(jnp.float32)).astype(jnp.bfloat16)
    return a, b, c


def mm(a, b, contract=((1,), (0,))):
    return lax.dot_general(a, b, (contract, ((), ())), preferred_element_type=jnp.float32)


def time_kernel():
    rows = 8
    sample = lax.broadcasted_iota(jnp.int32, (rows, SAMPLES), 1).astype(jnp.float32)
    step = lax.broadcasted_iota(jnp.int32, (rows, SAMPLES), 0).astype(jnp.float32)
    centre = (step + 0.5) * (SAMPLES / STEPS)
    spread = SAMPLES / (4.0 * STEPS)
    kernel = jnp.exp(-jnp.square((sample - centre) / spread))
    kernel = jnp.where(step < STEPS - 0.5, kernel, 0.0)
    norm = jnp.sum(kernel * kernel, axis=1, keepdims=True)
    return kernel / jnp.sqrt(jnp.where(norm > 0.0, norm, 1.0))


def pack(devices, cells, data_ref, tile_ref, cell_ref, comp_ref):
    blocks, width = tile_ref.shape
    kernel = time_kernel()
    before = (
        lax.broadcasted_iota(jnp.int32, (width, width), 0)
        < lax.broadcasted_iota(jnp.int32, (width, width), 1)
    ).astype(jnp.bfloat16)
    every = jnp.ones((width, width), jnp.bfloat16)
    destination = lax.broadcasted_iota(jnp.int32, (devices, width), 0)
    slot = lax.broadcasted_iota(jnp.int32, (SPAN, width), 0).astype(jnp.float32)
    seen = jnp.zeros((devices, width), jnp.float32)
    packed = jnp.zeros((devices, LANES), jnp.float32)
    for b in range(blocks):
        onehot = (destination == tile_ref[b : b + 1, :]).astype(jnp.float32)
        hot = onehot.astype(jnp.bfloat16)
        rank = jnp.sum(onehot * (seen + mm(hot, before)), axis=0, keepdims=True)
        seen = seen + mm(hot, every)
        amplitude = lax.dot_general(
            kernel,
            data_ref[b * width : (b + 1) * width, :],
            (((1,), (1,)), ((), ())),
            precision=lax.Precision.HIGHEST,
            preferred_element_type=jnp.float32,
        )
        code = (comp_ref[b : b + 1, :] * cells + cell_ref[b : b + 1, :]).astype(jnp.float32)
        here = slot == rank
        fields = [amplitude[t : t + 1, :] for t in range(STEPS)] + [code]
        spread = jnp.concatenate([jnp.where(here, f, 0.0) for f in fields], axis=0)
        for term in split3(spread):
            packed = packed + mm(hot, term, ((1,), (1,)))
    return packed


def sweep(start, count, body, width):
    def several(n, _):
        for k in range(width):
            body(start + n * width + k)
        return 0

    turns = count // width
    lax.fori_loop(0, turns, several, 0)
    for p in range(turns * width, count):
        body(start + p)


class Place:
    def __init__(self, nx, ny):
        self.nx, self.ny = nx, ny
        self.ix, self.iy = lax.axis_index("gx"), lax.axis_index("gy")
        self.lo_x, self.hi_x = lax.rem(self.ix + nx - 1, nx), lax.rem(self.ix + 1, nx)
        self.lo_y, self.hi_y = lax.rem(self.iy + ny - 1, ny), lax.rem(self.iy + 1, ny)
        one, zero = jnp.float32(1.0), jnp.float32(0.0)
        self.keep_lo_x = jnp.where(self.ix == 0, zero, one)
        self.keep_hi_x = jnp.where(self.ix == nx - 1, zero, one)
        self.keep_lo_y = jnp.where(self.iy == 0, zero, one)
        self.keep_hi_y = jnp.where(self.iy == ny - 1, zero, one)

    def corners(self):
        return [(x, y) for x in (self.lo_x, self.hi_x) for y in (self.lo_y, self.hi_y)]

    def sides(self):
        return [(self.lo_x, self.iy), (self.hi_x, self.iy), (self.ix, self.lo_y), (self.ix, self.hi_y)]

    def plane(self, p, size_x):
        return jnp.where(p < 2, self.keep_lo_x, jnp.where(p >= size_x + 2, self.keep_hi_x, 1.0))


def shifts(rows, depth):
    lane = lax.broadcasted_iota(jnp.int32, (rows, depth), 1)

    def up_z(f):
        return jnp.where(lane == depth - 1, 0.0, pltpu.roll(f, depth - 1, 1))

    def down_z(f):
        return jnp.where(lane == 0, 0.0, pltpu.roll(f, 1, 1))

    def up_y(f):
        return pltpu.roll(f, rows - 1, 0)

    def down_y(f):
        return pltpu.roll(f, 1, 0)

    return up_z, down_z, up_y, down_y


def h_plane(e, h_from, h_to, p, factor, moves):
    up_z, _, up_y, _ = moves
    ex, ey, ez = e[0, p], e[1, p], e[2, p]
    curl_x = (up_y(ez) - ez) - (up_z(ey) - ey)
    curl_y = (up_z(ex) - ex) - (e[2, p + 1] - ez)
    curl_z = (e[1, p + 1] - ey) - (up_y(ex) - ex)
    for c, curl in enumerate((curl_x, curl_y, curl_z)):
        h_to[c, p] = h_from[c, p] - factor * curl


def curl_h(h, p, moves):
    _, down_z, _, down_y = moves
    hx, hy, hz = h[0, p], h[1, p], h[2, p]
    curl_x = (hz - down_y(hz)) - (hy - down_z(hy))
    curl_y = (hx - down_z(hx)) - (hz - h[2, p - 1])
    curl_z = (hy - h[1, p - 1]) - (hx - down_y(hx))
    return curl_x, curl_y, curl_z


def h_factor(place, size_y, rows, depth):
    row = lax.broadcasted_iota(jnp.int32, (rows, depth), 0)
    beyond = jnp.where(row < size_y + 4, place.keep_hi_y, place.keep_lo_y)
    return time_step * jnp.where(row < size_y, 1.0, beyond)


def row_copies(dn_put, up_put, up_got, lo_got, size_x, place):
    first, last, low, high = pl.ds(0, 2), pl.ds(size_x - 2, 2), pl.ds(0, 2), pl.ds(size_x + 2, 2)
    whole = pl.ds(2, size_x)
    return [
        (dn_put, up_got.at[:, whole], (place.ix, place.lo_y)),
        (up_put, lo_got.at[:, whole], (place.ix, place.hi_y)),
        (dn_put.at[:, first], up_got.at[:, high], (place.lo_x, place.lo_y)),
        (dn_put.at[:, last], up_got.at[:, low], (place.hi_x, place.lo_y)),
        (up_put.at[:, first], lo_got.at[:, high], (place.lo_x, place.hi_y)),
        (up_put.at[:, last], lo_got.at[:, low], (place.hi_x, place.hi_y)),
    ]


def plane_copies(array, count, size_x, size_y, place):
    lead = (slice(None),) * (len(array.shape) - 3)
    rows = pl.ds(0, size_y)

    def part(start):
        return array.at[(*lead, pl.ds(start, count), rows)]

    return [
        (part(2), part(size_x + 2), (place.lo_x, place.iy)),
        (part(size_x + 2 - count), part(2 - count), (place.hi_x, place.iy)),
    ]


def start_copies(parts, send, recv):
    copies = [
        pltpu.make_async_remote_copy(
            src_ref=a,
            dst_ref=b,
            send_sem=send.at[n],
            recv_sem=recv.at[n],
            device_id=device,
            device_id_type=MESH,
        )
        for n, (a, b, device) in enumerate(parts)
    ]
    for copy in copies:
        copy.start()
    return copies


def route_kernel(
    nx,
    ny,
    cells,
    data_in,
    tile_in,
    cell_in,
    comp_in,
    e_in,
    h_in,
    cond_in,
    perm_in,
    got_ref,
    code_ref,
    h,
    base,
    decay,
    gain,
    data_ref,
    tile_ref,
    cell_ref,
    comp_ref,
    e,
    first,
    mid,
    second,
    last,
    dn_put,
    up_put,
    up_got,
    lo_got,
    load,
    send_y,
    recv_y,
    send_x,
    recv_x,
    send,
    recv,
):
    place = Place(nx, ny)
    ix, iy = place.ix, place.iy
    size_x, size_y, depth = base.shape[1:]
    rows = size_y + 8
    inner = (pl.ds(2, size_x), pl.ds(0, size_y))
    pairs = (
        (tile_in, tile_ref),
        (cell_in, cell_ref),
        (comp_in, comp_ref),
        (data_in, data_ref),
        (e_in, e.at[:, inner[0], inner[1]]),
        (h_in, h.at[:, inner[0], inner[1]]),
        (cond_in, decay.at[inner[0], inner[1]]),
        (perm_in, gain.at[inner[0], inner[1]]),
    )
    loads = [pltpu.make_async_copy(a, b, load.at[n]) for n, (a, b) in enumerate(pairs)]
    for copy in loads:
        copy.start()
    barrier = pltpu.get_barrier_semaphore()
    for k in range(1, nx):
        pl.semaphore_signal(barrier, inc=1, device_id=(lax.rem(ix + k, nx), iy), device_id_type=MESH)
    for k in range(1, ny):
        pl.semaphore_signal(barrier, inc=1, device_id=(ix, lax.rem(iy + k, ny)), device_id_type=MESH)
    for other in place.corners():
        pl.semaphore_signal(barrier, inc=1, device_id=other, device_id_type=MESH)
    for copy in loads:
        copy.wait()

    def stage(x):
        p = x + 2
        n = 0
        for array in (e, h):
            for c in range(3):
                for r in range(2):
                    dn_put[n, x] = array[c, p, r : r + 1, :]
                    up_put[n, x] = array[c, p, size_y - 2 + r : size_y - 1 + r, :]
                    n += 1
        for array in (decay, gain):
            dn_put[n, x] = array[p, 0:1, :]
            up_put[n, x] = array[p, size_y - 1 : size_y, :]
            n += 1

    sweep(0, size_x, stage, 4)
    pl.semaphore_wait(barrier, nx + ny + 2)
    halos = start_copies(
        row_copies(dn_put, up_put, up_got, lo_got, size_x, place)
        + plane_copies(e, 2, size_x, size_y, place)
        + plane_copies(h, 2, size_x, size_y, place)
        + plane_copies(decay, 1, size_x, size_y, place)
        + plane_copies(gain, 1, size_x, size_y, place),
        send,
        recv,
    )
    first[...] = pack(nx * ny, cells, data_ref, tile_ref, cell_ref, comp_ref)

    copies = []
    for k in range(1, nx):
        to = lax.rem(ix + k, nx)
        copy = pltpu.make_async_remote_copy(
            src_ref=first.at[pl.ds(pl.multiple_of(to * ny, ny), ny), :],
            dst_ref=mid.at[pl.ds(pl.multiple_of(ix * ny, ny), ny), :],
            send_sem=send_x.at[k - 1],
            recv_sem=recv_x.at[k - 1],
            device_id=(to, iy),
            device_id_type=MESH,
        )
        copy.start()
        copies.append(copy)
    own = pl.ds(pl.multiple_of(ix * ny, ny), ny)
    mid[own, :] = first[own, :]
    for copy in copies:
        copy.wait_recv()
    for j in range(ny):
        second[j * nx : (j + 1) * nx, :] = mid[pl.ds(j, nx, stride=ny), :]
    later = []
    for k in range(1, ny):
        to = lax.rem(iy + k, ny)
        copy = pltpu.make_async_remote_copy(
            src_ref=second.at[pl.ds(pl.multiple_of(to * nx, nx), nx), :],
            dst_ref=last.at[pl.ds(pl.multiple_of(iy * nx, nx), nx), :],
            send_sem=send_y.at[k - 1],
            recv_sem=recv_y.at[k - 1],
            device_id=(ix, to),
            device_id_type=MESH,
        )
        copy.start()
        later.append(copy)
    own = pl.ds(pl.multiple_of(iy * nx, nx), nx)
    last[own, :] = second[own, :]
    for copy in copies:
        copy.wait_send()

    for copy in halos:
        copy.wait()
    for p in (0, 1, size_x + 2, size_x + 3):
        keep = place.plane(p, size_x)
        for c in range(3):
            for array in (e, h):
                array[c, p, :size_y] = array[c, p, :size_y] * keep

    def unstage(p):
        keep = place.plane(p, size_x)
        above, below = keep * place.keep_hi_y, keep * place.keep_lo_y
        n = 0
        gap = jnp.zeros((4, depth), jnp.float32)
        for array in (e, h):
            for c in range(3):
                array[c, p, size_y:] = jnp.concatenate(
                    [up_got[n, p] * above, up_got[n + 1, p] * above, gap, lo_got[n, p] * below, lo_got[n + 1, p] * below],
                    axis=0,
                )
                n += 2

    sweep(0, size_x + 4, unstage, 4)
    row = lax.broadcasted_iota(jnp.int32, (rows, depth), 0)
    inside = jnp.where(
        row < size_y,
        1.0,
        jnp.where(row == size_y, place.keep_hi_y, jnp.where(row == rows - 1, place.keep_lo_y, 0.0)),
    )
    ones = jnp.ones((6, depth), jnp.float32)

    def coefficients(p):
        decay[p, size_y:] = jnp.concatenate([up_got[12, p], ones, lo_got[12, p]], axis=0)
        gain[p, size_y:] = jnp.concatenate([up_got[13, p], ones, lo_got[13, p]], axis=0)
        half_loss = decay[p] * (0.5 * time_step)
        eps = gain[p]
        inverse = 1.0 / (eps + half_loss)
        keep = inside * place.plane(p, size_x)
        decay[p] = (eps - half_loss) * inverse * keep
        gain[p] = time_step * inverse * keep

    sweep(1, size_x + 2, coefficients, 2)
    moves = shifts(rows, depth)
    factor = h_factor(place, size_y, rows, depth)

    def h_step(p):
        h_plane(e, h, h, p, factor * place.plane(p, size_x), moves)

    sweep(0, size_x + 3, h_step, 7)

    def e_step(x):
        p = x + 2
        for c, curl in enumerate(curl_h(h, p, moves)):
            new = decay[p] * e[c, p] + gain[p] * curl
            base[c, x] = new[:size_y]

    sweep(0, size_x, e_step, 8)

    for copy in later:
        copy.wait()
    got_ref[...] = last[...]
    quarter = nx * ny // FIELDS
    lane = lax.broadcasted_iota(jnp.int32, (quarter, LANES), 1) // SPAN
    codes = jnp.zeros((quarter, LANES), jnp.int32)
    for k in range(FIELDS):
        code = last[pl.ds(k, quarter, stride=FIELDS), :].astype(jnp.int32)
        word = jnp.bitwise_and(code, LANES - 1) + jnp.bitwise_and(code, -LANES) * FIELDS
        codes = jnp.where(lane == k, pltpu.roll(word, (k + 1) * SPAN % LANES, 1), codes)
    code_ref[...] = codes


def in_vmem(count):
    return [pl.BlockSpec(memory_space=pltpu.VMEM)] * count


def f32(*shape):
    return jax.ShapeDtypeStruct(shape, jnp.float32)


def route(nx, ny, data, tile, cell, comp, e, h, cond, perm):
    devices = nx * ny
    size_x, size_y, depth = cond.shape
    wide, tall = size_x + 4, size_y + 8
    inputs = (data, tile, cell, comp, e, h, cond, perm)
    rows = lambda: pltpu.VMEM((devices, LANES), jnp.float32)
    count = 14
    return pl.pallas_call(
        functools.partial(route_kernel, nx, ny, size_x * size_y * depth),
        out_shape=[
            f32(devices, LANES),
            jax.ShapeDtypeStruct((devices // FIELDS, LANES), jnp.int32),
            f32(3, wide, tall, depth),
            f32(3, size_x, size_y, depth),
            f32(wide, tall, depth),
            f32(wide, tall, depth),
        ],
        in_specs=[pl.BlockSpec(memory_space=pltpu.HBM)] * 8,
        out_specs=in_vmem(6),
        scratch_shapes=[
            *(pltpu.VMEM(a.shape, a.dtype) for a in (data, tile, cell, comp)),
            pltpu.VMEM((3, wide, tall, depth), jnp.float32),
            rows(),
            rows(),
            rows(),
            rows(),
            pltpu.VMEM((count, size_x, 1, depth), jnp.float32),
            pltpu.VMEM((count, size_x, 1, depth), jnp.float32),
            pltpu.VMEM((count, wide, 1, depth), jnp.float32),
            pltpu.VMEM((count, wide, 1, depth), jnp.float32),
            pltpu.SemaphoreType.DMA((8,)),
            pltpu.SemaphoreType.DMA((ny - 1,)),
            pltpu.SemaphoreType.DMA((ny - 1,)),
            pltpu.SemaphoreType.DMA((nx - 1,)),
            pltpu.SemaphoreType.DMA((nx - 1,)),
            pltpu.SemaphoreType.DMA((14,)),
            pltpu.SemaphoreType.DMA((14,)),
        ],
        compiler_params=pltpu.CompilerParams(
            collective_id=0, has_side_effects=True, vmem_limit_bytes=16 * MIB
        ),
        name="route",
    )(*(pltpu.with_memory_space_constraint(a, pltpu.HBM) for a in inputs))


def scatter_kernel(cap, code_ref, got_ref, out_ref, quad, wide):
    devices = got_ref.shape[0]
    got = got_ref[...]
    lane = lax.broadcasted_iota(jnp.int32, (devices, LANES), 1)
    slot = jnp.bitwise_and(lane, SPAN - 1)
    codes = jnp.where(lane >= (FIELDS - 1) * SPAN, got, 0.0)
    codes = codes + pltpu.roll(codes, SPAN, 1)
    codes = codes + pltpu.roll(codes, 2 * SPAN, 1)
    total = got
    place_in_group = slot - slot // GROUP * GROUP
    for d in range(1, GROUP):
        same = (codes == pltpu.roll(codes, d, 1)) & (place_in_group >= d)
        total = total + jnp.where(same, pltpu.roll(got, d, 1), 0.0)
    for t in range(FIELDS):
        quad[pl.ds(t, devices, stride=FIELDS), :] = jnp.where(
            (lane >= t * SPAN) & (lane < (t + 1) * SPAN), total, 0.0
        )
    values = quad[...]
    high = values.astype(jnp.bfloat16)
    low = (values - high.astype(jnp.float32)).astype(jnp.bfloat16)
    terms = jnp.concatenate([high, low], axis=1)
    row_slot = jnp.bitwise_and(lax.broadcasted_iota(jnp.int32, (2 * LANES, 2 * LANES), 0), SPAN - 1)
    column = lax.broadcasted_iota(jnp.int32, (2 * LANES, 2 * LANES), 1) // LANES
    for i in range(0, cap, 2):
        pick = (row_slot == column + i).astype(jnp.bfloat16)
        both = mm(terms, pick)
        wide[i] = both[:, :LANES]
        wide[i + 1] = both[:, LANES:]

    rows = out_ref.shape[0]
    step = 128

    def clear(n, _):
        out_ref[pl.ds(pl.multiple_of(n * step, step), step), :] = jnp.zeros((step, LANES), jnp.float32)
        return 0

    lax.fori_loop(0, rows // step, clear, 0)
    depth = lax.broadcasted_iota(jnp.int32, (FIELDS, LANES), 1)

    def place(q, _):
        for p in range(FIELDS):
            s = q * FIELDS + p
            for start in range(0, cap, GROUP):
                where, news = [], []
                for i in range(start, min(cap, start + GROUP)):
                    word = code_ref[q, p * SPAN + i]
                    row = pl.ds(pl.multiple_of(lax.shift_right_logical(word, 7), FIELDS), FIELDS)
                    news.append(out_ref[row, :] + wide[i, pl.ds(pl.multiple_of(s * FIELDS, FIELDS), FIELDS), :])
                    column = jnp.bitwise_and(jnp.full((FIELDS, LANES), word, jnp.int32), LANES - 1)
                    where.append((row, depth == column))
                for (row, mask), new in zip(where, news):
                    pltpu.store(out_ref.at[row, :], new, mask=mask)
        return 0

    lax.fori_loop(0, devices // FIELDS, place, 0)


def scatter(cap, rows, codes, got):
    devices = got.shape[0]
    return pl.pallas_call(
        functools.partial(scatter_kernel, cap),
        out_shape=jax.ShapeDtypeStruct((rows * FIELDS, LANES), jnp.float32),
        in_specs=[pl.BlockSpec(memory_space=pltpu.SMEM), pl.BlockSpec(memory_space=pltpu.VMEM)],
        out_specs=pl.BlockSpec(memory_space=pltpu.VMEM),
        scratch_shapes=[
            pltpu.VMEM((devices * FIELDS, LANES), jnp.float32),
            pltpu.VMEM((cap, devices * FIELDS, LANES), jnp.float32),
        ],
        compiler_params=pltpu.CompilerParams(vmem_limit_bytes=24 * MIB),
        name="scatter",
    )(codes, got)


def share_kernel(
    nx, ny, base, gain, src, fwd, e, src1, grad, dn_put, up_put, up_got, lo_got, send, recv
):
    place = Place(nx, ny)
    size_x, size_y, depth = base.shape[1:]
    barrier = pltpu.get_barrier_semaphore()
    others = place.sides() + place.corners()
    for other in others:
        pl.semaphore_signal(barrier, inc=1, device_id=other, device_id_type=MESH)

    def own(x):
        p = x + 2
        rise = gain[p, :size_y]
        for c in range(3):
            new = base[c, x] - rise * src[c, x, pl.ds(0, size_y, stride=FIELDS), :]
            e[c, p, :size_y] = new
            source = src[c, x, pl.ds(1, size_y, stride=FIELDS), :]
            src1[c, p, :size_y] = source
            for r in range(2):
                dn_put[2 * c + r, x] = new[r : r + 1]
                up_put[2 * c + r, x] = new[size_y - 2 + r : size_y - 1 + r]
            dn_put[6 + c, x] = source[:1]
            up_put[6 + c, x] = source[size_y - 1 :]

    sweep(0, size_x, own, 4)
    pl.semaphore_wait(barrier, len(others))
    copies = start_copies(
        row_copies(dn_put, up_put, up_got, lo_got, size_x, place)
        + plane_copies(e, 2, size_x, size_y, place)
        + plane_copies(src1, 1, size_x, size_y, place),
        send,
        recv,
    )

    def product(x):
        total = fwd[0, 0, x].astype(jnp.float32) * e[0, x + 2, :size_y]
        for c in (1, 2):
            total = total + fwd[0, c, x].astype(jnp.float32) * e[c, x + 2, :size_y]
        grad[x] = total

    sweep(0, size_x, product, 4)
    for copy in copies:
        copy.wait()
    for p in (0, 1, size_x + 2, size_x + 3):
        keep = place.plane(p, size_x)
        for c in range(3):
            e[c, p, :size_y] = e[c, p, :size_y] * keep

    def unstage(p):
        keep = place.plane(p, size_x)
        above, below = keep * place.keep_hi_y, keep * place.keep_lo_y
        gap = jnp.zeros((4, depth), jnp.float32)
        for c in range(3):
            n = 2 * c
            e[c, p, size_y:] = jnp.concatenate(
                [up_got[n, p] * above, up_got[n + 1, p] * above, gap, lo_got[n, p] * below, lo_got[n + 1, p] * below],
                axis=0,
            )
            src1[c, p, size_y:] = jnp.concatenate([up_got[6 + c, p], gap, gap[:2], lo_got[6 + c, p]], axis=0)

    sweep(0, size_x + 4, unstage, 4)


def share(nx, ny, base, gain, src, fwd):
    size_x, size_y, depth = base.shape[1:]
    wide, tall = size_x + 4, size_y + 8
    count = 9
    return pl.pallas_call(
        functools.partial(share_kernel, nx, ny),
        out_shape=[f32(3, wide, tall, depth), f32(3, wide, tall, depth), f32(size_x, size_y, depth)],
        in_specs=in_vmem(4),
        out_specs=in_vmem(3),
        scratch_shapes=[
            pltpu.VMEM((count, size_x, 1, depth), jnp.float32),
            pltpu.VMEM((count, size_x, 1, depth), jnp.float32),
            pltpu.VMEM((count, wide, 1, depth), jnp.float32),
            pltpu.VMEM((count, wide, 1, depth), jnp.float32),
            pltpu.SemaphoreType.DMA((10,)),
            pltpu.SemaphoreType.DMA((10,)),
        ],
        compiler_params=pltpu.CompilerParams(
            collective_id=1, has_side_effects=True, vmem_limit_bytes=6 * MIB
        ),
        name="share",
    )(base, gain, src, fwd)


def finish_kernel(
    nx, ny, e1, h1, decay, gain, src1, src, fwd, grad1, e_out, h_out, grad_out, e, h, grad, sem
):
    place = Place(nx, ny)
    size_x, size_y, depth = grad1.shape
    rows = size_y + 8
    moves = shifts(rows, depth)
    factor = h_factor(place, size_y, rows, depth)

    def h_second(p):
        h_plane(e1, h1, h, p, factor * place.plane(p, size_x), moves)

    sweep(0, size_x + 3, h_second, 7)

    def e_second(p, inner):
        fade, rise = decay[p], gain[p]
        total = None
        for c, curl in enumerate(curl_h(h, p, moves)):
            new = fade * e1[c, p] + rise * (curl - src1[c, p])
            e[c, p] = new
            if inner:
                term = fwd[1, c, p - 2].astype(jnp.float32) * new[:size_y]
                total = term if total is None else total + term
        if inner:
            grad[p - 2] = grad1[p - 2] + total

    e_second(1, False)

    def e_inner(p):
        e_second(p, True)

    sweep(2, size_x, e_inner, 8)
    e_second(size_x + 2, False)

    def h_third(p):
        h_plane(e, h, h, p, factor * place.plane(p, size_x), moves)

    sweep(1, size_x + 1, h_third, 11)
    inside = pl.ds(0, size_y)
    h_copy = pltpu.make_async_copy(h.at[:, pl.ds(2, size_x), inside], h_out, sem.at[0])
    h_copy.start()

    def e_third(x):
        p = x + 2
        fade, rise = decay[p, :size_y], gain[p, :size_y]
        total = grad[x]
        for c, curl in enumerate(curl_h(h, p, moves)):
            source = src[c, x, pl.ds(2, size_y, stride=FIELDS), :]
            new = fade * e[c, p, :size_y] + rise * (curl[:size_y] - source)
            e[c, p, :size_y] = new
            total = total + fwd[2, c, x].astype(jnp.float32) * new
        grad[x] = total

    each = size_x // PARTS

    def results(k):
        here = pl.ds(k * each, each)
        return (
            pltpu.make_async_copy(e.at[:, pl.ds(2 + k * each, each), inside], e_out.at[:, here], sem.at[1 + 2 * k]),
            pltpu.make_async_copy(grad.at[here], grad_out.at[here], sem.at[2 + 2 * k]),
        )

    def part(k, _):
        for x in range(each):
            e_third(k * each + x)
        for copy in results(k):
            copy.start()
        return 0

    lax.fori_loop(0, PARTS, part, 0)
    h_copy.wait()
    for k in range(PARTS):
        for copy in results(k):
            copy.wait()


def finish(nx, ny, e1, h1, decay, gain, src1, src, fwd, grad1):
    size_x, size_y, depth = grad1.shape
    field = f32(3, size_x, size_y, depth)
    return pl.pallas_call(
        functools.partial(finish_kernel, nx, ny),
        out_shape=[field, field, f32(size_x, size_y, depth)],
        in_specs=in_vmem(8),
        out_specs=[pl.BlockSpec(memory_space=pltpu.HBM)] * 3,
        scratch_shapes=[
            pltpu.VMEM(e1.shape, jnp.float32),
            pltpu.VMEM(h1.shape, jnp.float32),
            pltpu.VMEM(grad1.shape, jnp.float32),
            pltpu.SemaphoreType.DMA((1 + 2 * PARTS,)),
        ],
        compiler_params=pltpu.CompilerParams(vmem_limit_bytes=10 * MIB),
        name="finish",
    )(e1, h1, decay, gain, src1, src, fwd, grad1)


def per_device(
    e_adjoint,
    h_adjoint,
    conductivity,
    permittivity,
    forward_e,
    receiver_data,
    receiver_tile,
    receiver_cell,
    receiver_comp,
):
    _, size_x, size_y, depth = e_adjoint.shape
    nx, ny = lax.axis_size("gx"), lax.axis_size("gy")
    receivers = receiver_data.shape[0]
    cap = 3 * receivers // (nx * ny)
    by_lane = lambda a: a.reshape(receivers // LANES, LANES)
    got, codes, h1, base, decay, gain = route(
        nx,
        ny,
        receiver_data,
        by_lane(receiver_tile),
        by_lane(receiver_cell),
        by_lane(receiver_comp),
        e_adjoint,
        h_adjoint,
        conductivity,
        permittivity,
    )
    placed = scatter(cap, 3 * size_x * size_y, codes, got)
    placed = placed.reshape(3, size_x, size_y * FIELDS, depth)
    e1, src1, grad1 = share(nx, ny, base, gain, placed, forward_e)
    return tuple(finish(nx, ny, e1, h1, decay, gain, src1, placed, forward_e, grad1))


def solution(mesh):
    placed = (
        P(None, "gx", "gy", None),
        P(None, "gx", "gy", None),
        P("gx", "gy", None),
        P("gx", "gy", None),
        P(None, None, "gx", "gy", None),
        P(("gx", "gy"), None),
        P(("gx", "gy"), None),
        P(("gx", "gy")),
        P(("gx", "gy")),
    )
    return jax.shard_map(
        per_device,
        mesh=mesh,
        in_specs=placed,
        out_specs=(P(None, "gx", "gy", None), P(None, "gx", "gy", None), P("gx", "gy", None)),
        check_vma=False,
    )
```

```python
import functools

import jax
import jax.numpy as jnp
from jax import lax
from jax.experimental import pallas as pl
from jax.experimental.pallas import tpu as pltpu
from jax.sharding import PartitionSpec as P

STEPS = 3
SAMPLES = 128
LANES = 128
FIELDS = 4
SPAN = LANES // FIELDS
MESH = pl.DeviceIdType.MESH
GROUP = 8
PARTS = 4
MIB = 1 << 20

time_step = 0.55


def split3(x):
    a = x.astype(jnp.bfloat16)
    rest = x - a.astype(jnp.float32)
    b = rest.astype(jnp.bfloat16)
    c = (rest - b.astype(jnp.float32)).astype(jnp.bfloat16)
    return a, b, c


def mm(a, b, contract=((1,), (0,))):
    return lax.dot_general(a, b, (contract, ((), ())), preferred_element_type=jnp.float32)


def time_kernel():
    shape = (SAMPLES, LANES)
    sample = lax.broadcasted_iota(jnp.int32, shape, 0).astype(jnp.float32)
    field = lax.broadcasted_iota(jnp.int32, shape, 1) // SPAN
    centre = (field.astype(jnp.float32) + 0.5) * (SAMPLES / STEPS)
    spread = SAMPLES / (4.0 * STEPS)
    kernel = jnp.exp(-jnp.square((sample - centre) / spread))
    norm = jnp.sum(kernel * kernel, axis=0, keepdims=True)
    return jnp.where(field < STEPS, kernel / jnp.sqrt(norm), 0.0)


def pack(devices, cells, data_ref, tile_ref, cell_ref, comp_ref):
    blocks, width = tile_ref.shape
    kernel = time_kernel()
    at, to = (lax.broadcasted_iota(jnp.int32, (width, width), n) for n in (0, 1))
    before = (at < to).astype(jnp.bfloat16)
    every = jnp.ones((width, width), jnp.bfloat16)
    diagonal = at == to
    destination = lax.broadcasted_iota(jnp.int32, (devices, width), 0)
    lane = lax.broadcasted_iota(jnp.int32, (width, LANES), 1)
    slot = jnp.bitwise_and(lane, SPAN - 1).astype(jnp.float32)
    is_code = lane >= STEPS * SPAN
    down = jnp.ones((width, LANES), jnp.bfloat16)
    seen = jnp.zeros((devices, width), jnp.float32)
    packed = jnp.zeros((devices, LANES), jnp.float32)

    def column(row):
        return jnp.where(diagonal, row.astype(jnp.float32), 0.0).astype(jnp.bfloat16)

    for b in range(blocks):
        onehot = (destination == tile_ref[b : b + 1, :]).astype(jnp.float32)
        hot = onehot.astype(jnp.bfloat16)
        rank = jnp.sum(onehot * (seen + mm(hot, before)), axis=0, keepdims=True)
        seen = seen + mm(hot, every)
        amplitude = lax.dot_general(
            data_ref[b * width : (b + 1) * width, :],
            kernel,
            (((1,), (0,)), ((), ())),
            precision=lax.Precision.HIGHEST,
            preferred_element_type=jnp.float32,
        )
        code = comp_ref[b : b + 1, :] * cells + cell_ref[b : b + 1, :]
        low = jnp.bitwise_and(code, 255)
        middle = jnp.bitwise_and(code, 255 << 8)
        high = code - low - middle
        codes = mm(column(low), down) + mm(column(middle), down) + mm(column(high), down)
        spread = jnp.where(
            slot == mm(column(rank), down), jnp.where(is_code, codes, amplitude), 0.0
        )
        for term in split3(spread):
            packed = packed + mm(hot, term)
    return packed


def sweep(start, count, body, width):
    def several(n, _):
        for k in range(width):
            body(start + n * width + k)
        return 0

    turns = count // width
    lax.fori_loop(0, turns, several, 0)
    for p in range(turns * width, count):
        body(start + p)


class Place:
    def __init__(self, nx, ny):
        self.nx, self.ny = nx, ny
        self.ix, self.iy = lax.axis_index("gx"), lax.axis_index("gy")
        self.lo_x, self.hi_x = lax.rem(self.ix + nx - 1, nx), lax.rem(self.ix + 1, nx)
        self.lo_y, self.hi_y = lax.rem(self.iy + ny - 1, ny), lax.rem(self.iy + 1, ny)
        one, zero = jnp.float32(1.0), jnp.float32(0.0)
        self.keep_lo_x = jnp.where(self.ix == 0, zero, one)
        self.keep_hi_x = jnp.where(self.ix == nx - 1, zero, one)
        self.keep_lo_y = jnp.where(self.iy == 0, zero, one)
        self.keep_hi_y = jnp.where(self.iy == ny - 1, zero, one)

    def corners(self):
        return [(x, y) for x in (self.lo_x, self.hi_x) for y in (self.lo_y, self.hi_y)]

    def sides(self):
        return [(self.lo_x, self.iy), (self.hi_x, self.iy), (self.ix, self.lo_y), (self.ix, self.hi_y)]

    def plane(self, p, size_x):
        return jnp.where(p < 2, self.keep_lo_x, jnp.where(p >= size_x + 2, self.keep_hi_x, 1.0))


def shifts(rows, depth):
    lane = lax.broadcasted_iota(jnp.int32, (rows, depth), 1)

    def up_z(f):
        return jnp.where(lane == depth - 1, 0.0, pltpu.roll(f, depth - 1, 1))

    def down_z(f):
        return jnp.where(lane == 0, 0.0, pltpu.roll(f, 1, 1))

    def up_y(f):
        return pltpu.roll(f, rows - 1, 0)

    def down_y(f):
        return pltpu.roll(f, 1, 0)

    return up_z, down_z, up_y, down_y


def h_plane(e, h_from, h_to, p, factor, moves):
    up_z, _, up_y, _ = moves
    ex, ey, ez = e[0, p], e[1, p], e[2, p]
    curl_x = (up_y(ez) - ez) - (up_z(ey) - ey)
    curl_y = (up_z(ex) - ex) - (e[2, p + 1] - ez)
    curl_z = (e[1, p + 1] - ey) - (up_y(ex) - ex)
    for c, curl in enumerate((curl_x, curl_y, curl_z)):
        h_to[c, p] = h_from[c, p] - factor * curl


def curl_h(h, p, moves):
    _, down_z, _, down_y = moves
    hx, hy, hz = h[0, p], h[1, p], h[2, p]
    curl_x = (hz - down_y(hz)) - (hy - down_z(hy))
    curl_y = (hx - down_z(hx)) - (hz - h[2, p - 1])
    curl_z = (hy - h[1, p - 1]) - (hx - down_y(hx))
    return curl_x, curl_y, curl_z


def h_factor(place, size_y, rows, depth):
    row = lax.broadcasted_iota(jnp.int32, (rows, depth), 0)
    beyond = jnp.where(row < size_y + 4, place.keep_hi_y, place.keep_lo_y)
    return time_step * jnp.where(row < size_y, 1.0, beyond)


def row_copies(dn_put, up_put, up_got, lo_got, size_x, place):
    first, last, low, high = pl.ds(0, 2), pl.ds(size_x - 2, 2), pl.ds(0, 2), pl.ds(size_x + 2, 2)
    whole = pl.ds(2, size_x)
    return [
        (dn_put, up_got.at[:, whole], (place.ix, place.lo_y)),
        (up_put, lo_got.at[:, whole], (place.ix, place.hi_y)),
        (dn_put.at[:, first], up_got.at[:, high], (place.lo_x, place.lo_y)),
        (dn_put.at[:, last], up_got.at[:, low], (place.hi_x, place.lo_y)),
        (up_put.at[:, first], lo_got.at[:, high], (place.lo_x, place.hi_y)),
        (up_put.at[:, last], lo_got.at[:, low], (place.hi_x, place.hi_y)),
    ]


def plane_copies(array, count, size_x, size_y, place):
    lead = (slice(None),) * (len(array.shape) - 3)
    rows = pl.ds(0, size_y)

    def part(start):
        return array.at[(*lead, pl.ds(start, count), rows)]

    return [
        (part(2), part(size_x + 2), (place.lo_x, place.iy)),
        (part(size_x + 2 - count), part(2 - count), (place.hi_x, place.iy)),
    ]


FIELD_DOWN = ((0, 0, 0), (0, 1, 0), (0, 2, 0), (0, 0, 1), (0, 2, 1))
FIELD_UP = tuple((0, c, r) for c in range(3) for r in range(2))
ROUTE_DOWN = (*FIELD_DOWN, (1, 0, 0), (1, 1, 0), (1, 2, 0), (2, 0, 0), (3, 0, 0))
ROUTE_UP = (*FIELD_UP, (1, 0, 0), (1, 2, 0), (1, 0, 1), (1, 1, 1), (1, 2, 1), (2, 0, 1), (3, 0, 1))
SHARE_DOWN = (*FIELD_DOWN, (1, 0, 0), (1, 2, 0))
SHARE_UP = (*FIELD_UP, (1, 0, 1), (1, 1, 1), (1, 2, 1))


def halo_scratch(down, up, size_x, depth):
    shapes = [(len(down), size_x), (len(up), size_x), (len(down), size_x + 4), (len(up), size_x + 4)]
    return [pltpu.VMEM((*shape, 1, depth), jnp.float32) for shape in shapes]


def halo_rows(array, c, p, down, up, up_got, lo_got, above, below, fill):
    def one(names, got, r, keep):
        if (array, c, r) not in names:
            return fill
        return got[names.index((array, c, r)), p] * keep

    return jnp.concatenate(
        [one(down, up_got, 0, above), one(down, up_got, 1, above)]
        + [fill] * 4
        + [one(up, lo_got, 0, below), one(up, lo_got, 1, below)],
        axis=0,
    )


def start_copies(parts, send, recv):
    copies = [
        pltpu.make_async_remote_copy(
            src_ref=a,
            dst_ref=b,
            send_sem=send.at[n],
            recv_sem=recv.at[n],
            device_id=device,
            device_id_type=MESH,
        )
        for n, (a, b, device) in enumerate(parts)
    ]
    for copy in copies:
        copy.start()
    return copies


def route_kernel(
    nx,
    ny,
    cells,
    data_in,
    tile_in,
    cell_in,
    comp_in,
    e_in,
    h_in,
    cond_in,
    perm_in,
    got_ref,
    code_ref,
    h,
    base,
    decay,
    gain,
    data_ref,
    tile_ref,
    cell_ref,
    comp_ref,
    e,
    first,
    mid,
    second,
    last,
    dn_put,
    up_put,
    up_got,
    lo_got,
    load,
    send_y,
    recv_y,
    send_x,
    recv_x,
    send,
    recv,
):
    place = Place(nx, ny)
    ix, iy = place.ix, place.iy
    size_x, size_y, depth = base.shape[1:]
    rows = size_y + 8
    inner = (pl.ds(2, size_x), pl.ds(0, size_y))
    pairs = (
        (tile_in, tile_ref),
        (cell_in, cell_ref),
        (comp_in, comp_ref),
        (data_in, data_ref),
        (e_in, e.at[:, inner[0], inner[1]]),
        (h_in, h.at[:, inner[0], inner[1]]),
        (cond_in, decay.at[inner[0], inner[1]]),
        (perm_in, gain.at[inner[0], inner[1]]),
    )
    loads = [pltpu.make_async_copy(a, b, load.at[n]) for n, (a, b) in enumerate(pairs)]
    for copy in loads:
        copy.start()
    barrier = pltpu.get_barrier_semaphore()
    for k in range(1, nx):
        pl.semaphore_signal(barrier, inc=1, device_id=(lax.rem(ix + k, nx), iy), device_id_type=MESH)
    for k in range(1, ny):
        pl.semaphore_signal(barrier, inc=1, device_id=(ix, lax.rem(iy + k, ny)), device_id_type=MESH)
    for other in place.corners():
        pl.semaphore_signal(barrier, inc=1, device_id=other, device_id_type=MESH)
    for copy in loads[:4]:
        copy.wait()
    first[...] = pack(nx * ny, cells, data_ref, tile_ref, cell_ref, comp_ref)
    for copy in loads[4:]:
        copy.wait()

    def stage(x):
        p = x + 2
        arrays = ((e.at[0], e.at[1], e.at[2]), (h.at[0], h.at[1], h.at[2]), (decay,), (gain,))
        for n, (array, c, r) in enumerate(ROUTE_DOWN):
            dn_put[n, x] = arrays[array][c][p, r : r + 1, :]
        for n, (array, c, r) in enumerate(ROUTE_UP):
            up_put[n, x] = arrays[array][c][p, size_y - 2 + r : size_y - 1 + r, :]

    sweep(0, size_x, stage, 4)
    pl.semaphore_wait(barrier, nx + ny + 2)
    halos = start_copies(
        row_copies(dn_put, up_put, up_got, lo_got, size_x, place), send.at[0], recv.at[0]
    )
    copies = []
    for k in range(1, nx):
        to = lax.rem(ix + k, nx)
        copy = pltpu.make_async_remote_copy(
            src_ref=first.at[pl.ds(pl.multiple_of(to * ny, ny), ny), :],
            dst_ref=mid.at[pl.ds(pl.multiple_of(ix * ny, ny), ny), :],
            send_sem=send_x.at[k - 1],
            recv_sem=recv_x.at[k - 1],
            device_id=(to, iy),
            device_id_type=MESH,
        )
        copy.start()
        copies.append(copy)
    halos += start_copies(
        plane_copies(e, 2, size_x, size_y, place)
        + plane_copies(h, 2, size_x, size_y, place)
        + plane_copies(decay, 1, size_x, size_y, place)
        + plane_copies(gain, 1, size_x, size_y, place),
        send.at[1],
        recv.at[1],
    )
    own = pl.ds(pl.multiple_of(ix * ny, ny), ny)
    mid[own, :] = first[own, :]
    for copy in copies:
        copy.wait_recv()
    for j in range(ny):
        second[j * nx : (j + 1) * nx, :] = mid[pl.ds(j, nx, stride=ny), :]
    later = []
    for k in range(1, ny):
        to = lax.rem(iy + k, ny)
        copy = pltpu.make_async_remote_copy(
            src_ref=second.at[pl.ds(pl.multiple_of(to * nx, nx), nx), :],
            dst_ref=last.at[pl.ds(pl.multiple_of(iy * nx, nx), nx), :],
            send_sem=send_y.at[k - 1],
            recv_sem=recv_y.at[k - 1],
            device_id=(ix, to),
            device_id_type=MESH,
        )
        copy.start()
        later.append(copy)
    own = pl.ds(pl.multiple_of(iy * nx, nx), nx)
    last[own, :] = second[own, :]
    for copy in copies:
        copy.wait_send()

    for copy in halos:
        copy.wait()
    for p in (0, 1, size_x + 2, size_x + 3):
        keep = place.plane(p, size_x)
        for c in range(3):
            for array in (e, h):
                array[c, p, :size_y] = array[c, p, :size_y] * keep

    def unstage(p):
        keep = place.plane(p, size_x)
        above, below = keep * place.keep_hi_y, keep * place.keep_lo_y
        gap = jnp.zeros((1, depth), jnp.float32)
        for array, field in enumerate((e, h)):
            for c in range(3):
                field[c, p, size_y:] = halo_rows(
                    array, c, p, ROUTE_DOWN, ROUTE_UP, up_got, lo_got, above, below, gap
                )

    sweep(0, size_x + 4, unstage, 4)
    row = lax.broadcasted_iota(jnp.int32, (rows, depth), 0)
    inside = jnp.where(
        row < size_y,
        1.0,
        jnp.where(row == size_y, place.keep_hi_y, jnp.where(row == rows - 1, place.keep_lo_y, 0.0)),
    )
    ones = jnp.ones((1, depth), jnp.float32)

    def coefficients(p):
        for array, field in ((2, decay), (3, gain)):
            field[p, size_y:] = halo_rows(array, 0, p, ROUTE_DOWN, ROUTE_UP, up_got, lo_got, 1.0, 1.0, ones)
        half_loss = decay[p] * (0.5 * time_step)
        eps = gain[p]
        inverse = 1.0 / (eps + half_loss)
        keep = inside * place.plane(p, size_x)
        decay[p] = (eps - half_loss) * inverse * keep
        gain[p] = time_step * inverse * keep

    sweep(1, size_x + 2, coefficients, 2)
    moves = shifts(rows, depth)
    factor = h_factor(place, size_y, rows, depth)

    def h_step(p):
        h_plane(e, h, h, p, factor * place.plane(p, size_x), moves)

    sweep(0, size_x + 3, h_step, 7)

    def e_step(x):
        p = x + 2
        for c, curl in enumerate(curl_h(h, p, moves)):
            new = decay[p] * e[c, p] + gain[p] * curl
            base[c, x] = new[:size_y]

    sweep(0, size_x, e_step, 8)

    for copy in later:
        copy.wait()
    got_ref[...] = last[...]
    quarter = nx * ny // FIELDS
    lane = lax.broadcasted_iota(jnp.int32, (quarter, LANES), 1) // SPAN
    codes = jnp.zeros((quarter, LANES), jnp.int32)
    for k in range(FIELDS):
        code = last[pl.ds(k, quarter, stride=FIELDS), :].astype(jnp.int32)
        word = jnp.bitwise_and(code, LANES - 1) + jnp.bitwise_and(code, -LANES) * FIELDS
        codes = jnp.where(lane == k, pltpu.roll(word, (k + 1) * SPAN % LANES, 1), codes)
    code_ref[...] = codes


def in_vmem(count):
    return [pl.BlockSpec(memory_space=pltpu.VMEM)] * count


def f32(*shape):
    return jax.ShapeDtypeStruct(shape, jnp.float32)


def route(nx, ny, data, tile, cell, comp, e, h, cond, perm):
    devices = nx * ny
    size_x, size_y, depth = cond.shape
    wide, tall = size_x + 4, size_y + 8
    inputs = (data, tile, cell, comp, e, h, cond, perm)
    rows = lambda: pltpu.VMEM((devices, LANES), jnp.float32)
    return pl.pallas_call(
        functools.partial(route_kernel, nx, ny, size_x * size_y * depth),
        out_shape=[
            f32(devices, LANES),
            jax.ShapeDtypeStruct((devices // FIELDS, LANES), jnp.int32),
            f32(3, wide, tall, depth),
            f32(3, size_x, size_y, depth),
            f32(wide, tall, depth),
            f32(wide, tall, depth),
        ],
        in_specs=[pl.BlockSpec(memory_space=pltpu.HBM)] * 8,
        out_specs=in_vmem(6),
        scratch_shapes=[
            *(pltpu.VMEM(a.shape, a.dtype) for a in (data, tile, cell, comp)),
            pltpu.VMEM((3, wide, tall, depth), jnp.float32),
            rows(),
            rows(),
            rows(),
            rows(),
            *halo_scratch(ROUTE_DOWN, ROUTE_UP, size_x, depth),
            pltpu.SemaphoreType.DMA((8,)),
            pltpu.SemaphoreType.DMA((ny - 1,)),
            pltpu.SemaphoreType.DMA((ny - 1,)),
            pltpu.SemaphoreType.DMA((nx - 1,)),
            pltpu.SemaphoreType.DMA((nx - 1,)),
            pltpu.SemaphoreType.DMA((2, 8)),
            pltpu.SemaphoreType.DMA((2, 8)),
        ],
        compiler_params=pltpu.CompilerParams(
            collective_id=0, has_side_effects=True, vmem_limit_bytes=16 * MIB
        ),
        name="route",
    )(*(pltpu.with_memory_space_constraint(a, pltpu.HBM) for a in inputs))


def scatter_kernel(cap, code_in, got_ref, out_ref, code_ref, quad, terms, wide, sem):
    fetch = pltpu.make_async_copy(code_in, code_ref, sem)
    fetch.start()
    devices = got_ref.shape[0]
    got = got_ref[...]
    lane = lax.broadcasted_iota(jnp.int32, (devices, LANES), 1)
    slot = jnp.bitwise_and(lane, SPAN - 1)
    codes = jnp.where(lane >= (FIELDS - 1) * SPAN, got, 0.0)
    codes = codes + pltpu.roll(codes, SPAN, 1)
    codes = codes + pltpu.roll(codes, 2 * SPAN, 1)
    total = got
    place_in_group = slot - slot // GROUP * GROUP
    for d in range(1, GROUP):
        same = (codes == pltpu.roll(codes, d, 1)) & (place_in_group >= d)
        total = total + jnp.where(same, pltpu.roll(got, d, 1), 0.0)
    for t in range(FIELDS):
        quad[pl.ds(t, devices, stride=FIELDS), :] = jnp.where(
            (lane >= t * SPAN) & (lane < (t + 1) * SPAN), total, 0.0
        )
    values = quad[...]
    high = values.astype(jnp.bfloat16)
    low = (values - high.astype(jnp.float32)).astype(jnp.bfloat16)
    terms[:, :LANES] = high
    terms[:, LANES:] = low
    row_slot = jnp.bitwise_and(lax.broadcasted_iota(jnp.int32, (2 * LANES, 2 * LANES), 0), SPAN - 1)
    column = lax.broadcasted_iota(jnp.int32, (2 * LANES, 2 * LANES), 1) // LANES
    for i in range(0, cap, 2):
        both = mm(terms[...], (row_slot == column + i).astype(jnp.bfloat16))
        wide[i] = both[:, :LANES]
        wide[i + 1] = both[:, LANES:]
    step = 512

    def clear(n, _):
        out_ref[pl.ds(pl.multiple_of(n * step, step), step), :] = jnp.zeros((step, LANES), jnp.float32)
        return 0

    lax.fori_loop(0, out_ref.shape[0] // step, clear, 0)
    fetch.wait()
    depth = lax.broadcasted_iota(jnp.int32, (FIELDS, LANES), 1)

    def place(q, _):
        for p in range(FIELDS):
            s = q * FIELDS + p
            for start in range(0, cap, GROUP):
                where, news = [], []
                for i in range(start, min(cap, start + GROUP)):
                    word = code_ref[q, p * SPAN + i]
                    row = pl.ds(pl.multiple_of(lax.shift_right_logical(word, 7), FIELDS), FIELDS)
                    news.append(out_ref[row, :] + wide[i, pl.ds(pl.multiple_of(s * FIELDS, FIELDS), FIELDS), :])
                    column = jnp.bitwise_and(jnp.full((FIELDS, LANES), word, jnp.int32), LANES - 1)
                    where.append((row, depth == column))
                for (row, mask), new in zip(where, news):
                    pltpu.store(out_ref.at[row, :], new, mask=mask)
        return 0

    lax.fori_loop(0, devices // FIELDS, place, 0)


def scatter(cap, rows, codes, got):
    devices = got.shape[0]
    return pl.pallas_call(
        functools.partial(scatter_kernel, cap),
        out_shape=jax.ShapeDtypeStruct((rows * FIELDS, LANES), jnp.float32),
        in_specs=[pl.BlockSpec(memory_space=pltpu.VMEM)] * 2,
        out_specs=pl.BlockSpec(memory_space=pltpu.VMEM),
        scratch_shapes=[
            pltpu.SMEM(codes.shape, jnp.int32),
            pltpu.VMEM((devices * FIELDS, LANES), jnp.float32),
            pltpu.VMEM((devices * FIELDS, 2 * LANES), jnp.bfloat16),
            pltpu.VMEM((cap, devices * FIELDS, LANES), jnp.float32),
            pltpu.SemaphoreType.DMA,
        ],
        compiler_params=pltpu.CompilerParams(vmem_limit_bytes=24 * MIB),
        name="scatter",
    )(codes, got)


def share_kernel(
    nx, ny, base, gain, src, fwd, e, src1, grad, dn_put, up_put, up_got, lo_got, send, recv
):
    place = Place(nx, ny)
    size_x, size_y, depth = base.shape[1:]
    barrier = pltpu.get_barrier_semaphore()
    others = place.sides() + place.corners()
    for other in others:
        pl.semaphore_signal(barrier, inc=1, device_id=other, device_id_type=MESH)

    def own(x):
        p = x + 2
        rise = gain[p, :size_y]
        for c in range(3):
            new = base[c, x] - rise * src[c, x, pl.ds(0, size_y, stride=FIELDS), :]
            e[c, p, :size_y] = new
            source = src[c, x, pl.ds(1, size_y, stride=FIELDS), :]
            src1[c, p, :size_y] = source
            for n, (array, comp, r) in enumerate(SHARE_DOWN):
                if comp == c:
                    dn_put[n, x] = (new, source)[array][r : r + 1]
            for n, (array, comp, r) in enumerate(SHARE_UP):
                if comp == c:
                    up_put[n, x] = (new, source)[array][size_y - 2 + r : size_y - 1 + r]

    sweep(0, size_x, own, 4)
    pl.semaphore_wait(barrier, len(others))
    copies = start_copies(
        row_copies(dn_put, up_put, up_got, lo_got, size_x, place)
        + plane_copies(e, 2, size_x, size_y, place)
        + plane_copies(src1, 1, size_x, size_y, place),
        send,
        recv,
    )

    def product(x):
        total = fwd[0, 0, x].astype(jnp.float32) * e[0, x + 2, :size_y]
        for c in (1, 2):
            total = total + fwd[0, c, x].astype(jnp.float32) * e[c, x + 2, :size_y]
        grad[x] = total

    sweep(0, size_x, product, 4)
    for copy in copies:
        copy.wait()
    for p in (0, 1, size_x + 2, size_x + 3):
        keep = place.plane(p, size_x)
        for c in range(3):
            e[c, p, :size_y] = e[c, p, :size_y] * keep

    def unstage(p):
        keep = place.plane(p, size_x)
        above, below = keep * place.keep_hi_y, keep * place.keep_lo_y
        gap = jnp.zeros((1, depth), jnp.float32)
        for array, field in enumerate((e, src1)):
            for c in range(3):
                field[c, p, size_y:] = halo_rows(
                    array, c, p, SHARE_DOWN, SHARE_UP, up_got, lo_got, above, below, gap
                )

    sweep(0, size_x + 4, unstage, 4)


def share(nx, ny, base, gain, src, fwd):
    size_x, size_y, depth = base.shape[1:]
    wide, tall = size_x + 4, size_y + 8
    return pl.pallas_call(
        functools.partial(share_kernel, nx, ny),
        out_shape=[f32(3, wide, tall, depth), f32(3, wide, tall, depth), f32(size_x, size_y, depth)],
        in_specs=in_vmem(4),
        out_specs=in_vmem(3),
        scratch_shapes=[
            *halo_scratch(SHARE_DOWN, SHARE_UP, size_x, depth),
            pltpu.SemaphoreType.DMA((10,)),
            pltpu.SemaphoreType.DMA((10,)),
        ],
        compiler_params=pltpu.CompilerParams(
            collective_id=1, has_side_effects=True, vmem_limit_bytes=6 * MIB
        ),
        name="share",
    )(base, gain, src, fwd)


def finish_kernel(
    nx, ny, e1, h1, decay, gain, src1, src, fwd, grad1, e_out, h_out, grad_out, e, h, grad, sem
):
    place = Place(nx, ny)
    size_x, size_y, depth = grad1.shape
    rows = size_y + 8
    moves = shifts(rows, depth)
    factor = h_factor(place, size_y, rows, depth)

    def h_second(p):
        h_plane(e1, h1, h, p, factor * place.plane(p, size_x), moves)

    sweep(0, size_x + 3, h_second, 7)

    def e_second(p, inner):
        fade, rise = decay[p], gain[p]
        total = None
        for c, curl in enumerate(curl_h(h, p, moves)):
            new = fade * e1[c, p] + rise * (curl - src1[c, p])
            e[c, p] = new
            if inner:
                term = fwd[1, c, p - 2].astype(jnp.float32) * new[:size_y]
                total = term if total is None else total + term
        if inner:
            grad[p - 2] = grad1[p - 2] + total

    e_second(1, False)

    def e_inner(p):
        e_second(p, True)

    sweep(2, size_x, e_inner, 8)
    e_second(size_x + 2, False)

    def h_third(p):
        h_plane(e, h, h, p, factor * place.plane(p, size_x), moves)

    sweep(1, size_x + 1, h_third, 11)
    inside = pl.ds(0, size_y)
    h_copy = pltpu.make_async_copy(h.at[:, pl.ds(2, size_x), inside], h_out, sem.at[0])
    h_copy.start()

    def e_third(x):
        p = x + 2
        fade, rise = decay[p, :size_y], gain[p, :size_y]
        total = grad[x]
        for c, curl in enumerate(curl_h(h, p, moves)):
            source = src[c, x, pl.ds(2, size_y, stride=FIELDS), :]
            new = fade * e[c, p, :size_y] + rise * (curl[:size_y] - source)
            e[c, p, :size_y] = new
            total = total + fwd[2, c, x].astype(jnp.float32) * new
        grad[x] = total

    each = size_x // PARTS

    def results(k):
        here = pl.ds(k * each, each)
        return (
            pltpu.make_async_copy(e.at[:, pl.ds(2 + k * each, each), inside], e_out.at[:, here], sem.at[1 + 2 * k]),
            pltpu.make_async_copy(grad.at[here], grad_out.at[here], sem.at[2 + 2 * k]),
        )

    def part(k, _):
        for x in range(each):
            e_third(k * each + x)
        for copy in results(k):
            copy.start()
        return 0

    lax.fori_loop(0, PARTS, part, 0)
    h_copy.wait()
    for k in range(PARTS):
        for copy in results(k):
            copy.wait()


def finish(nx, ny, e1, h1, decay, gain, src1, src, fwd, grad1):
    size_x, size_y, depth = grad1.shape
    field = f32(3, size_x, size_y, depth)
    return pl.pallas_call(
        functools.partial(finish_kernel, nx, ny),
        out_shape=[field, field, f32(size_x, size_y, depth)],
        in_specs=in_vmem(8),
        out_specs=[pl.BlockSpec(memory_space=pltpu.HBM)] * 3,
        scratch_shapes=[
            pltpu.VMEM(e1.shape, jnp.float32),
            pltpu.VMEM(h1.shape, jnp.float32),
            pltpu.VMEM(grad1.shape, jnp.float32),
            pltpu.SemaphoreType.DMA((1 + 2 * PARTS,)),
        ],
        compiler_params=pltpu.CompilerParams(vmem_limit_bytes=10 * MIB),
        name="finish",
    )(e1, h1, decay, gain, src1, src, fwd, grad1)


def per_device(
    e_adjoint,
    h_adjoint,
    conductivity,
    permittivity,
    forward_e,
    receiver_data,
    receiver_tile,
    receiver_cell,
    receiver_comp,
):
    _, size_x, size_y, depth = e_adjoint.shape
    nx, ny = lax.axis_size("gx"), lax.axis_size("gy")
    receivers = receiver_data.shape[0]
    cap = 3 * receivers // (nx * ny)
    by_lane = lambda a: a.reshape(receivers // LANES, LANES)
    got, codes, h1, base, decay, gain = route(
        nx,
        ny,
        receiver_data,
        by_lane(receiver_tile),
        by_lane(receiver_cell),
        by_lane(receiver_comp),
        e_adjoint,
        h_adjoint,
        conductivity,
        permittivity,
    )
    placed = scatter(cap, 3 * size_x * size_y, codes, got)
    placed = placed.reshape(3, size_x, size_y * FIELDS, depth)
    e1, src1, grad1 = share(nx, ny, base, gain, placed, forward_e)
    return tuple(finish(nx, ny, e1, h1, decay, gain, src1, placed, forward_e, grad1))


def solution(mesh):
    placed = (
        P(None, "gx", "gy", None),
        P(None, "gx", "gy", None),
        P("gx", "gy", None),
        P("gx", "gy", None),
        P(None, None, "gx", "gy", None),
        P(("gx", "gy"), None),
        P(("gx", "gy"), None),
        P(("gx", "gy")),
        P(("gx", "gy")),
    )
    return jax.shard_map(
        per_device,
        mesh=mesh,
        in_specs=placed,
        out_specs=(P(None, "gx", "gy", None), P(None, "gx", "gy", None), P("gx", "gy", None)),
        check_vma=False,
    )
```

```python
import functools

import jax
import jax.numpy as jnp
from jax import lax
from jax.experimental import pallas as pl
from jax.experimental.pallas import tpu as pltpu
from jax.sharding import PartitionSpec as P

STEPS = 3
SAMPLES = 128
LANES = 128
FIELDS = 4
SPAN = LANES // FIELDS
MESH = pl.DeviceIdType.MESH
GROUP = 8
PARTS = 4
MIB = 1 << 20

time_step = 0.55


def split3(x):
    a = x.astype(jnp.bfloat16)
    rest = x - a.astype(jnp.float32)
    b = rest.astype(jnp.bfloat16)
    c = (rest - b.astype(jnp.float32)).astype(jnp.bfloat16)
    return a, b, c


def mm(a, b, contract=((1,), (0,))):
    return lax.dot_general(a, b, (contract, ((), ())), preferred_element_type=jnp.float32)


def time_kernel():
    shape = (SAMPLES, LANES)
    sample = lax.broadcasted_iota(jnp.int32, shape, 0).astype(jnp.float32)
    field = lax.broadcasted_iota(jnp.int32, shape, 1) // SPAN
    centre = (field.astype(jnp.float32) + 0.5) * (SAMPLES / STEPS)
    spread = SAMPLES / (4.0 * STEPS)
    kernel = jnp.exp(-jnp.square((sample - centre) / spread))
    norm = jnp.sum(kernel * kernel, axis=0, keepdims=True)
    return jnp.where(field < STEPS, kernel / jnp.sqrt(norm), 0.0)


def pack(devices, cells, data_ref, tile_ref, cell_ref, comp_ref):
    blocks, width = tile_ref.shape
    kernel = time_kernel()
    at, to = (lax.broadcasted_iota(jnp.int32, (width, width), n) for n in (0, 1))
    before = (at < to).astype(jnp.bfloat16)
    every = jnp.ones((width, width), jnp.bfloat16)
    diagonal = at == to
    destination = lax.broadcasted_iota(jnp.int32, (devices, width), 0)
    lane = lax.broadcasted_iota(jnp.int32, (width, LANES), 1)
    slot = jnp.bitwise_and(lane, SPAN - 1).astype(jnp.float32)
    is_code = lane >= STEPS * SPAN
    down = jnp.ones((width, LANES), jnp.bfloat16)
    seen = jnp.zeros((devices, width), jnp.float32)
    packed = jnp.zeros((devices, LANES), jnp.float32)

    def column(row):
        return jnp.where(diagonal, row.astype(jnp.float32), 0.0).astype(jnp.bfloat16)

    for b in range(blocks):
        onehot = (destination == tile_ref[b : b + 1, :]).astype(jnp.float32)
        hot = onehot.astype(jnp.bfloat16)
        rank = jnp.sum(onehot * (seen + mm(hot, before)), axis=0, keepdims=True)
        seen = seen + mm(hot, every)
        amplitude = lax.dot_general(
            data_ref[b * width : (b + 1) * width, :],
            kernel,
            (((1,), (0,)), ((), ())),
            precision=lax.Precision.HIGHEST,
            preferred_element_type=jnp.float32,
        )
        code = comp_ref[b : b + 1, :] * cells + cell_ref[b : b + 1, :]
        low = jnp.bitwise_and(code, 255)
        middle = jnp.bitwise_and(code, 255 << 8)
        high = code - low - middle
        codes = mm(column(low), down) + mm(column(middle), down) + mm(column(high), down)
        spread = jnp.where(
            slot == mm(column(rank), down), jnp.where(is_code, codes, amplitude), 0.0
        )
        for term in split3(spread):
            packed = packed + mm(hot, term)
    return packed


def sweep(start, count, body, width):
    def several(n, _):
        for k in range(width):
            body(start + n * width + k)
        return 0

    turns = count // width
    lax.fori_loop(0, turns, several, 0)
    for p in range(turns * width, count):
        body(start + p)


class Place:
    def __init__(self, nx, ny):
        self.nx, self.ny = nx, ny
        self.ix, self.iy = lax.axis_index("gx"), lax.axis_index("gy")
        self.inside_x = {-1: self.ix > 0, 0: None, 1: self.ix < nx - 1}
        self.inside_y = {-1: self.iy > 0, 0: None, 1: self.iy < ny - 1}

    def other(self, dx, dy):
        return lax.rem(self.ix + dx + self.nx, self.nx), lax.rem(self.iy + dy + self.ny, self.ny)

    def has(self, dx, dy):
        x, y = self.inside_x[dx], self.inside_y[dy]
        if x is None or y is None:
            return y if x is None else x
        return jnp.logical_and(x, y)

    def plane(self, p, size_x):
        low, high = jnp.logical_or(p >= 2, self.ix > 0), jnp.logical_or(p < size_x + 2, self.ix < self.nx - 1)
        return jnp.logical_and(low, high)


AROUND = tuple((dx, dy) for dx in (-1, 0, 1) for dy in (-1, 0, 1) if (dx, dy) != (0, 0))


def greet(place, barrier, offsets):
    count = jnp.int32(0)
    for dx, dy in offsets:
        here = place.has(dx, dy)
        count = count + here.astype(jnp.int32)

        @pl.when(here)
        def _(dx=dx, dy=dy):
            pl.semaphore_signal(barrier, inc=1, device_id=place.other(dx, dy), device_id_type=MESH)

    return count


def shifts(rows, depth):
    lane = lax.broadcasted_iota(jnp.int32, (rows, depth), 1)

    def up_z(f):
        return jnp.where(lane == depth - 1, 0.0, pltpu.roll(f, depth - 1, 1))

    def down_z(f):
        return jnp.where(lane == 0, 0.0, pltpu.roll(f, 1, 1))

    def up_y(f):
        return pltpu.roll(f, rows - 1, 0)

    def down_y(f):
        return pltpu.roll(f, 1, 0)

    return up_z, down_z, up_y, down_y


def h_plane(e, h_from, h_to, p, factor, moves):
    up_z, _, up_y, _ = moves
    ex, ey, ez = e[0, p], e[1, p], e[2, p]
    curl_x = (up_y(ez) - ez) - (up_z(ey) - ey)
    curl_y = (up_z(ex) - ex) - (e[2, p + 1] - ez)
    curl_z = (e[1, p + 1] - ey) - (up_y(ex) - ex)
    for c, curl in enumerate((curl_x, curl_y, curl_z)):
        h_to[c, p] = h_from[c, p] - factor * curl


def curl_h(h, p, moves):
    _, down_z, _, down_y = moves
    hx, hy, hz = h[0, p], h[1, p], h[2, p]
    curl_x = (hz - down_y(hz)) - (hy - down_z(hy))
    curl_y = (hx - down_z(hx)) - (hz - h[2, p - 1])
    curl_z = (hy - h[1, p - 1]) - (hx - down_y(hx))
    return curl_x, curl_y, curl_z


def h_factor(place, size_y, rows, depth):
    row = lax.broadcasted_iota(jnp.int32, (rows, depth), 0)
    above, below = jnp.where(place.has(0, 1), 1.0, 0.0), jnp.where(place.has(0, -1), 1.0, 0.0)
    return time_step * jnp.where(row < size_y, 1.0, jnp.where(row < size_y + 4, above, below))


def row_copies(dn_put, up_put, up_got, lo_got, size_x):
    first, last, low, high = pl.ds(0, 2), pl.ds(size_x - 2, 2), pl.ds(0, 2), pl.ds(size_x + 2, 2)
    whole = pl.ds(2, size_x)
    return [
        (dn_put, up_got.at[:, whole], 0, -1),
        (up_put, lo_got.at[:, whole], 0, 1),
        (dn_put.at[:, first], up_got.at[:, high], -1, -1),
        (dn_put.at[:, last], up_got.at[:, low], 1, -1),
        (up_put.at[:, first], lo_got.at[:, high], -1, 1),
        (up_put.at[:, last], lo_got.at[:, low], 1, 1),
    ]


def plane_copies(array, count, size_x, size_y):
    lead = (slice(None),) * (len(array.shape) - 3)
    rows = pl.ds(0, size_y)

    def part(start):
        return array.at[(*lead, pl.ds(start, count), rows)]

    return [
        (part(2), part(size_x + 2), -1, 0),
        (part(size_x + 2 - count), part(2 - count), 1, 0),
    ]


FIELD_DOWN = ((0, 0, 0), (0, 1, 0), (0, 2, 0), (0, 0, 1), (0, 2, 1))
FIELD_UP = tuple((0, c, r) for c in range(3) for r in range(2))
ROUTE_DOWN = (*FIELD_DOWN, (1, 0, 0), (1, 1, 0), (1, 2, 0), (2, 0, 0), (3, 0, 0))
ROUTE_UP = (*FIELD_UP, (1, 0, 0), (1, 2, 0), (1, 0, 1), (1, 1, 1), (1, 2, 1), (2, 0, 1), (3, 0, 1))
SHARE_DOWN = (*FIELD_DOWN, (1, 0, 0), (1, 2, 0))
SHARE_UP = (*FIELD_UP, (1, 0, 1), (1, 1, 1), (1, 2, 1))


def halo_scratch(down, up, size_x, depth):
    shapes = [(len(down), size_x), (len(up), size_x), (len(down), size_x + 4), (len(up), size_x + 4)]
    return [pltpu.VMEM((*shape, 1, depth), jnp.float32) for shape in shapes]


def halo_rows(array, c, p, down, up, up_got, lo_got, above, below, fill):
    def one(names, got, r, keep):
        if (array, c, r) not in names:
            return fill
        return jnp.where(keep, got[names.index((array, c, r)), p], fill)

    return jnp.concatenate(
        [one(down, up_got, 0, above), one(down, up_got, 1, above)]
        + [fill] * 4
        + [one(up, lo_got, 0, below), one(up, lo_got, 1, below)],
        axis=0,
    )


class Exchange:
    def __init__(self, place, parts, send, recv):
        self.parts = []
        for n, (a, b, dx, dy) in enumerate(parts):
            copy = pltpu.make_async_remote_copy(
                src_ref=a,
                dst_ref=b,
                send_sem=send.at[n],
                recv_sem=recv.at[n],
                device_id=place.other(dx, dy),
                device_id_type=MESH,
            )
            self.parts.append((copy, place.has(dx, dy), place.has(-dx, -dy)))
            pl.when(self.parts[-1][1])(copy.start)

    def wait(self):
        for copy, goes, comes in self.parts:
            pl.when(comes)(copy.wait_recv)
            pl.when(goes)(copy.wait_send)


def route_kernel(
    nx,
    ny,
    cells,
    data_in,
    tile_in,
    cell_in,
    comp_in,
    e_in,
    h_in,
    cond_in,
    perm_in,
    got_ref,
    code_ref,
    h,
    base,
    decay,
    gain,
    data_ref,
    tile_ref,
    cell_ref,
    comp_ref,
    e,
    first,
    mid,
    second,
    last,
    dn_put,
    up_put,
    up_got,
    lo_got,
    load,
    send_y,
    recv_y,
    send_x,
    recv_x,
    send,
    recv,
):
    place = Place(nx, ny)
    ix, iy = place.ix, place.iy
    size_x, size_y, depth = base.shape[1:]
    rows = size_y + 8
    inner = (pl.ds(2, size_x), pl.ds(0, size_y))
    pairs = (
        (tile_in, tile_ref),
        (cell_in, cell_ref),
        (comp_in, comp_ref),
        (data_in, data_ref),
        (e_in, e.at[:, inner[0], inner[1]]),
        (h_in, h.at[:, inner[0], inner[1]]),
        (cond_in, decay.at[inner[0], inner[1]]),
        (perm_in, gain.at[inner[0], inner[1]]),
    )
    loads = [pltpu.make_async_copy(a, b, load.at[n]) for n, (a, b) in enumerate(pairs)]
    for copy in loads:
        copy.start()
    barrier = pltpu.get_barrier_semaphore()
    for k in range(1, nx):
        pl.semaphore_signal(barrier, inc=1, device_id=(lax.rem(ix + k, nx), iy), device_id_type=MESH)
    for k in range(1, ny):
        pl.semaphore_signal(barrier, inc=1, device_id=(ix, lax.rem(iy + k, ny)), device_id_type=MESH)
    corners = greet(place, barrier, [o for o in AROUND if 0 not in o])
    for copy in loads[:4]:
        copy.wait()
    first[...] = pack(nx * ny, cells, data_ref, tile_ref, cell_ref, comp_ref)
    for copy in loads[4:]:
        copy.wait()

    def stage(x):
        p = x + 2
        arrays = ((e.at[0], e.at[1], e.at[2]), (h.at[0], h.at[1], h.at[2]), (decay,), (gain,))
        for n, (array, c, r) in enumerate(ROUTE_DOWN):
            dn_put[n, x] = arrays[array][c][p, r : r + 1, :]
        for n, (array, c, r) in enumerate(ROUTE_UP):
            up_put[n, x] = arrays[array][c][p, size_y - 2 + r : size_y - 1 + r, :]

    sweep(0, size_x, stage, 4)
    pl.semaphore_wait(barrier, corners + (nx + ny - 2))
    by_row = Exchange(
        place, row_copies(dn_put, up_put, up_got, lo_got, size_x), send.at[0], recv.at[0]
    )
    copies = []
    for k in range(1, nx):
        to = lax.rem(ix + k, nx)
        copy = pltpu.make_async_remote_copy(
            src_ref=first.at[pl.ds(pl.multiple_of(to * ny, ny), ny), :],
            dst_ref=mid.at[pl.ds(pl.multiple_of(ix * ny, ny), ny), :],
            send_sem=send_x.at[k - 1],
            recv_sem=recv_x.at[k - 1],
            device_id=(to, iy),
            device_id_type=MESH,
        )
        copy.start()
        copies.append(copy)
    by_plane = Exchange(
        place,
        plane_copies(e, 2, size_x, size_y)
        + plane_copies(h, 2, size_x, size_y)
        + plane_copies(decay, 1, size_x, size_y)
        + plane_copies(gain, 1, size_x, size_y),
        send.at[1],
        recv.at[1],
    )
    own = pl.ds(pl.multiple_of(ix * ny, ny), ny)
    mid[own, :] = first[own, :]
    for copy in copies:
        copy.wait_recv()
    for j in range(ny):
        second[j * nx : (j + 1) * nx, :] = mid[pl.ds(j, nx, stride=ny), :]
    later = []
    for k in range(1, ny):
        to = lax.rem(iy + k, ny)
        copy = pltpu.make_async_remote_copy(
            src_ref=second.at[pl.ds(pl.multiple_of(to * nx, nx), nx), :],
            dst_ref=last.at[pl.ds(pl.multiple_of(iy * nx, nx), nx), :],
            send_sem=send_y.at[k - 1],
            recv_sem=recv_y.at[k - 1],
            device_id=(ix, to),
            device_id_type=MESH,
        )
        copy.start()
        later.append(copy)
    own = pl.ds(pl.multiple_of(iy * nx, nx), nx)
    last[own, :] = second[own, :]
    for copy in copies:
        copy.wait_send()

    by_plane.wait()
    by_row.wait()
    for p in (0, 1, size_x + 2, size_x + 3):
        keep = place.plane(p, size_x)
        for c in range(3):
            for array in (e, h):
                array[c, p, :size_y] = jnp.where(keep, array[c, p, :size_y], 0.0)

    def unstage(p):
        keep = place.plane(p, size_x)
        above, below = jnp.logical_and(keep, place.has(0, 1)), jnp.logical_and(keep, place.has(0, -1))
        gap = jnp.zeros((1, depth), jnp.float32)
        for array, field in enumerate((e, h)):
            for c in range(3):
                field[c, p, size_y:] = halo_rows(
                    array, c, p, ROUTE_DOWN, ROUTE_UP, up_got, lo_got, above, below, gap
                )

    sweep(0, size_x + 4, unstage, 4)
    row = lax.broadcasted_iota(jnp.int32, (rows, depth), 0)
    inside = jnp.where(
        row < size_y,
        1.0,
        jnp.where(
            row == size_y,
            jnp.where(place.has(0, 1), 1.0, 0.0),
            jnp.where(row == rows - 1, jnp.where(place.has(0, -1), 1.0, 0.0), 0.0),
        ),
    )
    ones = jnp.ones((1, depth), jnp.float32)

    def coefficients(p):
        for array, field in ((2, decay), (3, gain)):
            field[p, size_y:] = halo_rows(array, 0, p, ROUTE_DOWN, ROUTE_UP, up_got, lo_got, True, True, ones)
        half_loss = decay[p] * (0.5 * time_step)
        eps = gain[p]
        inverse = 1.0 / (eps + half_loss)
        keep = inside > jnp.where(place.plane(p, size_x), 0.5, 1.5)
        decay[p] = jnp.where(keep, (eps - half_loss) * inverse, 0.0)
        gain[p] = jnp.where(keep, time_step * inverse, 0.0)

    sweep(1, size_x + 2, coefficients, 2)
    moves = shifts(rows, depth)
    factor = h_factor(place, size_y, rows, depth)

    def h_step(p):
        h_plane(e, h, h, p, factor * jnp.where(place.plane(p, size_x), 1.0, 0.0), moves)

    sweep(0, size_x + 3, h_step, 7)

    def e_step(x):
        p = x + 2
        for c, curl in enumerate(curl_h(h, p, moves)):
            new = decay[p] * e[c, p] + gain[p] * curl
            base[c, x] = new[:size_y]

    sweep(0, size_x, e_step, 8)

    for copy in later:
        copy.wait()
    got_ref[...] = last[...]
    quarter = nx * ny // FIELDS
    lane = lax.broadcasted_iota(jnp.int32, (quarter, LANES), 1) // SPAN
    codes = jnp.zeros((quarter, LANES), jnp.int32)
    for k in range(FIELDS):
        code = last[pl.ds(k, quarter, stride=FIELDS), :].astype(jnp.int32)
        word = jnp.bitwise_and(code, LANES - 1) + jnp.bitwise_and(code, -LANES) * FIELDS
        codes = jnp.where(lane == k, pltpu.roll(word, (k + 1) * SPAN % LANES, 1), codes)
    code_ref[...] = codes


def in_vmem(count):
    return [pl.BlockSpec(memory_space=pltpu.VMEM)] * count


def f32(*shape):
    return jax.ShapeDtypeStruct(shape, jnp.float32)


def route(nx, ny, data, tile, cell, comp, e, h, cond, perm):
    devices = nx * ny
    size_x, size_y, depth = cond.shape
    wide, tall = size_x + 4, size_y + 8
    inputs = (data, tile, cell, comp, e, h, cond, perm)
    rows = lambda: pltpu.VMEM((devices, LANES), jnp.float32)
    return pl.pallas_call(
        functools.partial(route_kernel, nx, ny, size_x * size_y * depth),
        out_shape=[
            f32(devices, LANES),
            jax.ShapeDtypeStruct((devices // FIELDS, LANES), jnp.int32),
            f32(3, wide, tall, depth),
            f32(3, size_x, size_y, depth),
            f32(wide, tall, depth),
            f32(wide, tall, depth),
        ],
        in_specs=[pl.BlockSpec(memory_space=pltpu.HBM)] * 8,
        out_specs=in_vmem(6),
        scratch_shapes=[
            *(pltpu.VMEM(a.shape, a.dtype) for a in (data, tile, cell, comp)),
            pltpu.VMEM((3, wide, tall, depth), jnp.float32),
            rows(),
            rows(),
            rows(),
            rows(),
            *halo_scratch(ROUTE_DOWN, ROUTE_UP, size_x, depth),
            pltpu.SemaphoreType.DMA((8,)),
            pltpu.SemaphoreType.DMA((ny - 1,)),
            pltpu.SemaphoreType.DMA((ny - 1,)),
            pltpu.SemaphoreType.DMA((nx - 1,)),
            pltpu.SemaphoreType.DMA((nx - 1,)),
            pltpu.SemaphoreType.DMA((2, 8)),
            pltpu.SemaphoreType.DMA((2, 8)),
        ],
        compiler_params=pltpu.CompilerParams(
            collective_id=0, has_side_effects=True, vmem_limit_bytes=16 * MIB
        ),
        name="route",
    )(*(pltpu.with_memory_space_constraint(a, pltpu.HBM) for a in inputs))


def scatter_kernel(cap, code_in, got_ref, out_ref, code_ref, quad, terms, wide, sem):
    fetch = pltpu.make_async_copy(code_in, code_ref, sem)
    fetch.start()
    devices = got_ref.shape[0]
    got = got_ref[...]
    lane = lax.broadcasted_iota(jnp.int32, (devices, LANES), 1)
    slot = jnp.bitwise_and(lane, SPAN - 1)
    codes = jnp.where(lane >= (FIELDS - 1) * SPAN, got, 0.0)
    codes = codes + pltpu.roll(codes, SPAN, 1)
    codes = codes + pltpu.roll(codes, 2 * SPAN, 1)
    total = got
    place_in_group = slot - slot // GROUP * GROUP
    for d in range(1, GROUP):
        same = (codes == pltpu.roll(codes, d, 1)) & (place_in_group >= d)
        total = total + jnp.where(same, pltpu.roll(got, d, 1), 0.0)
    for t in range(FIELDS):
        quad[pl.ds(t, devices, stride=FIELDS), :] = jnp.where(
            (lane >= t * SPAN) & (lane < (t + 1) * SPAN), total, 0.0
        )
    values = quad[...]
    high = values.astype(jnp.bfloat16)
    low = (values - high.astype(jnp.float32)).astype(jnp.bfloat16)
    terms[:, :LANES] = high
    terms[:, LANES:] = low
    row_slot = jnp.bitwise_and(lax.broadcasted_iota(jnp.int32, (2 * LANES, 2 * LANES), 0), SPAN - 1)
    column = lax.broadcasted_iota(jnp.int32, (2 * LANES, 2 * LANES), 1) // LANES
    for i in range(0, cap, 2):
        both = mm(terms[...], (row_slot == column + i).astype(jnp.bfloat16))
        wide[i] = both[:, :LANES]
        wide[i + 1] = both[:, LANES:]
    step = 512

    def clear(n, _):
        out_ref[pl.ds(pl.multiple_of(n * step, step), step), :] = jnp.zeros((step, LANES), jnp.float32)
        return 0

    lax.fori_loop(0, out_ref.shape[0] // step, clear, 0)
    fetch.wait()
    depth = lax.broadcasted_iota(jnp.int32, (FIELDS, LANES), 1)

    def place(q, _):
        for p in range(FIELDS):
            s = q * FIELDS + p
            for start in range(0, cap, GROUP):
                where, news = [], []
                for i in range(start, min(cap, start + GROUP)):
                    word = code_ref[q, p * SPAN + i]
                    row = pl.ds(pl.multiple_of(lax.shift_right_logical(word, 7), FIELDS), FIELDS)
                    news.append(out_ref[row, :] + wide[i, pl.ds(pl.multiple_of(s * FIELDS, FIELDS), FIELDS), :])
                    column = jnp.bitwise_and(jnp.full((FIELDS, LANES), word, jnp.int32), LANES - 1)
                    where.append((row, depth == column))
                for (row, mask), new in zip(where, news):
                    pltpu.store(out_ref.at[row, :], new, mask=mask)
        return 0

    lax.fori_loop(0, devices // FIELDS, place, 0)


def scatter(cap, rows, codes, got):
    devices = got.shape[0]
    return pl.pallas_call(
        functools.partial(scatter_kernel, cap),
        out_shape=jax.ShapeDtypeStruct((rows * FIELDS, LANES), jnp.float32),
        in_specs=[pl.BlockSpec(memory_space=pltpu.VMEM)] * 2,
        out_specs=pl.BlockSpec(memory_space=pltpu.VMEM),
        scratch_shapes=[
            pltpu.SMEM(codes.shape, jnp.int32),
            pltpu.VMEM((devices * FIELDS, LANES), jnp.float32),
            pltpu.VMEM((devices * FIELDS, 2 * LANES), jnp.bfloat16),
            pltpu.VMEM((cap, devices * FIELDS, LANES), jnp.float32),
            pltpu.SemaphoreType.DMA,
        ],
        compiler_params=pltpu.CompilerParams(vmem_limit_bytes=24 * MIB),
        name="scatter",
    )(codes, got)


def share_kernel(
    nx, ny, base, gain, src, fwd, e, src1, grad, dn_put, up_put, up_got, lo_got, send, recv
):
    place = Place(nx, ny)
    size_x, size_y, depth = base.shape[1:]
    barrier = pltpu.get_barrier_semaphore()
    others = greet(place, barrier, AROUND)

    def own(x):
        p = x + 2
        rise = gain[p, :size_y]
        for c in range(3):
            new = base[c, x] - rise * src[c, x, pl.ds(0, size_y, stride=FIELDS), :]
            e[c, p, :size_y] = new
            source = src[c, x, pl.ds(1, size_y, stride=FIELDS), :]
            src1[c, p, :size_y] = source
            for n, (array, comp, r) in enumerate(SHARE_DOWN):
                if comp == c:
                    dn_put[n, x] = (new, source)[array][r : r + 1]
            for n, (array, comp, r) in enumerate(SHARE_UP):
                if comp == c:
                    up_put[n, x] = (new, source)[array][size_y - 2 + r : size_y - 1 + r]

    sweep(0, size_x, own, 4)
    pl.semaphore_wait(barrier, others)
    halos = Exchange(
        place,
        row_copies(dn_put, up_put, up_got, lo_got, size_x)
        + plane_copies(e, 2, size_x, size_y)
        + plane_copies(src1, 1, size_x, size_y),
        send,
        recv,
    )

    def product(x):
        total = fwd[0, 0, x].astype(jnp.float32) * e[0, x + 2, :size_y]
        for c in (1, 2):
            total = total + fwd[0, c, x].astype(jnp.float32) * e[c, x + 2, :size_y]
        grad[x] = total

    sweep(0, size_x, product, 4)
    halos.wait()
    for p in (0, 1, size_x + 2, size_x + 3):
        keep = place.plane(p, size_x)
        for c in range(3):
            e[c, p, :size_y] = jnp.where(keep, e[c, p, :size_y], 0.0)
            src1[c, p, :size_y] = jnp.where(keep, src1[c, p, :size_y], 0.0)

    def unstage(p):
        keep = place.plane(p, size_x)
        above, below = jnp.logical_and(keep, place.has(0, 1)), jnp.logical_and(keep, place.has(0, -1))
        gap = jnp.zeros((1, depth), jnp.float32)
        for array, field in enumerate((e, src1)):
            for c in range(3):
                field[c, p, size_y:] = halo_rows(
                    array, c, p, SHARE_DOWN, SHARE_UP, up_got, lo_got, above, below, gap
                )

    sweep(0, size_x + 4, unstage, 4)


def share(nx, ny, base, gain, src, fwd):
    size_x, size_y, depth = base.shape[1:]
    wide, tall = size_x + 4, size_y + 8
    return pl.pallas_call(
        functools.partial(share_kernel, nx, ny),
        out_shape=[f32(3, wide, tall, depth), f32(3, wide, tall, depth), f32(size_x, size_y, depth)],
        in_specs=in_vmem(4),
        out_specs=in_vmem(3),
        scratch_shapes=[
            *halo_scratch(SHARE_DOWN, SHARE_UP, size_x, depth),
            pltpu.SemaphoreType.DMA((10,)),
            pltpu.SemaphoreType.DMA((10,)),
        ],
        compiler_params=pltpu.CompilerParams(
            collective_id=1, has_side_effects=True, vmem_limit_bytes=6 * MIB
        ),
        name="share",
    )(base, gain, src, fwd)


def finish_kernel(
    nx, ny, e1, h1, decay, gain, src1, src, fwd, grad1, e_out, h_out, grad_out, e, h, grad, sem
):
    place = Place(nx, ny)
    size_x, size_y, depth = grad1.shape
    rows = size_y + 8
    moves = shifts(rows, depth)
    factor = h_factor(place, size_y, rows, depth)

    def h_second(p):
        h_plane(e1, h1, h, p, factor * jnp.where(place.plane(p, size_x), 1.0, 0.0), moves)

    sweep(0, size_x + 3, h_second, 7)

    def e_second(p, inner):
        fade, rise = decay[p], gain[p]
        total = None
        for c, curl in enumerate(curl_h(h, p, moves)):
            new = fade * e1[c, p] + rise * (curl - src1[c, p])
            e[c, p] = new
            if inner:
                term = fwd[1, c, p - 2].astype(jnp.float32) * new[:size_y]
                total = term if total is None else total + term
        if inner:
            grad[p - 2] = grad1[p - 2] + total

    e_second(1, False)

    def e_inner(p):
        e_second(p, True)

    sweep(2, size_x, e_inner, 8)
    e_second(size_x + 2, False)

    def h_third(p):
        h_plane(e, h, h, p, factor * jnp.where(place.plane(p, size_x), 1.0, 0.0), moves)

    sweep(1, size_x + 1, h_third, 11)
    inside = pl.ds(0, size_y)
    h_copy = pltpu.make_async_copy(h.at[:, pl.ds(2, size_x), inside], h_out, sem.at[0])
    h_copy.start()

    def e_third(x):
        p = x + 2
        fade, rise = decay[p, :size_y], gain[p, :size_y]
        total = grad[x]
        for c, curl in enumerate(curl_h(h, p, moves)):
            source = src[c, x, pl.ds(2, size_y, stride=FIELDS), :]
            new = fade * e[c, p, :size_y] + rise * (curl[:size_y] - source)
            e[c, p, :size_y] = new
            total = total + fwd[2, c, x].astype(jnp.float32) * new
        grad[x] = total

    each = size_x // PARTS

    def results(k):
        here = pl.ds(k * each, each)
        return (
            pltpu.make_async_copy(e.at[:, pl.ds(2 + k * each, each), inside], e_out.at[:, here], sem.at[1 + 2 * k]),
            pltpu.make_async_copy(grad.at[here], grad_out.at[here], sem.at[2 + 2 * k]),
        )

    def part(k, _):
        for x in range(each):
            e_third(k * each + x)
        for copy in results(k):
            copy.start()
        return 0

    lax.fori_loop(0, PARTS, part, 0)
    h_copy.wait()
    for k in range(PARTS):
        for copy in results(k):
            copy.wait()


def finish(nx, ny, e1, h1, decay, gain, src1, src, fwd, grad1):
    size_x, size_y, depth = grad1.shape
    field = f32(3, size_x, size_y, depth)
    return pl.pallas_call(
        functools.partial(finish_kernel, nx, ny),
        out_shape=[field, field, f32(size_x, size_y, depth)],
        in_specs=in_vmem(8),
        out_specs=[pl.BlockSpec(memory_space=pltpu.HBM)] * 3,
        scratch_shapes=[
            pltpu.VMEM(e1.shape, jnp.float32),
            pltpu.VMEM(h1.shape, jnp.float32),
            pltpu.VMEM(grad1.shape, jnp.float32),
            pltpu.SemaphoreType.DMA((1 + 2 * PARTS,)),
        ],
        compiler_params=pltpu.CompilerParams(vmem_limit_bytes=10 * MIB),
        name="finish",
    )(e1, h1, decay, gain, src1, src, fwd, grad1)


def per_device(
    e_adjoint,
    h_adjoint,
    conductivity,
    permittivity,
    forward_e,
    receiver_data,
    receiver_tile,
    receiver_cell,
    receiver_comp,
):
    _, size_x, size_y, depth = e_adjoint.shape
    nx, ny = lax.axis_size("gx"), lax.axis_size("gy")
    receivers = receiver_data.shape[0]
    cap = 3 * receivers // (nx * ny)
    by_lane = lambda a: a.reshape(receivers // LANES, LANES)
    got, codes, h1, base, decay, gain = route(
        nx,
        ny,
        receiver_data,
        by_lane(receiver_tile),
        by_lane(receiver_cell),
        by_lane(receiver_comp),
        e_adjoint,
        h_adjoint,
        conductivity,
        permittivity,
    )
    placed = scatter(cap, 3 * size_x * size_y, codes, got)
    placed = placed.reshape(3, size_x, size_y * FIELDS, depth)
    e1, src1, grad1 = share(nx, ny, base, gain, placed, forward_e)
    return tuple(finish(nx, ny, e1, h1, decay, gain, src1, placed, forward_e, grad1))


def solution(mesh):
    placed = (
        P(None, "gx", "gy", None),
        P(None, "gx", "gy", None),
        P("gx", "gy", None),
        P("gx", "gy", None),
        P(None, None, "gx", "gy", None),
        P(("gx", "gy"), None),
        P(("gx", "gy"), None),
        P(("gx", "gy")),
        P(("gx", "gy")),
    )
    return jax.shard_map(
        per_device,
        mesh=mesh,
        in_specs=placed,
        out_specs=(P(None, "gx", "gy", None), P(None, "gx", "gy", None), P("gx", "gy", None)),
        check_vma=False,
    )
```

```python
import functools

import jax
import jax.numpy as jnp
from jax import lax
from jax.experimental import pallas as pl
from jax.experimental.pallas import tpu as pltpu
from jax.sharding import PartitionSpec as P

STEPS = 3
SAMPLES = 128
LANES = 128
FIELDS = 4
SPAN = LANES // FIELDS
MESH = pl.DeviceIdType.MESH
GROUP = 8
PARTS = 4
MIB = 1 << 20

time_step = 0.55


def split3(x):
    a = x.astype(jnp.bfloat16)
    rest = x - a.astype(jnp.float32)
    b = rest.astype(jnp.bfloat16)
    c = (rest - b.astype(jnp.float32)).astype(jnp.bfloat16)
    return a, b, c


def mm(a, b, contract=((1,), (0,))):
    return lax.dot_general(a, b, (contract, ((), ())), preferred_element_type=jnp.float32)


def time_kernel():
    shape = (SAMPLES, LANES)
    sample = lax.broadcasted_iota(jnp.int32, shape, 0).astype(jnp.float32)
    field = lax.broadcasted_iota(jnp.int32, shape, 1) // SPAN
    centre = (field.astype(jnp.float32) + 0.5) * (SAMPLES / STEPS)
    spread = SAMPLES / (4.0 * STEPS)
    kernel = jnp.exp(-jnp.square((sample - centre) / spread))
    norm = jnp.sum(kernel * kernel, axis=0, keepdims=True)
    return jnp.where(field < STEPS, kernel / jnp.sqrt(norm), 0.0)


def pack(devices, cells, data_ref, tile_ref, cell_ref, comp_ref):
    blocks, width = tile_ref.shape
    kernel = time_kernel()
    at, to = (lax.broadcasted_iota(jnp.int32, (width, width), n) for n in (0, 1))
    before = (at < to).astype(jnp.bfloat16)
    every = jnp.ones((width, width), jnp.bfloat16)
    diagonal = at == to
    destination = lax.broadcasted_iota(jnp.int32, (devices, width), 0)
    lane = lax.broadcasted_iota(jnp.int32, (width, LANES), 1)
    slot = jnp.bitwise_and(lane, SPAN - 1).astype(jnp.float32)
    is_code = lane >= STEPS * SPAN
    down = jnp.ones((width, LANES), jnp.bfloat16)
    seen = jnp.zeros((devices, width), jnp.float32)
    packed = jnp.zeros((devices, LANES), jnp.float32)

    def column(row):
        return jnp.where(diagonal, row.astype(jnp.float32), 0.0).astype(jnp.bfloat16)

    for b in range(blocks):
        onehot = (destination == tile_ref[b : b + 1, :]).astype(jnp.float32)
        hot = onehot.astype(jnp.bfloat16)
        rank = jnp.sum(onehot * (seen + mm(hot, before)), axis=0, keepdims=True)
        seen = seen + mm(hot, every)
        amplitude = lax.dot_general(
            data_ref[b * width : (b + 1) * width, :],
            kernel,
            (((1,), (0,)), ((), ())),
            precision=lax.Precision.HIGHEST,
            preferred_element_type=jnp.float32,
        )
        code = comp_ref[b : b + 1, :] * cells + cell_ref[b : b + 1, :]
        low = jnp.bitwise_and(code, 255)
        middle = jnp.bitwise_and(code, 255 << 8)
        high = code - low - middle
        codes = mm(column(low), down) + mm(column(middle), down) + mm(column(high), down)
        spread = jnp.where(
            slot == mm(column(rank), down), jnp.where(is_code, codes, amplitude), 0.0
        )
        for term in split3(spread):
            packed = packed + mm(hot, term)
    return packed


def sweep(start, count, body, width):
    def several(n, _):
        for k in range(width):
            body(start + n * width + k)
        return 0

    turns = count // width
    lax.fori_loop(0, turns, several, 0)
    for p in range(turns * width, count):
        body(start + p)


class Place:
    def __init__(self, nx, ny):
        self.nx, self.ny = nx, ny
        self.ix, self.iy = lax.axis_index("gx"), lax.axis_index("gy")
        self.inside_x = {-1: self.ix > 0, 0: None, 1: self.ix < nx - 1}
        self.inside_y = {-1: self.iy > 0, 0: None, 1: self.iy < ny - 1}

    def other(self, dx, dy):
        return lax.rem(self.ix + dx + self.nx, self.nx), lax.rem(self.iy + dy + self.ny, self.ny)

    def has(self, dx, dy):
        x, y = self.inside_x[dx], self.inside_y[dy]
        if x is None or y is None:
            return y if x is None else x
        return jnp.logical_and(x, y)

    def plane(self, p, size_x):
        low, high = jnp.logical_or(p >= 2, self.ix > 0), jnp.logical_or(p < size_x + 2, self.ix < self.nx - 1)
        return jnp.logical_and(low, high)


AROUND = tuple((dx, dy) for dx in (-1, 0, 1) for dy in (-1, 0, 1) if (dx, dy) != (0, 0))


def greet(place, barrier, offsets):
    count = jnp.int32(0)
    for dx, dy in offsets:
        here = place.has(dx, dy)
        count = count + here.astype(jnp.int32)

        @pl.when(here)
        def _(dx=dx, dy=dy):
            pl.semaphore_signal(barrier, inc=1, device_id=place.other(dx, dy), device_id_type=MESH)

    return count


def shifts(rows, depth):
    lane = lax.broadcasted_iota(jnp.int32, (rows, depth), 1)

    def up_z(f):
        return jnp.where(lane == depth - 1, 0.0, pltpu.roll(f, depth - 1, 1))

    def down_z(f):
        return jnp.where(lane == 0, 0.0, pltpu.roll(f, 1, 1))

    def up_y(f):
        return pltpu.roll(f, rows - 1, 0)

    def down_y(f):
        return pltpu.roll(f, 1, 0)

    return up_z, down_z, up_y, down_y


def h_plane(e, h_from, h_to, p, factor, moves):
    up_z, _, up_y, _ = moves
    ex, ey, ez = e[0, p], e[1, p], e[2, p]
    curl_x = (up_y(ez) - ez) - (up_z(ey) - ey)
    curl_y = (up_z(ex) - ex) - (e[2, p + 1] - ez)
    curl_z = (e[1, p + 1] - ey) - (up_y(ex) - ex)
    for c, curl in enumerate((curl_x, curl_y, curl_z)):
        h_to[c, p] = h_from[c, p] - factor * curl


def curl_h(h, p, moves):
    _, down_z, _, down_y = moves
    hx, hy, hz = h[0, p], h[1, p], h[2, p]
    curl_x = (hz - down_y(hz)) - (hy - down_z(hy))
    curl_y = (hx - down_z(hx)) - (hz - h[2, p - 1])
    curl_z = (hy - h[1, p - 1]) - (hx - down_y(hx))
    return curl_x, curl_y, curl_z


def h_factor(place, size_y, rows, depth):
    row = lax.broadcasted_iota(jnp.int32, (rows, depth), 0)
    above, below = jnp.where(place.has(0, 1), 1.0, 0.0), jnp.where(place.has(0, -1), 1.0, 0.0)
    return time_step * jnp.where(row < size_y, 1.0, jnp.where(row < size_y + 4, above, below))


def row_copies(dn_put, up_put, up_got, lo_got, size_x):
    first, last, low, high = pl.ds(0, 2), pl.ds(size_x - 2, 2), pl.ds(0, 2), pl.ds(size_x + 2, 2)
    whole = pl.ds(2, size_x)
    return [
        (dn_put.at[:, first], up_got.at[:, high], -1, -1),
        (dn_put.at[:, last], up_got.at[:, low], 1, -1),
        (up_put.at[:, first], lo_got.at[:, high], -1, 1),
        (up_put.at[:, last], lo_got.at[:, low], 1, 1),
        (dn_put, up_got.at[:, whole], 0, -1),
        (up_put, lo_got.at[:, whole], 0, 1),
    ]


def plane_copies(array, count, size_x, size_y):
    lead = (slice(None),) * (len(array.shape) - 3)
    rows = pl.ds(0, size_y)

    def part(start):
        return array.at[(*lead, pl.ds(start, count), rows)]

    return [
        (part(2), part(size_x + 2), -1, 0),
        (part(size_x + 2 - count), part(2 - count), 1, 0),
    ]


FIELD_DOWN = ((0, 0, 0), (0, 1, 0), (0, 2, 0), (0, 0, 1), (0, 2, 1))
FIELD_UP = tuple((0, c, r) for c in range(3) for r in range(2))
ROUTE_DOWN = (*FIELD_DOWN, (1, 0, 0), (1, 1, 0), (1, 2, 0), (2, 0, 0), (3, 0, 0))
ROUTE_UP = (*FIELD_UP, (1, 0, 0), (1, 2, 0), (1, 0, 1), (1, 1, 1), (1, 2, 1), (2, 0, 1), (3, 0, 1))
SHARE_DOWN = (*FIELD_DOWN, (1, 0, 0), (1, 2, 0))
SHARE_UP = (*FIELD_UP, (1, 0, 1), (1, 1, 1), (1, 2, 1))


def halo_scratch(down, up, size_x, depth):
    shapes = [(len(down), size_x), (len(up), size_x), (len(down), size_x + 4), (len(up), size_x + 4)]
    return [pltpu.VMEM((*shape, 1, depth), jnp.float32) for shape in shapes]


def halo_rows(array, c, p, down, up, up_got, lo_got, above, below, fill):
    def one(names, got, r, keep):
        if (array, c, r) not in names:
            return fill
        return jnp.where(keep, got[names.index((array, c, r)), p], fill)

    return jnp.concatenate(
        [one(down, up_got, 0, above), one(down, up_got, 1, above)]
        + [fill] * 4
        + [one(up, lo_got, 0, below), one(up, lo_got, 1, below)],
        axis=0,
    )


class Exchange:
    def __init__(self, place, parts, send, recv):
        self.parts = []
        for n, (a, b, dx, dy) in enumerate(parts):
            copy = pltpu.make_async_remote_copy(
                src_ref=a,
                dst_ref=b,
                send_sem=send.at[n],
                recv_sem=recv.at[n],
                device_id=place.other(dx, dy),
                device_id_type=MESH,
            )
            self.parts.append((copy, place.has(dx, dy), place.has(-dx, -dy)))
            pl.when(self.parts[-1][1])(copy.start)

    def wait(self):
        for copy, goes, comes in self.parts:
            pl.when(comes)(copy.wait_recv)
            pl.when(goes)(copy.wait_send)


def parts_of(state):
    return state.at[pl.ds(0, 3)], state.at[pl.ds(3, 3)], state.at[6], state.at[7]


def route_kernel(
    nx,
    ny,
    cells,
    data_in,
    tile_in,
    cell_in,
    comp_in,
    e_in,
    h_in,
    cond_in,
    perm_in,
    got_ref,
    code_ref,
    state,
    base,
    data_ref,
    tile_ref,
    cell_ref,
    comp_ref,
    first,
    mid,
    second,
    last,
    dn_put,
    up_put,
    up_got,
    lo_got,
    load,
    send_y,
    recv_y,
    send_x,
    recv_x,
    send,
    recv,
):
    place = Place(nx, ny)
    ix, iy = place.ix, place.iy
    e, h, decay, gain = parts_of(state)
    size_x, size_y, depth = base.shape[1:]
    rows = size_y + 8
    inner = (pl.ds(2, size_x), pl.ds(0, size_y))
    pairs = (
        (tile_in, tile_ref),
        (cell_in, cell_ref),
        (comp_in, comp_ref),
        (data_in, data_ref),
        (e_in, e.at[:, inner[0], inner[1]]),
        (h_in, h.at[:, inner[0], inner[1]]),
        (cond_in, decay.at[inner[0], inner[1]]),
        (perm_in, gain.at[inner[0], inner[1]]),
    )
    loads = [pltpu.make_async_copy(a, b, load.at[n]) for n, (a, b) in enumerate(pairs)]
    for copy in loads:
        copy.start()
    barrier = pltpu.get_barrier_semaphore()
    for k in range(1, nx):
        pl.semaphore_signal(barrier, inc=1, device_id=(lax.rem(ix + k, nx), iy), device_id_type=MESH)
    for k in range(1, ny):
        pl.semaphore_signal(barrier, inc=1, device_id=(ix, lax.rem(iy + k, ny)), device_id_type=MESH)
    corners = greet(place, barrier, [o for o in AROUND if 0 not in o])
    for copy in loads[:4]:
        copy.wait()
    first[...] = pack(nx * ny, cells, data_ref, tile_ref, cell_ref, comp_ref)
    for copy in loads[4:]:
        copy.wait()

    def stage(x):
        p = x + 2
        arrays = ((e.at[0], e.at[1], e.at[2]), (h.at[0], h.at[1], h.at[2]), (decay,), (gain,))
        for n, (array, c, r) in enumerate(ROUTE_DOWN):
            dn_put[n, x] = arrays[array][c][p, r : r + 1, :]
        for n, (array, c, r) in enumerate(ROUTE_UP):
            up_put[n, x] = arrays[array][c][p, size_y - 2 + r : size_y - 1 + r, :]

    sweep(0, size_x, stage, 4)
    pl.semaphore_wait(barrier, corners + (nx + ny - 2))
    by_row = Exchange(
        place, row_copies(dn_put, up_put, up_got, lo_got, size_x), send.at[0], recv.at[0]
    )
    copies = []
    for k in range(1, nx):
        to = lax.rem(ix + k, nx)
        copy = pltpu.make_async_remote_copy(
            src_ref=first.at[pl.ds(pl.multiple_of(to * ny, ny), ny), :],
            dst_ref=mid.at[pl.ds(pl.multiple_of(ix * ny, ny), ny), :],
            send_sem=send_x.at[k - 1],
            recv_sem=recv_x.at[k - 1],
            device_id=(to, iy),
            device_id_type=MESH,
        )
        copy.start()
        copies.append(copy)
    by_plane = Exchange(
        place, plane_copies(state, 2, size_x, size_y), send.at[1], recv.at[1]
    )
    own = pl.ds(pl.multiple_of(ix * ny, ny), ny)
    mid[own, :] = first[own, :]
    for copy in copies:
        copy.wait_recv()
    for j in range(ny):
        second[j * nx : (j + 1) * nx, :] = mid[pl.ds(j, nx, stride=ny), :]
    later = []
    for k in range(1, ny):
        to = lax.rem(iy + k, ny)
        copy = pltpu.make_async_remote_copy(
            src_ref=second.at[pl.ds(pl.multiple_of(to * nx, nx), nx), :],
            dst_ref=last.at[pl.ds(pl.multiple_of(iy * nx, nx), nx), :],
            send_sem=send_y.at[k - 1],
            recv_sem=recv_y.at[k - 1],
            device_id=(ix, to),
            device_id_type=MESH,
        )
        copy.start()
        later.append(copy)
    own = pl.ds(pl.multiple_of(iy * nx, nx), nx)
    last[own, :] = second[own, :]
    for copy in copies:
        copy.wait_send()

    by_plane.wait()
    by_row.wait()
    for p in (0, 1, size_x + 2, size_x + 3):
        keep = place.plane(p, size_x)
        for c in range(3):
            for array in (e, h):
                array[c, p, :size_y] = jnp.where(keep, array[c, p, :size_y], 0.0)

    def unstage(p):
        keep = place.plane(p, size_x)
        above, below = jnp.logical_and(keep, place.has(0, 1)), jnp.logical_and(keep, place.has(0, -1))
        gap = jnp.zeros((1, depth), jnp.float32)
        for array, field in enumerate((e, h)):
            for c in range(3):
                field[c, p, size_y:] = halo_rows(
                    array, c, p, ROUTE_DOWN, ROUTE_UP, up_got, lo_got, above, below, gap
                )

    sweep(0, size_x + 4, unstage, 4)
    row = lax.broadcasted_iota(jnp.int32, (rows, depth), 0)
    inside = jnp.where(
        row < size_y,
        1.0,
        jnp.where(
            row == size_y,
            jnp.where(place.has(0, 1), 1.0, 0.0),
            jnp.where(row == rows - 1, jnp.where(place.has(0, -1), 1.0, 0.0), 0.0),
        ),
    )
    ones = jnp.ones((1, depth), jnp.float32)

    def coefficients(p):
        for array, field in ((2, decay), (3, gain)):
            field[p, size_y:] = halo_rows(array, 0, p, ROUTE_DOWN, ROUTE_UP, up_got, lo_got, True, True, ones)
        half_loss = decay[p] * (0.5 * time_step)
        eps = gain[p]
        inverse = 1.0 / (eps + half_loss)
        keep = inside > jnp.where(place.plane(p, size_x), 0.5, 1.5)
        decay[p] = jnp.where(keep, (eps - half_loss) * inverse, 0.0)
        gain[p] = jnp.where(keep, time_step * inverse, 0.0)

    sweep(1, size_x + 2, coefficients, 2)
    moves = shifts(rows, depth)
    factor = h_factor(place, size_y, rows, depth)

    def h_step(p):
        h_plane(e, h, h, p, factor * jnp.where(place.plane(p, size_x), 1.0, 0.0), moves)

    sweep(0, size_x + 3, h_step, 7)

    def e_step(x):
        p = x + 2
        for c, curl in enumerate(curl_h(h, p, moves)):
            new = decay[p] * e[c, p] + gain[p] * curl
            base[c, x] = new[:size_y]

    sweep(0, size_x, e_step, 8)

    for copy in later:
        copy.wait()
    got_ref[...] = last[...]
    quarter = nx * ny // FIELDS
    lane = lax.broadcasted_iota(jnp.int32, (quarter, LANES), 1) // SPAN
    codes = jnp.zeros((quarter, LANES), jnp.int32)
    for k in range(FIELDS):
        code = last[pl.ds(k, quarter, stride=FIELDS), :].astype(jnp.int32)
        word = jnp.bitwise_and(code, LANES - 1) + jnp.bitwise_and(code, -LANES) * FIELDS
        codes = jnp.where(lane == k, pltpu.roll(word, (k + 1) * SPAN % LANES, 1), codes)
    code_ref[...] = codes


def in_vmem(count):
    return [pl.BlockSpec(memory_space=pltpu.VMEM)] * count


def f32(*shape):
    return jax.ShapeDtypeStruct(shape, jnp.float32)


def route(nx, ny, data, tile, cell, comp, e, h, cond, perm):
    devices = nx * ny
    size_x, size_y, depth = cond.shape
    wide, tall = size_x + 4, size_y + 8
    inputs = (data, tile, cell, comp, e, h, cond, perm)
    rows = lambda: pltpu.VMEM((devices, LANES), jnp.float32)
    return pl.pallas_call(
        functools.partial(route_kernel, nx, ny, size_x * size_y * depth),
        out_shape=[
            f32(devices, LANES),
            jax.ShapeDtypeStruct((devices // FIELDS, LANES), jnp.int32),
            f32(8, wide, tall, depth),
            f32(3, size_x, size_y, depth),
        ],
        in_specs=[pl.BlockSpec(memory_space=pltpu.HBM)] * 8,
        out_specs=in_vmem(4),
        scratch_shapes=[
            *(pltpu.VMEM(a.shape, a.dtype) for a in (data, tile, cell, comp)),
            rows(),
            rows(),
            rows(),
            rows(),
            *halo_scratch(ROUTE_DOWN, ROUTE_UP, size_x, depth),
            pltpu.SemaphoreType.DMA((8,)),
            pltpu.SemaphoreType.DMA((ny - 1,)),
            pltpu.SemaphoreType.DMA((ny - 1,)),
            pltpu.SemaphoreType.DMA((nx - 1,)),
            pltpu.SemaphoreType.DMA((nx - 1,)),
            pltpu.SemaphoreType.DMA((2, 8)),
            pltpu.SemaphoreType.DMA((2, 8)),
        ],
        compiler_params=pltpu.CompilerParams(
            collective_id=0, has_side_effects=True, vmem_limit_bytes=16 * MIB
        ),
        name="route",
    )(*(pltpu.with_memory_space_constraint(a, pltpu.HBM) for a in inputs))


def scatter_kernel(cap, code_in, got_ref, out_ref, code_ref, quad, terms, wide, sem):
    fetch = pltpu.make_async_copy(code_in, code_ref, sem)
    fetch.start()
    devices = got_ref.shape[0]
    got = got_ref[...]
    lane = lax.broadcasted_iota(jnp.int32, (devices, LANES), 1)
    slot = jnp.bitwise_and(lane, SPAN - 1)
    codes = jnp.where(lane >= (FIELDS - 1) * SPAN, got, 0.0)
    codes = codes + pltpu.roll(codes, SPAN, 1)
    codes = codes + pltpu.roll(codes, 2 * SPAN, 1)
    total = got
    place_in_group = slot - slot // GROUP * GROUP
    for d in range(1, GROUP):
        same = (codes == pltpu.roll(codes, d, 1)) & (place_in_group >= d)
        total = total + jnp.where(same, pltpu.roll(got, d, 1), 0.0)
    for t in range(FIELDS):
        quad[pl.ds(t, devices, stride=FIELDS), :] = jnp.where(
            (lane >= t * SPAN) & (lane < (t + 1) * SPAN), total, 0.0
        )
    values = quad[...]
    high = values.astype(jnp.bfloat16)
    low = (values - high.astype(jnp.float32)).astype(jnp.bfloat16)
    terms[:, :LANES] = high
    terms[:, LANES:] = low
    row_slot = jnp.bitwise_and(lax.broadcasted_iota(jnp.int32, (2 * LANES, 2 * LANES), 0), SPAN - 1)
    column = lax.broadcasted_iota(jnp.int32, (2 * LANES, 2 * LANES), 1) // LANES
    for i in range(0, cap, 2):
        both = mm(terms[...], (row_slot == column + i).astype(jnp.bfloat16))
        wide[i] = both[:, :LANES]
        wide[i + 1] = both[:, LANES:]
    step = 512

    def clear(n, _):
        out_ref[pl.ds(pl.multiple_of(n * step, step), step), :] = jnp.zeros((step, LANES), jnp.float32)
        return 0

    lax.fori_loop(0, out_ref.shape[0] // step, clear, 0)
    fetch.wait()
    depth = lax.broadcasted_iota(jnp.int32, (FIELDS, LANES), 1)

    def place(q, _):
        for p in range(FIELDS):
            s = q * FIELDS + p
            for start in range(0, cap, GROUP):
                where, news = [], []
                for i in range(start, min(cap, start + GROUP)):
                    word = code_ref[q, p * SPAN + i]
                    row = pl.ds(pl.multiple_of(lax.shift_right_logical(word, 7), FIELDS), FIELDS)
                    news.append(out_ref[row, :] + wide[i, pl.ds(pl.multiple_of(s * FIELDS, FIELDS), FIELDS), :])
                    column = jnp.bitwise_and(jnp.full((FIELDS, LANES), word, jnp.int32), LANES - 1)
                    where.append((row, depth == column))
                for (row, mask), new in zip(where, news):
                    pltpu.store(out_ref.at[row, :], new, mask=mask)
        return 0

    lax.fori_loop(0, devices // FIELDS, place, 0)


def scatter(cap, rows, codes, got):
    devices = got.shape[0]
    return pl.pallas_call(
        functools.partial(scatter_kernel, cap),
        out_shape=jax.ShapeDtypeStruct((rows * FIELDS, LANES), jnp.float32),
        in_specs=[pl.BlockSpec(memory_space=pltpu.VMEM)] * 2,
        out_specs=pl.BlockSpec(memory_space=pltpu.VMEM),
        scratch_shapes=[
            pltpu.SMEM(codes.shape, jnp.int32),
            pltpu.VMEM((devices * FIELDS, LANES), jnp.float32),
            pltpu.VMEM((devices * FIELDS, 2 * LANES), jnp.bfloat16),
            pltpu.VMEM((cap, devices * FIELDS, LANES), jnp.float32),
            pltpu.SemaphoreType.DMA,
        ],
        compiler_params=pltpu.CompilerParams(vmem_limit_bytes=24 * MIB),
        name="scatter",
    )(codes, got)


def share_kernel(
    nx, ny, base, state, src, fwd, both, grad, dn_put, up_put, up_got, lo_got, send, recv
):
    place = Place(nx, ny)
    gain = parts_of(state)[3]
    e, src1 = both.at[pl.ds(0, 3)], both.at[pl.ds(3, 3)]
    size_x, size_y, depth = base.shape[1:]
    barrier = pltpu.get_barrier_semaphore()
    others = greet(place, barrier, AROUND)

    def own(x):
        p = x + 2
        rise = gain[p, :size_y]
        for c in range(3):
            new = base[c, x] - rise * src[c, x, pl.ds(0, size_y, stride=FIELDS), :]
            e[c, p, :size_y] = new
            source = src[c, x, pl.ds(1, size_y, stride=FIELDS), :]
            src1[c, p, :size_y] = source
            for n, (array, comp, r) in enumerate(SHARE_DOWN):
                if comp == c:
                    dn_put[n, x] = (new, source)[array][r : r + 1]
            for n, (array, comp, r) in enumerate(SHARE_UP):
                if comp == c:
                    up_put[n, x] = (new, source)[array][size_y - 2 + r : size_y - 1 + r]

    sweep(0, size_x, own, 4)
    pl.semaphore_wait(barrier, others)
    halos = Exchange(
        place,
        row_copies(dn_put, up_put, up_got, lo_got, size_x)
        + plane_copies(both, 2, size_x, size_y),
        send,
        recv,
    )

    def product(x):
        total = fwd[0, 0, x].astype(jnp.float32) * e[0, x + 2, :size_y]
        for c in (1, 2):
            total = total + fwd[0, c, x].astype(jnp.float32) * e[c, x + 2, :size_y]
        grad[x] = total

    sweep(0, size_x, product, 4)
    halos.wait()
    for p in (0, 1, size_x + 2, size_x + 3):
        keep = place.plane(p, size_x)
        for c in range(3):
            e[c, p, :size_y] = jnp.where(keep, e[c, p, :size_y], 0.0)
            src1[c, p, :size_y] = jnp.where(keep, src1[c, p, :size_y], 0.0)

    def unstage(p):
        keep = place.plane(p, size_x)
        above, below = jnp.logical_and(keep, place.has(0, 1)), jnp.logical_and(keep, place.has(0, -1))
        gap = jnp.zeros((1, depth), jnp.float32)
        for array, field in enumerate((e, src1)):
            for c in range(3):
                field[c, p, size_y:] = halo_rows(
                    array, c, p, SHARE_DOWN, SHARE_UP, up_got, lo_got, above, below, gap
                )

    sweep(0, size_x + 4, unstage, 4)


def share(nx, ny, base, state, src, fwd):
    size_x, size_y, depth = base.shape[1:]
    wide, tall = size_x + 4, size_y + 8
    return pl.pallas_call(
        functools.partial(share_kernel, nx, ny),
        out_shape=[f32(6, wide, tall, depth), f32(size_x, size_y, depth)],
        in_specs=in_vmem(4),
        out_specs=in_vmem(2),
        scratch_shapes=[
            *halo_scratch(SHARE_DOWN, SHARE_UP, size_x, depth),
            pltpu.SemaphoreType.DMA((8,)),
            pltpu.SemaphoreType.DMA((8,)),
        ],
        compiler_params=pltpu.CompilerParams(
            collective_id=1, has_side_effects=True, vmem_limit_bytes=6 * MIB
        ),
        name="share",
    )(base, state, src, fwd)


def finish_kernel(
    nx, ny, both, state, src, fwd, grad1, e_out, h_out, grad_out, e, h, grad, sem
):
    place = Place(nx, ny)
    e1, src1 = both.at[pl.ds(0, 3)], both.at[pl.ds(3, 3)]
    _, h1, decay, gain = parts_of(state)
    size_x, size_y, depth = grad1.shape
    rows = size_y + 8
    moves = shifts(rows, depth)
    factor = h_factor(place, size_y, rows, depth)

    def h_second(p):
        h_plane(e1, h1, h, p, factor * jnp.where(place.plane(p, size_x), 1.0, 0.0), moves)

    sweep(0, size_x + 3, h_second, 7)

    def e_second(p, inner):
        fade, rise = decay[p], gain[p]
        total = None
        for c, curl in enumerate(curl_h(h, p, moves)):
            new = fade * e1[c, p] + rise * (curl - src1[c, p])
            e[c, p] = new
            if inner:
                term = fwd[1, c, p - 2].astype(jnp.float32) * new[:size_y]
                total = term if total is None else total + term
        if inner:
            grad[p - 2] = grad1[p - 2] + total

    e_second(1, False)

    def e_inner(p):
        e_second(p, True)

    sweep(2, size_x, e_inner, 8)
    e_second(size_x + 2, False)

    def h_third(p):
        h_plane(e, h, h, p, factor * jnp.where(place.plane(p, size_x), 1.0, 0.0), moves)

    sweep(1, size_x + 1, h_third, 11)
    inside = pl.ds(0, size_y)
    h_copy = pltpu.make_async_copy(h.at[:, pl.ds(2, size_x), inside], h_out, sem.at[0])
    h_copy.start()

    def e_third(x):
        p = x + 2
        fade, rise = decay[p, :size_y], gain[p, :size_y]
        total = grad[x]
        for c, curl in enumerate(curl_h(h, p, moves)):
            source = src[c, x, pl.ds(2, size_y, stride=FIELDS), :]
            new = fade * e[c, p, :size_y] + rise * (curl[:size_y] - source)
            e[c, p, :size_y] = new
            total = total + fwd[2, c, x].astype(jnp.float32) * new
        grad[x] = total

    each = size_x // PARTS

    def results(k):
        here = pl.ds(k * each, each)
        return (
            pltpu.make_async_copy(e.at[:, pl.ds(2 + k * each, each), inside], e_out.at[:, here], sem.at[1 + 2 * k]),
            pltpu.make_async_copy(grad.at[here], grad_out.at[here], sem.at[2 + 2 * k]),
        )

    def part(k, _):
        for x in range(each):
            e_third(k * each + x)
        for copy in results(k):
            copy.start()
        return 0

    lax.fori_loop(0, PARTS, part, 0)
    h_copy.wait()
    for k in range(PARTS):
        for copy in results(k):
            copy.wait()


def finish(nx, ny, both, state, src, fwd, grad1):
    size_x, size_y, depth = grad1.shape
    field = f32(3, size_x, size_y, depth)
    return pl.pallas_call(
        functools.partial(finish_kernel, nx, ny),
        out_shape=[field, field, f32(size_x, size_y, depth)],
        in_specs=in_vmem(5),
        out_specs=[pl.BlockSpec(memory_space=pltpu.HBM)] * 3,
        scratch_shapes=[
            pltpu.VMEM((3, *both.shape[1:]), jnp.float32),
            pltpu.VMEM((3, *both.shape[1:]), jnp.float32),
            pltpu.VMEM(grad1.shape, jnp.float32),
            pltpu.SemaphoreType.DMA((1 + 2 * PARTS,)),
        ],
        compiler_params=pltpu.CompilerParams(vmem_limit_bytes=10 * MIB),
        name="finish",
    )(both, state, src, fwd, grad1)


def per_device(
    e_adjoint,
    h_adjoint,
    conductivity,
    permittivity,
    forward_e,
    receiver_data,
    receiver_tile,
    receiver_cell,
    receiver_comp,
):
    _, size_x, size_y, depth = e_adjoint.shape
    nx, ny = lax.axis_size("gx"), lax.axis_size("gy")
    receivers = receiver_data.shape[0]
    cap = 3 * receivers // (nx * ny)
    by_lane = lambda a: a.reshape(receivers // LANES, LANES)
    got, codes, state, base = route(
        nx,
        ny,
        receiver_data,
        by_lane(receiver_tile),
        by_lane(receiver_cell),
        by_lane(receiver_comp),
        e_adjoint,
        h_adjoint,
        conductivity,
        permittivity,
    )
    placed = scatter(cap, 3 * size_x * size_y, codes, got)
    placed = placed.reshape(3, size_x, size_y * FIELDS, depth)
    both, grad1 = share(nx, ny, base, state, placed, forward_e)
    return tuple(finish(nx, ny, both, state, placed, forward_e, grad1))


def solution(mesh):
    placed = (
        P(None, "gx", "gy", None),
        P(None, "gx", "gy", None),
        P("gx", "gy", None),
        P("gx", "gy", None),
        P(None, None, "gx", "gy", None),
        P(("gx", "gy"), None),
        P(("gx", "gy"), None),
        P(("gx", "gy")),
        P(("gx", "gy")),
    )
    return jax.shard_map(
        per_device,
        mesh=mesh,
        in_specs=placed,
        out_specs=(P(None, "gx", "gy", None), P(None, "gx", "gy", None), P("gx", "gy", None)),
        check_vma=False,
    )
```

```python
import functools

import jax
import jax.numpy as jnp
from jax import lax
from jax.experimental import pallas as pl
from jax.experimental.pallas import tpu as pltpu
from jax.sharding import PartitionSpec as P

STEPS = 3
SAMPLES = 128
LANES = 128
FIELDS = 4
SPAN = LANES // FIELDS
MESH = pl.DeviceIdType.MESH
GROUP = 8
PARTS = 4
MIB = 1 << 20

time_step = 0.55


def split3(x):
    a = x.astype(jnp.bfloat16)
    rest = x - a.astype(jnp.float32)
    b = rest.astype(jnp.bfloat16)
    c = (rest - b.astype(jnp.float32)).astype(jnp.bfloat16)
    return a, b, c


def mm(a, b, contract=((1,), (0,))):
    return lax.dot_general(a, b, (contract, ((), ())), preferred_element_type=jnp.float32)


def time_kernel():
    shape = (SAMPLES, LANES)
    sample = lax.broadcasted_iota(jnp.int32, shape, 0).astype(jnp.float32)
    field = lax.broadcasted_iota(jnp.int32, shape, 1) // SPAN
    centre = (field.astype(jnp.float32) + 0.5) * (SAMPLES / STEPS)
    spread = SAMPLES / (4.0 * STEPS)
    kernel = jnp.exp(-jnp.square((sample - centre) / spread))
    norm = jnp.sum(kernel * kernel, axis=0, keepdims=True)
    return jnp.where(field < STEPS, kernel / jnp.sqrt(norm), 0.0)


def pack(devices, cells, data_ref, tile_ref, cell_ref, comp_ref):
    blocks, width = tile_ref.shape
    kernel = time_kernel()
    at, to = (lax.broadcasted_iota(jnp.int32, (width, width), n) for n in (0, 1))
    before = (at < to).astype(jnp.bfloat16)
    every = jnp.ones((width, width), jnp.bfloat16)
    diagonal = at == to
    destination = lax.broadcasted_iota(jnp.int32, (devices, width), 0)
    lane = lax.broadcasted_iota(jnp.int32, (width, LANES), 1)
    slot = jnp.bitwise_and(lane, SPAN - 1).astype(jnp.float32)
    is_code = lane >= STEPS * SPAN
    down = jnp.ones((width, LANES), jnp.bfloat16)
    seen = jnp.zeros((devices, width), jnp.float32)
    packed = jnp.zeros((devices, LANES), jnp.float32)

    def column(row):
        return jnp.where(diagonal, row.astype(jnp.float32), 0.0).astype(jnp.bfloat16)

    for b in range(blocks):
        onehot = (destination == tile_ref[b : b + 1, :]).astype(jnp.float32)
        hot = onehot.astype(jnp.bfloat16)
        rank = jnp.sum(onehot * (seen + mm(hot, before)), axis=0, keepdims=True)
        seen = seen + mm(hot, every)
        amplitude = lax.dot_general(
            data_ref[b * width : (b + 1) * width, :],
            kernel,
            (((1,), (0,)), ((), ())),
            precision=lax.Precision.HIGHEST,
            preferred_element_type=jnp.float32,
        )
        code = comp_ref[b : b + 1, :] * cells + cell_ref[b : b + 1, :]
        low = jnp.bitwise_and(code, 255)
        middle = jnp.bitwise_and(code, 255 << 8)
        high = code - low - middle
        codes = mm(column(low), down) + mm(column(middle), down) + mm(column(high), down)
        spread = jnp.where(
            slot == mm(column(rank), down), jnp.where(is_code, codes, amplitude), 0.0
        )
        for term in split3(spread):
            packed = packed + mm(hot, term)
    return packed


def sweep(start, count, body, width):
    def several(n, _):
        for k in range(width):
            body(start + n * width + k)
        return 0

    turns = count // width
    lax.fori_loop(0, turns, several, 0)
    for p in range(turns * width, count):
        body(start + p)


class Place:
    def __init__(self, nx, ny):
        self.nx, self.ny = nx, ny
        self.ix, self.iy = lax.axis_index("gx"), lax.axis_index("gy")
        self.inside_x = {-1: self.ix > 0, 0: None, 1: self.ix < nx - 1}
        self.inside_y = {-1: self.iy > 0, 0: None, 1: self.iy < ny - 1}

    def other(self, dx, dy):
        return lax.rem(self.ix + dx + self.nx, self.nx), lax.rem(self.iy + dy + self.ny, self.ny)

    def has(self, dx, dy):
        x, y = self.inside_x[dx], self.inside_y[dy]
        if x is None or y is None:
            return y if x is None else x
        return jnp.logical_and(x, y)

    def plane(self, p, size_x):
        low, high = jnp.logical_or(p >= 2, self.ix > 0), jnp.logical_or(p < size_x + 2, self.ix < self.nx - 1)
        return jnp.logical_and(low, high)


AROUND = tuple((dx, dy) for dx in (-1, 0, 1) for dy in (-1, 0, 1) if (dx, dy) != (0, 0))


def greet(place, barrier, offsets):
    count = jnp.int32(0)
    for dx, dy in offsets:
        here = place.has(dx, dy)
        count = count + here.astype(jnp.int32)

        @pl.when(here)
        def _(dx=dx, dy=dy):
            pl.semaphore_signal(barrier, inc=1, device_id=place.other(dx, dy), device_id_type=MESH)

    return count


def shifts(rows, depth):
    lane = lax.broadcasted_iota(jnp.int32, (rows, depth), 1)

    def up_z(f):
        return jnp.where(lane == depth - 1, 0.0, pltpu.roll(f, depth - 1, 1))

    def down_z(f):
        return jnp.where(lane == 0, 0.0, pltpu.roll(f, 1, 1))

    def up_y(f):
        return pltpu.roll(f, rows - 1, 0)

    def down_y(f):
        return pltpu.roll(f, 1, 0)

    return up_z, down_z, up_y, down_y


def h_plane(e, h_from, h_to, p, factor, moves):
    up_z, _, up_y, _ = moves
    ex, ey, ez = e[0, p], e[1, p], e[2, p]
    curl_x = (up_y(ez) - ez) - (up_z(ey) - ey)
    curl_y = (up_z(ex) - ex) - (e[2, p + 1] - ez)
    curl_z = (e[1, p + 1] - ey) - (up_y(ex) - ex)
    for c, curl in enumerate((curl_x, curl_y, curl_z)):
        h_to[c, p] = h_from[c, p] - factor * curl


def curl_h(h, p, moves):
    _, down_z, _, down_y = moves
    hx, hy, hz = h[0, p], h[1, p], h[2, p]
    curl_x = (hz - down_y(hz)) - (hy - down_z(hy))
    curl_y = (hx - down_z(hx)) - (hz - h[2, p - 1])
    curl_z = (hy - h[1, p - 1]) - (hx - down_y(hx))
    return curl_x, curl_y, curl_z


def h_factor(place, size_y, rows, depth):
    row = lax.broadcasted_iota(jnp.int32, (rows, depth), 0)
    above, below = jnp.where(place.has(0, 1), 1.0, 0.0), jnp.where(place.has(0, -1), 1.0, 0.0)
    return time_step * jnp.where(row < size_y, 1.0, jnp.where(row < size_y + 4, above, below))


def row_copies(dn_put, up_put, up_got, lo_got, size_x):
    first, last, low, high = pl.ds(0, 2), pl.ds(size_x - 2, 2), pl.ds(0, 2), pl.ds(size_x + 2, 2)
    whole = pl.ds(2, size_x)
    return [
        (dn_put.at[:, first], up_got.at[:, high], -1, -1),
        (dn_put.at[:, last], up_got.at[:, low], 1, -1),
        (up_put.at[:, first], lo_got.at[:, high], -1, 1),
        (up_put.at[:, last], lo_got.at[:, low], 1, 1),
        (dn_put, up_got.at[:, whole], 0, -1),
        (up_put, lo_got.at[:, whole], 0, 1),
    ]


def plane_copies(array, count, size_x, size_y):
    lead = (slice(None),) * (len(array.shape) - 3)
    rows = pl.ds(0, size_y)

    def part(start):
        return array.at[(*lead, pl.ds(start, count), rows)]

    return [
        (part(2), part(size_x + 2), -1, 0),
        (part(size_x + 2 - count), part(2 - count), 1, 0),
    ]


FIELD_DOWN = ((0, 0, 0), (0, 1, 0), (0, 2, 0), (0, 0, 1), (0, 2, 1))
FIELD_UP = tuple((0, c, r) for c in range(3) for r in range(2))
ROUTE_DOWN = (*FIELD_DOWN, (1, 0, 0), (1, 1, 0), (1, 2, 0), (2, 0, 0), (3, 0, 0))
ROUTE_UP = (*FIELD_UP, (1, 0, 0), (1, 2, 0), (1, 0, 1), (1, 1, 1), (1, 2, 1), (2, 0, 1), (3, 0, 1))
SHARE_DOWN = (*FIELD_DOWN, (1, 0, 0), (1, 2, 0))
SHARE_UP = (*FIELD_UP, (1, 0, 1), (1, 1, 1), (1, 2, 1))


def halo_scratch(down, up, size_x, depth):
    shapes = [(len(down), size_x), (len(up), size_x), (len(down), size_x + 4), (len(up), size_x + 4)]
    return [pltpu.VMEM((*shape, 1, depth), jnp.float32) for shape in shapes]


def halo_rows(array, c, p, down, up, up_got, lo_got, above, below, fill):
    def one(names, got, r, keep):
        if (array, c, r) not in names:
            return fill
        return jnp.where(keep, got[names.index((array, c, r)), p], fill)

    return jnp.concatenate(
        [one(down, up_got, 0, above), one(down, up_got, 1, above)]
        + [fill] * 4
        + [one(up, lo_got, 0, below), one(up, lo_got, 1, below)],
        axis=0,
    )


class Exchange:
    def __init__(self, place, parts, send, recv):
        self.parts = []
        for n, (a, b, dx, dy) in enumerate(parts):
            copy = pltpu.make_async_remote_copy(
                src_ref=a,
                dst_ref=b,
                send_sem=send.at[n],
                recv_sem=recv.at[n],
                device_id=place.other(dx, dy),
                device_id_type=MESH,
            )
            self.parts.append((copy, place.has(dx, dy), place.has(-dx, -dy)))
            pl.when(self.parts[-1][1])(copy.start)

    def wait(self):
        for copy, goes, comes in self.parts:
            pl.when(comes)(copy.wait_recv)
            pl.when(goes)(copy.wait_send)


def parts_of(state):
    return state.at[pl.ds(0, 3)], state.at[pl.ds(3, 3)], state.at[6], state.at[7]


def route_kernel(
    nx,
    ny,
    cells,
    data_in,
    tile_in,
    cell_in,
    comp_in,
    e_in,
    h_in,
    cond_in,
    perm_in,
    got_ref,
    code_ref,
    state,
    data_ref,
    tile_ref,
    cell_ref,
    comp_ref,
    first,
    mid,
    second,
    last,
    dn_put,
    up_put,
    up_got,
    lo_got,
    load,
    send_y,
    recv_y,
    send_x,
    recv_x,
    send,
    recv,
):
    place = Place(nx, ny)
    ix, iy = place.ix, place.iy
    e, h, decay, gain = parts_of(state)
    size_x, size_y, depth = cond_in.shape
    rows = size_y + 8
    inner = (pl.ds(2, size_x), pl.ds(0, size_y))
    pairs = (
        (tile_in, tile_ref),
        (cell_in, cell_ref),
        (comp_in, comp_ref),
        (data_in, data_ref),
        (e_in, e.at[:, inner[0], inner[1]]),
        (h_in, h.at[:, inner[0], inner[1]]),
        (cond_in, decay.at[inner[0], inner[1]]),
        (perm_in, gain.at[inner[0], inner[1]]),
    )
    loads = [pltpu.make_async_copy(a, b, load.at[n]) for n, (a, b) in enumerate(pairs)]
    for copy in loads:
        copy.start()
    barrier = pltpu.get_barrier_semaphore()
    for k in range(1, nx):
        pl.semaphore_signal(barrier, inc=1, device_id=(lax.rem(ix + k, nx), iy), device_id_type=MESH)
    for k in range(1, ny):
        pl.semaphore_signal(barrier, inc=1, device_id=(ix, lax.rem(iy + k, ny)), device_id_type=MESH)
    corners = greet(place, barrier, [o for o in AROUND if 0 not in o])
    for copy in loads[:4]:
        copy.wait()
    first[...] = pack(nx * ny, cells, data_ref, tile_ref, cell_ref, comp_ref)
    for copy in loads[4:]:
        copy.wait()

    def stage(x):
        p = x + 2
        arrays = ((e.at[0], e.at[1], e.at[2]), (h.at[0], h.at[1], h.at[2]), (decay,), (gain,))
        for n, (array, c, r) in enumerate(ROUTE_DOWN):
            dn_put[n, x] = arrays[array][c][p, r : r + 1, :]
        for n, (array, c, r) in enumerate(ROUTE_UP):
            up_put[n, x] = arrays[array][c][p, size_y - 2 + r : size_y - 1 + r, :]

    sweep(0, size_x, stage, 4)
    pl.semaphore_wait(barrier, corners + (nx + ny - 2))
    by_row = Exchange(
        place, row_copies(dn_put, up_put, up_got, lo_got, size_x), send.at[0], recv.at[0]
    )
    copies = []
    for k in range(1, nx):
        to = lax.rem(ix + k, nx)
        copy = pltpu.make_async_remote_copy(
            src_ref=first.at[pl.ds(pl.multiple_of(to * ny, ny), ny), :],
            dst_ref=mid.at[pl.ds(pl.multiple_of(ix * ny, ny), ny), :],
            send_sem=send_x.at[k - 1],
            recv_sem=recv_x.at[k - 1],
            device_id=(to, iy),
            device_id_type=MESH,
        )
        copy.start()
        copies.append(copy)
    by_plane = Exchange(
        place, plane_copies(state, 2, size_x, size_y), send.at[1], recv.at[1]
    )
    own = pl.ds(pl.multiple_of(ix * ny, ny), ny)
    mid[own, :] = first[own, :]
    for copy in copies:
        copy.wait_recv()
    for j in range(ny):
        second[j * nx : (j + 1) * nx, :] = mid[pl.ds(j, nx, stride=ny), :]
    later = []
    for k in range(1, ny):
        to = lax.rem(iy + k, ny)
        copy = pltpu.make_async_remote_copy(
            src_ref=second.at[pl.ds(pl.multiple_of(to * nx, nx), nx), :],
            dst_ref=last.at[pl.ds(pl.multiple_of(iy * nx, nx), nx), :],
            send_sem=send_y.at[k - 1],
            recv_sem=recv_y.at[k - 1],
            device_id=(ix, to),
            device_id_type=MESH,
        )
        copy.start()
        later.append(copy)
    own = pl.ds(pl.multiple_of(iy * nx, nx), nx)
    last[own, :] = second[own, :]
    for copy in copies:
        copy.wait_send()

    by_plane.wait()
    by_row.wait()
    for p in (0, 1, size_x + 2, size_x + 3):
        keep = place.plane(p, size_x)
        for c in range(3):
            for array in (e, h):
                array[c, p, :size_y] = jnp.where(keep, array[c, p, :size_y], 0.0)

    def unstage(p):
        keep = place.plane(p, size_x)
        above, below = jnp.logical_and(keep, place.has(0, 1)), jnp.logical_and(keep, place.has(0, -1))
        gap = jnp.zeros((1, depth), jnp.float32)
        for array, field in enumerate((e, h)):
            for c in range(3):
                field[c, p, size_y:] = halo_rows(
                    array, c, p, ROUTE_DOWN, ROUTE_UP, up_got, lo_got, above, below, gap
                )

    sweep(0, size_x + 4, unstage, 4)
    row = lax.broadcasted_iota(jnp.int32, (rows, depth), 0)
    inside = jnp.where(
        row < size_y,
        1.0,
        jnp.where(
            row == size_y,
            jnp.where(place.has(0, 1), 1.0, 0.0),
            jnp.where(row == rows - 1, jnp.where(place.has(0, -1), 1.0, 0.0), 0.0),
        ),
    )
    ones = jnp.ones((1, depth), jnp.float32)

    def coefficients(p):
        for array, field in ((2, decay), (3, gain)):
            field[p, size_y:] = halo_rows(array, 0, p, ROUTE_DOWN, ROUTE_UP, up_got, lo_got, True, True, ones)
        half_loss = decay[p] * (0.5 * time_step)
        eps = gain[p]
        inverse = 1.0 / (eps + half_loss)
        keep = inside > jnp.where(place.plane(p, size_x), 0.5, 1.5)
        decay[p] = jnp.where(keep, (eps - half_loss) * inverse, 0.0)
        gain[p] = jnp.where(keep, time_step * inverse, 0.0)

    sweep(1, size_x + 2, coefficients, 2)
    moves = shifts(rows, depth)
    factor = h_factor(place, size_y, rows, depth)

    def h_step(p):
        h_plane(e, h, h, p, factor * jnp.where(place.plane(p, size_x), 1.0, 0.0), moves)

    sweep(0, size_x + 3, h_step, 7)

    for copy in later:
        copy.wait()
    got_ref[...] = last[...]
    quarter = nx * ny // FIELDS
    lane = lax.broadcasted_iota(jnp.int32, (quarter, LANES), 1) // SPAN
    codes = jnp.zeros((quarter, LANES), jnp.int32)
    for k in range(FIELDS):
        code = last[pl.ds(k, quarter, stride=FIELDS), :].astype(jnp.int32)
        word = jnp.bitwise_and(code, LANES - 1) + jnp.bitwise_and(code, -LANES) * FIELDS
        codes = jnp.where(lane == k, pltpu.roll(word, (k + 1) * SPAN % LANES, 1), codes)
    code_ref[...] = codes


def in_vmem(count):
    return [pl.BlockSpec(memory_space=pltpu.VMEM)] * count


def f32(*shape):
    return jax.ShapeDtypeStruct(shape, jnp.float32)


def route(nx, ny, data, tile, cell, comp, e, h, cond, perm):
    devices = nx * ny
    size_x, size_y, depth = cond.shape
    wide, tall = size_x + 4, size_y + 8
    inputs = (data, tile, cell, comp, e, h, cond, perm)
    rows = lambda: pltpu.VMEM((devices, LANES), jnp.float32)
    return pl.pallas_call(
        functools.partial(route_kernel, nx, ny, size_x * size_y * depth),
        out_shape=[
            f32(devices, LANES),
            jax.ShapeDtypeStruct((devices // FIELDS, LANES), jnp.int32),
            f32(8, wide, tall, depth),
        ],
        in_specs=[pl.BlockSpec(memory_space=pltpu.HBM)] * 8,
        out_specs=in_vmem(3),
        scratch_shapes=[
            *(pltpu.VMEM(a.shape, a.dtype) for a in (data, tile, cell, comp)),
            rows(),
            rows(),
            rows(),
            rows(),
            *halo_scratch(ROUTE_DOWN, ROUTE_UP, size_x, depth),
            pltpu.SemaphoreType.DMA((8,)),
            pltpu.SemaphoreType.DMA((ny - 1,)),
            pltpu.SemaphoreType.DMA((ny - 1,)),
            pltpu.SemaphoreType.DMA((nx - 1,)),
            pltpu.SemaphoreType.DMA((nx - 1,)),
            pltpu.SemaphoreType.DMA((2, 8)),
            pltpu.SemaphoreType.DMA((2, 8)),
        ],
        compiler_params=pltpu.CompilerParams(
            collective_id=0, has_side_effects=True, vmem_limit_bytes=16 * MIB
        ),
        name="route",
    )(*(pltpu.with_memory_space_constraint(a, pltpu.HBM) for a in inputs))


def scatter_kernel(cap, code_in, got_ref, out_ref, code_ref, quad, terms, wide, sem):
    fetch = pltpu.make_async_copy(code_in, code_ref, sem)
    fetch.start()
    devices = got_ref.shape[0]
    got = got_ref[...]
    lane = lax.broadcasted_iota(jnp.int32, (devices, LANES), 1)
    slot = jnp.bitwise_and(lane, SPAN - 1)
    codes = jnp.where(lane >= (FIELDS - 1) * SPAN, got, 0.0)
    codes = codes + pltpu.roll(codes, SPAN, 1)
    codes = codes + pltpu.roll(codes, 2 * SPAN, 1)
    total = got
    place_in_group = slot - slot // GROUP * GROUP
    for d in range(1, GROUP):
        same = (codes == pltpu.roll(codes, d, 1)) & (place_in_group >= d)
        total = total + jnp.where(same, pltpu.roll(got, d, 1), 0.0)
    for t in range(FIELDS):
        quad[pl.ds(t, devices, stride=FIELDS), :] = jnp.where(
            (lane >= t * SPAN) & (lane < (t + 1) * SPAN), total, 0.0
        )
    values = quad[...]
    high = values.astype(jnp.bfloat16)
    low = (values - high.astype(jnp.float32)).astype(jnp.bfloat16)
    terms[:, :LANES] = high
    terms[:, LANES:] = low
    row_slot = jnp.bitwise_and(lax.broadcasted_iota(jnp.int32, (2 * LANES, 2 * LANES), 0), SPAN - 1)
    column = lax.broadcasted_iota(jnp.int32, (2 * LANES, 2 * LANES), 1) // LANES
    for i in range(0, cap, 2):
        both = mm(terms[...], (row_slot == column + i).astype(jnp.bfloat16))
        wide[i] = both[:, :LANES]
        wide[i + 1] = both[:, LANES:]
    step = 512

    def clear(n, _):
        out_ref[pl.ds(pl.multiple_of(n * step, step), step), :] = jnp.zeros((step, LANES), jnp.float32)
        return 0

    lax.fori_loop(0, out_ref.shape[0] // step, clear, 0)
    fetch.wait()
    depth = lax.broadcasted_iota(jnp.int32, (FIELDS, LANES), 1)

    def place(q, _):
        for p in range(FIELDS):
            s = q * FIELDS + p
            for start in range(0, cap, GROUP):
                where, news = [], []
                for i in range(start, min(cap, start + GROUP)):
                    word = code_ref[q, p * SPAN + i]
                    row = pl.ds(pl.multiple_of(lax.shift_right_logical(word, 7), FIELDS), FIELDS)
                    news.append(out_ref[row, :] + wide[i, pl.ds(pl.multiple_of(s * FIELDS, FIELDS), FIELDS), :])
                    column = jnp.bitwise_and(jnp.full((FIELDS, LANES), word, jnp.int32), LANES - 1)
                    where.append((row, depth == column))
                for (row, mask), new in zip(where, news):
                    pltpu.store(out_ref.at[row, :], new, mask=mask)
        return 0

    lax.fori_loop(0, devices // FIELDS, place, 0)


def scatter(cap, rows, codes, got):
    devices = got.shape[0]
    return pl.pallas_call(
        functools.partial(scatter_kernel, cap),
        out_shape=jax.ShapeDtypeStruct((rows * FIELDS, LANES), jnp.float32),
        in_specs=[pl.BlockSpec(memory_space=pltpu.VMEM)] * 2,
        out_specs=pl.BlockSpec(memory_space=pltpu.VMEM),
        scratch_shapes=[
            pltpu.SMEM(codes.shape, jnp.int32),
            pltpu.VMEM((devices * FIELDS, LANES), jnp.float32),
            pltpu.VMEM((devices * FIELDS, 2 * LANES), jnp.bfloat16),
            pltpu.VMEM((cap, devices * FIELDS, LANES), jnp.float32),
            pltpu.SemaphoreType.DMA,
        ],
        compiler_params=pltpu.CompilerParams(vmem_limit_bytes=24 * MIB),
        name="scatter",
    )(codes, got)


def share_kernel(
    nx, ny, state, src, fwd, both, grad, dn_put, up_put, up_got, lo_got, send, recv
):
    place = Place(nx, ny)
    e0, h1, decay, gain = parts_of(state)
    e, src1 = both.at[pl.ds(0, 3)], both.at[pl.ds(3, 3)]
    size_x, size_y, depth = grad.shape
    moves = shifts(size_y + 8, depth)
    barrier = pltpu.get_barrier_semaphore()
    others = greet(place, barrier, AROUND)

    def own(x):
        p = x + 2
        fade, rise = decay[p, :size_y], gain[p, :size_y]
        for c, curl in enumerate(curl_h(h1, p, moves)):
            source = src[c, x, pl.ds(0, size_y, stride=FIELDS), :]
            new = fade * e0[c, p, :size_y] + rise * (curl[:size_y] - source)
            e[c, p, :size_y] = new
            source = src[c, x, pl.ds(1, size_y, stride=FIELDS), :]
            src1[c, p, :size_y] = source
            for n, (array, comp, r) in enumerate(SHARE_DOWN):
                if comp == c:
                    dn_put[n, x] = (new, source)[array][r : r + 1]
            for n, (array, comp, r) in enumerate(SHARE_UP):
                if comp == c:
                    up_put[n, x] = (new, source)[array][size_y - 2 + r : size_y - 1 + r]

    sweep(0, size_x, own, 8)
    pl.semaphore_wait(barrier, others)
    halos = Exchange(
        place,
        row_copies(dn_put, up_put, up_got, lo_got, size_x)
        + plane_copies(both, 2, size_x, size_y),
        send,
        recv,
    )

    def product(x):
        total = fwd[0, 0, x].astype(jnp.float32) * e[0, x + 2, :size_y]
        for c in (1, 2):
            total = total + fwd[0, c, x].astype(jnp.float32) * e[c, x + 2, :size_y]
        grad[x] = total

    sweep(0, size_x, product, 4)
    halos.wait()
    for p in (0, 1, size_x + 2, size_x + 3):
        keep = place.plane(p, size_x)
        for c in range(3):
            e[c, p, :size_y] = jnp.where(keep, e[c, p, :size_y], 0.0)
            src1[c, p, :size_y] = jnp.where(keep, src1[c, p, :size_y], 0.0)

    def unstage(p):
        keep = place.plane(p, size_x)
        above, below = jnp.logical_and(keep, place.has(0, 1)), jnp.logical_and(keep, place.has(0, -1))
        gap = jnp.zeros((1, depth), jnp.float32)
        for array, field in enumerate((e, src1)):
            for c in range(3):
                field[c, p, size_y:] = halo_rows(
                    array, c, p, SHARE_DOWN, SHARE_UP, up_got, lo_got, above, below, gap
                )

    sweep(0, size_x + 4, unstage, 4)


def share(nx, ny, state, src, fwd):
    size_x, size_y, depth = fwd.shape[2:]
    wide, tall = size_x + 4, size_y + 8
    return pl.pallas_call(
        functools.partial(share_kernel, nx, ny),
        out_shape=[f32(6, wide, tall, depth), f32(size_x, size_y, depth)],
        in_specs=in_vmem(3),
        out_specs=in_vmem(2),
        scratch_shapes=[
            *halo_scratch(SHARE_DOWN, SHARE_UP, size_x, depth),
            pltpu.SemaphoreType.DMA((8,)),
            pltpu.SemaphoreType.DMA((8,)),
        ],
        compiler_params=pltpu.CompilerParams(
            collective_id=1, has_side_effects=True, vmem_limit_bytes=6 * MIB
        ),
        name="share",
    )(state, src, fwd)


def finish_kernel(
    nx, ny, both, state, src, fwd, grad1, e_out, h_out, grad_out, e, h, grad, sem
):
    place = Place(nx, ny)
    e1, src1 = both.at[pl.ds(0, 3)], both.at[pl.ds(3, 3)]
    _, h1, decay, gain = parts_of(state)
    size_x, size_y, depth = grad1.shape
    rows = size_y + 8
    moves = shifts(rows, depth)
    factor = h_factor(place, size_y, rows, depth)

    def h_second(p):
        h_plane(e1, h1, h, p, factor * jnp.where(place.plane(p, size_x), 1.0, 0.0), moves)

    sweep(0, size_x + 3, h_second, 7)

    def e_second(p, inner):
        fade, rise = decay[p], gain[p]
        total = None
        for c, curl in enumerate(curl_h(h, p, moves)):
            new = fade * e1[c, p] + rise * (curl - src1[c, p])
            e[c, p] = new
            if inner:
                term = fwd[1, c, p - 2].astype(jnp.float32) * new[:size_y]
                total = term if total is None else total + term
        if inner:
            grad[p - 2] = grad1[p - 2] + total

    e_second(1, False)

    def e_inner(p):
        e_second(p, True)

    sweep(2, size_x, e_inner, 8)
    e_second(size_x + 2, False)

    def h_third(p):
        h_plane(e, h, h, p, factor * jnp.where(place.plane(p, size_x), 1.0, 0.0), moves)

    sweep(1, size_x + 1, h_third, 11)
    inside = pl.ds(0, size_y)
    h_copy = pltpu.make_async_copy(h.at[:, pl.ds(2, size_x), inside], h_out, sem.at[0])
    h_copy.start()

    def e_third(x):
        p = x + 2
        fade, rise = decay[p, :size_y], gain[p, :size_y]
        total = grad[x]
        for c, curl in enumerate(curl_h(h, p, moves)):
            source = src[c, x, pl.ds(2, size_y, stride=FIELDS), :]
            new = fade * e[c, p, :size_y] + rise * (curl[:size_y] - source)
            e[c, p, :size_y] = new
            total = total + fwd[2, c, x].astype(jnp.float32) * new
        grad[x] = total

    each = size_x // PARTS

    def results(k):
        here = pl.ds(k * each, each)
        return (
            pltpu.make_async_copy(e.at[:, pl.ds(2 + k * each, each), inside], e_out.at[:, here], sem.at[1 + 2 * k]),
            pltpu.make_async_copy(grad.at[here], grad_out.at[here], sem.at[2 + 2 * k]),
        )

    def part(k, _):
        for x in range(each):
            e_third(k * each + x)
        for copy in results(k):
            copy.start()
        return 0

    lax.fori_loop(0, PARTS, part, 0)
    h_copy.wait()
    for k in range(PARTS):
        for copy in results(k):
            copy.wait()


def finish(nx, ny, both, state, src, fwd, grad1):
    size_x, size_y, depth = grad1.shape
    field = f32(3, size_x, size_y, depth)
    return pl.pallas_call(
        functools.partial(finish_kernel, nx, ny),
        out_shape=[field, field, f32(size_x, size_y, depth)],
        in_specs=in_vmem(5),
        out_specs=[pl.BlockSpec(memory_space=pltpu.HBM)] * 3,
        scratch_shapes=[
            pltpu.VMEM((3, *both.shape[1:]), jnp.float32),
            pltpu.VMEM((3, *both.shape[1:]), jnp.float32),
            pltpu.VMEM(grad1.shape, jnp.float32),
            pltpu.SemaphoreType.DMA((1 + 2 * PARTS,)),
        ],
        compiler_params=pltpu.CompilerParams(vmem_limit_bytes=10 * MIB),
        name="finish",
    )(both, state, src, fwd, grad1)


def per_device(
    e_adjoint,
    h_adjoint,
    conductivity,
    permittivity,
    forward_e,
    receiver_data,
    receiver_tile,
    receiver_cell,
    receiver_comp,
):
    _, size_x, size_y, depth = e_adjoint.shape
    nx, ny = lax.axis_size("gx"), lax.axis_size("gy")
    receivers = receiver_data.shape[0]
    cap = 3 * receivers // (nx * ny)
    by_lane = lambda a: a.reshape(receivers // LANES, LANES)
    got, codes, state = route(
        nx,
        ny,
        receiver_data,
        by_lane(receiver_tile),
        by_lane(receiver_cell),
        by_lane(receiver_comp),
        e_adjoint,
        h_adjoint,
        conductivity,
        permittivity,
    )
    placed = scatter(cap, 3 * size_x * size_y, codes, got)
    placed = placed.reshape(3, size_x, size_y * FIELDS, depth)
    both, grad1 = share(nx, ny, state, placed, forward_e)
    return tuple(finish(nx, ny, both, state, placed, forward_e, grad1))


def solution(mesh):
    placed = (
        P(None, "gx", "gy", None),
        P(None, "gx", "gy", None),
        P("gx", "gy", None),
        P("gx", "gy", None),
        P(None, None, "gx", "gy", None),
        P(("gx", "gy"), None),
        P(("gx", "gy"), None),
        P(("gx", "gy")),
        P(("gx", "gy")),
    )
    return jax.shard_map(
        per_device,
        mesh=mesh,
        in_specs=placed,
        out_specs=(P(None, "gx", "gy", None), P(None, "gx", "gy", None), P("gx", "gy", None)),
        check_vma=False,
    )
```

```python
import functools

import jax
import jax.numpy as jnp
from jax import lax
from jax.experimental import pallas as pl
from jax.experimental.pallas import tpu as pltpu
from jax.sharding import PartitionSpec as P

STEPS = 3
SAMPLES = 128
LANES = 128
FIELDS = 4
SPAN = LANES // FIELDS
MESH = pl.DeviceIdType.MESH
GROUP = 8
PARTS = 4
MIB = 1 << 20

time_step = 0.55


def split3(x):
    a = x.astype(jnp.bfloat16)
    rest = x - a.astype(jnp.float32)
    b = rest.astype(jnp.bfloat16)
    c = (rest - b.astype(jnp.float32)).astype(jnp.bfloat16)
    return a, b, c


def mm(a, b, contract=((1,), (0,))):
    return lax.dot_general(a, b, (contract, ((), ())), preferred_element_type=jnp.float32)


def time_kernel():
    shape = (SAMPLES, LANES)
    sample = lax.broadcasted_iota(jnp.int32, shape, 0).astype(jnp.float32)
    field = lax.broadcasted_iota(jnp.int32, shape, 1) // SPAN
    centre = (field.astype(jnp.float32) + 0.5) * (SAMPLES / STEPS)
    spread = SAMPLES / (4.0 * STEPS)
    kernel = jnp.exp(-jnp.square((sample - centre) / spread))
    norm = jnp.sum(kernel * kernel, axis=0, keepdims=True)
    return jnp.where(field < STEPS, kernel / jnp.sqrt(norm), 0.0)


def pack(devices, cells, data_ref, tile_ref, cell_ref, comp_ref):
    blocks, width = tile_ref.shape
    kernel = time_kernel()
    at, to = (lax.broadcasted_iota(jnp.int32, (width, width), n) for n in (0, 1))
    before = (at < to).astype(jnp.bfloat16)
    every = jnp.ones((width, width), jnp.bfloat16)
    diagonal = at == to
    destination = lax.broadcasted_iota(jnp.int32, (devices, width), 0)
    lane = lax.broadcasted_iota(jnp.int32, (width, LANES), 1)
    slot = jnp.bitwise_and(lane, SPAN - 1).astype(jnp.float32)
    is_code = lane >= STEPS * SPAN
    down = jnp.ones((width, LANES), jnp.bfloat16)
    seen = jnp.zeros((devices, width), jnp.float32)
    packed = jnp.zeros((devices, LANES), jnp.float32)

    def column(row):
        return jnp.where(diagonal, row.astype(jnp.float32), 0.0).astype(jnp.bfloat16)

    for b in range(blocks):
        onehot = (destination == tile_ref[b : b + 1, :]).astype(jnp.float32)
        hot = onehot.astype(jnp.bfloat16)
        rank = jnp.sum(onehot * (seen + mm(hot, before)), axis=0, keepdims=True)
        seen = seen + mm(hot, every)
        amplitude = lax.dot_general(
            data_ref[b * width : (b + 1) * width, :],
            kernel,
            (((1,), (0,)), ((), ())),
            precision=lax.Precision.HIGHEST,
            preferred_element_type=jnp.float32,
        )
        code = comp_ref[b : b + 1, :] * cells + cell_ref[b : b + 1, :]
        low = jnp.bitwise_and(code, 255)
        middle = jnp.bitwise_and(code, 255 << 8)
        high = code - low - middle
        codes = mm(column(low), down) + mm(column(middle), down) + mm(column(high), down)
        spread = jnp.where(
            slot == mm(column(rank), down), jnp.where(is_code, codes, amplitude), 0.0
        )
        for term in split3(spread):
            packed = packed + mm(hot, term)
    return packed


def sweep(start, count, body, width):
    def several(n, _):
        for k in range(width):
            body(start + n * width + k)
        return 0

    turns = count // width
    lax.fori_loop(0, turns, several, 0)
    for p in range(turns * width, count):
        body(start + p)


class Place:
    def __init__(self, nx, ny):
        self.nx, self.ny = nx, ny
        self.ix, self.iy = lax.axis_index("gx"), lax.axis_index("gy")
        self.inside_x = {-1: self.ix > 0, 0: None, 1: self.ix < nx - 1}
        self.inside_y = {-1: self.iy > 0, 0: None, 1: self.iy < ny - 1}

    def other(self, dx, dy):
        return lax.rem(self.ix + dx + self.nx, self.nx), lax.rem(self.iy + dy + self.ny, self.ny)

    def has(self, dx, dy):
        x, y = self.inside_x[dx], self.inside_y[dy]
        if x is None or y is None:
            return y if x is None else x
        return jnp.logical_and(x, y)

    def plane(self, p, size_x):
        low, high = jnp.logical_or(p >= 2, self.ix > 0), jnp.logical_or(p < size_x + 2, self.ix < self.nx - 1)
        return jnp.logical_and(low, high)


AROUND = tuple((dx, dy) for dx in (-1, 0, 1) for dy in (-1, 0, 1) if (dx, dy) != (0, 0))


def greet(place, barrier, offsets):
    count = jnp.int32(0)
    for dx, dy in offsets:
        here = place.has(dx, dy)
        count = count + here.astype(jnp.int32)

        @pl.when(here)
        def _(dx=dx, dy=dy):
            pl.semaphore_signal(barrier, inc=1, device_id=place.other(dx, dy), device_id_type=MESH)

    return count


def shifts(rows, depth):
    lane = lax.broadcasted_iota(jnp.int32, (rows, depth), 1)

    def up_z(f):
        return jnp.where(lane == depth - 1, 0.0, pltpu.roll(f, depth - 1, 1))

    def down_z(f):
        return jnp.where(lane == 0, 0.0, pltpu.roll(f, 1, 1))

    def up_y(f):
        return pltpu.roll(f, rows - 1, 0)

    def down_y(f):
        return pltpu.roll(f, 1, 0)

    return up_z, down_z, up_y, down_y


def h_plane(e, h_from, h_to, p, factor, moves):
    up_z, _, up_y, _ = moves
    ex, ey, ez = e[0, p], e[1, p], e[2, p]
    curl_x = (up_y(ez) - ez) - (up_z(ey) - ey)
    curl_y = (up_z(ex) - ex) - (e[2, p + 1] - ez)
    curl_z = (e[1, p + 1] - ey) - (up_y(ex) - ex)
    for c, curl in enumerate((curl_x, curl_y, curl_z)):
        h_to[c, p] = h_from[c, p] - factor * curl


def h_rows(e, h, p, rows, factor, up_z, up_y):
    ex, ey, ez = (e[c, p, rows] for c in range(3))
    curl_x = (up_y(2, ez) - ez) - (up_z(ey) - ey)
    curl_y = (up_z(ex) - ex) - (e[2, p + 1, rows] - ez)
    curl_z = (e[1, p + 1, rows] - ey) - (up_y(0, ex) - ex)
    return [h[c, p, rows] - factor * curl for c, curl in enumerate((curl_x, curl_y, curl_z))]


def curl_h(h, p, moves):
    _, down_z, _, down_y = moves
    hx, hy, hz = h[0, p], h[1, p], h[2, p]
    curl_x = (hz - down_y(hz)) - (hy - down_z(hy))
    curl_y = (hx - down_z(hx)) - (hz - h[2, p - 1])
    curl_z = (hy - h[1, p - 1]) - (hx - down_y(hx))
    return curl_x, curl_y, curl_z


def h_factor(place, size_y, rows, depth):
    row = lax.broadcasted_iota(jnp.int32, (rows, depth), 0)
    above, below = jnp.where(place.has(0, 1), 1.0, 0.0), jnp.where(place.has(0, -1), 1.0, 0.0)
    return time_step * jnp.where(row < size_y, 1.0, jnp.where(row < size_y + 4, above, below))


def row_copies(dn_put, up_put, up_got, lo_got, size_x):
    first, last, low, high = pl.ds(0, 2), pl.ds(size_x - 2, 2), pl.ds(0, 2), pl.ds(size_x + 2, 2)
    whole = pl.ds(2, size_x)
    return [
        (dn_put.at[:, first], up_got.at[:, high], -1, -1),
        (dn_put.at[:, last], up_got.at[:, low], 1, -1),
        (up_put.at[:, first], lo_got.at[:, high], -1, 1),
        (up_put.at[:, last], lo_got.at[:, low], 1, 1),
        (dn_put, up_got.at[:, whole], 0, -1),
        (up_put, lo_got.at[:, whole], 0, 1),
    ]


def plane_copies(array, count, size_x, size_y):
    lead = (slice(None),) * (len(array.shape) - 3)
    rows = pl.ds(0, size_y)

    def part(start):
        return array.at[(*lead, pl.ds(start, count), rows)]

    return [
        (part(2), part(size_x + 2), -1, 0),
        (part(size_x + 2 - count), part(2 - count), 1, 0),
    ]


FIELD_DOWN = ((0, 0, 0), (0, 1, 0), (0, 2, 0), (0, 0, 1), (0, 2, 1))
FIELD_UP = tuple((0, c, r) for c in range(3) for r in range(2))
ROUTE_DOWN = (*FIELD_DOWN, (1, 0, 0), (1, 1, 0), (1, 2, 0), (2, 0, 0), (3, 0, 0))
ROUTE_UP = (*FIELD_UP, (1, 0, 0), (1, 2, 0), (1, 0, 1), (1, 1, 1), (1, 2, 1), (2, 0, 1), (3, 0, 1))
SHARE_DOWN = (*FIELD_DOWN, (1, 0, 0), (1, 2, 0))
SHARE_UP = (*FIELD_UP, (1, 0, 1), (1, 1, 1), (1, 2, 1))


def halo_scratch(down, up, size_x, depth):
    shapes = [(len(down), size_x), (len(up), size_x), (len(down), size_x + 4), (len(up), size_x + 4)]
    return [pltpu.VMEM((*shape, 1, depth), jnp.float32) for shape in shapes]


def halo_rows(array, c, p, down, up, up_got, lo_got, above, below, fill):
    def one(names, got, r, keep):
        if (array, c, r) not in names:
            return fill
        return jnp.where(keep, got[names.index((array, c, r)), p], fill)

    return jnp.concatenate(
        [one(down, up_got, 0, above), one(down, up_got, 1, above)]
        + [fill] * 4
        + [one(up, lo_got, 0, below), one(up, lo_got, 1, below)],
        axis=0,
    )


class Exchange:
    def __init__(self, place, parts, send, recv):
        self.parts = []
        for n, (a, b, dx, dy) in enumerate(parts):
            copy = pltpu.make_async_remote_copy(
                src_ref=a,
                dst_ref=b,
                send_sem=send.at[n],
                recv_sem=recv.at[n],
                device_id=place.other(dx, dy),
                device_id_type=MESH,
            )
            self.parts.append((copy, place.has(dx, dy), place.has(-dx, -dy)))
            pl.when(self.parts[-1][1])(copy.start)

    def wait(self):
        for copy, goes, comes in self.parts:
            pl.when(comes)(copy.wait_recv)
            pl.when(goes)(copy.wait_send)


def parts_of(state):
    return state.at[pl.ds(0, 3)], state.at[pl.ds(3, 3)], state.at[6], state.at[7]


def route_kernel(
    nx,
    ny,
    cells,
    data_in,
    tile_in,
    cell_in,
    comp_in,
    e_in,
    h_in,
    cond_in,
    perm_in,
    got_ref,
    code_ref,
    state,
    data_ref,
    tile_ref,
    cell_ref,
    comp_ref,
    first,
    mid,
    second,
    last,
    dn_put,
    up_put,
    up_got,
    lo_got,
    load,
    send_y,
    recv_y,
    send_x,
    recv_x,
    send,
    recv,
):
    place = Place(nx, ny)
    ix, iy = place.ix, place.iy
    e, h, decay, gain = parts_of(state)
    size_x, size_y, depth = cond_in.shape
    rows = size_y + 8
    inner = (pl.ds(2, size_x), pl.ds(0, size_y))
    pairs = (
        (tile_in, tile_ref),
        (cell_in, cell_ref),
        (comp_in, comp_ref),
        (data_in, data_ref),
        (e_in, e.at[:, inner[0], inner[1]]),
        (h_in, h.at[:, inner[0], inner[1]]),
        (cond_in, decay.at[inner[0], inner[1]]),
        (perm_in, gain.at[inner[0], inner[1]]),
    )
    loads = [pltpu.make_async_copy(a, b, load.at[n]) for n, (a, b) in enumerate(pairs)]
    for copy in loads:
        copy.start()
    barrier = pltpu.get_barrier_semaphore()
    for k in range(1, nx):
        pl.semaphore_signal(barrier, inc=1, device_id=(lax.rem(ix + k, nx), iy), device_id_type=MESH)
    for k in range(1, ny):
        pl.semaphore_signal(barrier, inc=1, device_id=(ix, lax.rem(iy + k, ny)), device_id_type=MESH)
    corners = greet(place, barrier, [o for o in AROUND if 0 not in o])
    for copy in loads[:4]:
        copy.wait()
    first[...] = pack(nx * ny, cells, data_ref, tile_ref, cell_ref, comp_ref)
    for copy in loads[4:]:
        copy.wait()

    def stage(x):
        p = x + 2
        arrays = ((e.at[0], e.at[1], e.at[2]), (h.at[0], h.at[1], h.at[2]), (decay,), (gain,))
        for n, (array, c, r) in enumerate(ROUTE_DOWN):
            dn_put[n, x] = arrays[array][c][p, r : r + 1, :]
        for n, (array, c, r) in enumerate(ROUTE_UP):
            up_put[n, x] = arrays[array][c][p, size_y - 2 + r : size_y - 1 + r, :]

    sweep(0, size_x, stage, 4)
    pl.semaphore_wait(barrier, corners + (nx + ny - 2))
    by_row = Exchange(
        place, row_copies(dn_put, up_put, up_got, lo_got, size_x), send.at[0], recv.at[0]
    )
    copies = []
    for k in range(1, nx):
        to = lax.rem(ix + k, nx)
        copy = pltpu.make_async_remote_copy(
            src_ref=first.at[pl.ds(pl.multiple_of(to * ny, ny), ny), :],
            dst_ref=mid.at[pl.ds(pl.multiple_of(ix * ny, ny), ny), :],
            send_sem=send_x.at[k - 1],
            recv_sem=recv_x.at[k - 1],
            device_id=(to, iy),
            device_id_type=MESH,
        )
        copy.start()
        copies.append(copy)
    by_plane = Exchange(
        place, plane_copies(state, 2, size_x, size_y), send.at[1], recv.at[1]
    )
    own = pl.ds(pl.multiple_of(ix * ny, ny), ny)
    mid[own, :] = first[own, :]
    for copy in copies:
        copy.wait_recv()
    for j in range(ny):
        second[j * nx : (j + 1) * nx, :] = mid[pl.ds(j, nx, stride=ny), :]
    later = []
    for k in range(1, ny):
        to = lax.rem(iy + k, ny)
        copy = pltpu.make_async_remote_copy(
            src_ref=second.at[pl.ds(pl.multiple_of(to * nx, nx), nx), :],
            dst_ref=last.at[pl.ds(pl.multiple_of(iy * nx, nx), nx), :],
            send_sem=send_y.at[k - 1],
            recv_sem=recv_y.at[k - 1],
            device_id=(ix, to),
            device_id_type=MESH,
        )
        copy.start()
        later.append(copy)
    own = pl.ds(pl.multiple_of(iy * nx, nx), nx)
    last[own, :] = second[own, :]
    for copy in copies:
        copy.wait_send()

    by_plane.wait()
    by_row.wait()
    for p in (0, 1, size_x + 2, size_x + 3):
        keep = place.plane(p, size_x)
        for c in range(3):
            for array in (e, h):
                array[c, p, :size_y] = jnp.where(keep, array[c, p, :size_y], 0.0)

    def unstage(p):
        keep = place.plane(p, size_x)
        above, below = jnp.logical_and(keep, place.has(0, 1)), jnp.logical_and(keep, place.has(0, -1))
        gap = jnp.zeros((1, depth), jnp.float32)
        for array, field in enumerate((e, h)):
            for c in range(3):
                field[c, p, size_y:] = halo_rows(
                    array, c, p, ROUTE_DOWN, ROUTE_UP, up_got, lo_got, above, below, gap
                )

    sweep(0, size_x + 4, unstage, 4)
    row = lax.broadcasted_iota(jnp.int32, (rows, depth), 0)
    inside = jnp.where(
        row < size_y,
        1.0,
        jnp.where(
            row == size_y,
            jnp.where(place.has(0, 1), 1.0, 0.0),
            jnp.where(row == rows - 1, jnp.where(place.has(0, -1), 1.0, 0.0), 0.0),
        ),
    )
    ones = jnp.ones((1, depth), jnp.float32)

    def coefficients(p):
        for array, field in ((2, decay), (3, gain)):
            field[p, size_y:] = halo_rows(array, 0, p, ROUTE_DOWN, ROUTE_UP, up_got, lo_got, True, True, ones)
        half_loss = decay[p] * (0.5 * time_step)
        eps = gain[p]
        inverse = 1.0 / (eps + half_loss)
        keep = inside > jnp.where(place.plane(p, size_x), 0.5, 1.5)
        decay[p] = jnp.where(keep, (eps - half_loss) * inverse, 0.0)
        gain[p] = jnp.where(keep, time_step * inverse, 0.0)

    sweep(1, size_x + 2, coefficients, 2)
    moves = shifts(rows, depth)
    factor = h_factor(place, size_y, rows, depth)

    def h_step(p):
        h_plane(e, h, h, p, factor * jnp.where(place.plane(p, size_x), 1.0, 0.0), moves)

    sweep(0, size_x + 3, h_step, 7)

    for copy in later:
        copy.wait()
    got_ref[...] = last[...]
    quarter = nx * ny // FIELDS
    lane = lax.broadcasted_iota(jnp.int32, (quarter, LANES), 1) // SPAN
    codes = jnp.zeros((quarter, LANES), jnp.int32)
    for k in range(FIELDS):
        code = last[pl.ds(k, quarter, stride=FIELDS), :].astype(jnp.int32)
        word = jnp.bitwise_and(code, LANES - 1) + jnp.bitwise_and(code, -LANES) * FIELDS
        codes = jnp.where(lane == k, pltpu.roll(word, (k + 1) * SPAN % LANES, 1), codes)
    code_ref[...] = codes


def in_vmem(count):
    return [pl.BlockSpec(memory_space=pltpu.VMEM)] * count


def f32(*shape):
    return jax.ShapeDtypeStruct(shape, jnp.float32)


def route(nx, ny, data, tile, cell, comp, e, h, cond, perm):
    devices = nx * ny
    size_x, size_y, depth = cond.shape
    wide, tall = size_x + 4, size_y + 8
    inputs = (data, tile, cell, comp, e, h, cond, perm)
    rows = lambda: pltpu.VMEM((devices, LANES), jnp.float32)
    return pl.pallas_call(
        functools.partial(route_kernel, nx, ny, size_x * size_y * depth),
        out_shape=[
            f32(devices, LANES),
            jax.ShapeDtypeStruct((devices // FIELDS, LANES), jnp.int32),
            f32(8, wide, tall, depth),
        ],
        in_specs=[pl.BlockSpec(memory_space=pltpu.HBM)] * 8,
        out_specs=in_vmem(3),
        scratch_shapes=[
            *(pltpu.VMEM(a.shape, a.dtype) for a in (data, tile, cell, comp)),
            rows(),
            rows(),
            rows(),
            rows(),
            *halo_scratch(ROUTE_DOWN, ROUTE_UP, size_x, depth),
            pltpu.SemaphoreType.DMA((8,)),
            pltpu.SemaphoreType.DMA((ny - 1,)),
            pltpu.SemaphoreType.DMA((ny - 1,)),
            pltpu.SemaphoreType.DMA((nx - 1,)),
            pltpu.SemaphoreType.DMA((nx - 1,)),
            pltpu.SemaphoreType.DMA((2, 8)),
            pltpu.SemaphoreType.DMA((2, 8)),
        ],
        compiler_params=pltpu.CompilerParams(
            collective_id=0, has_side_effects=True, vmem_limit_bytes=16 * MIB
        ),
        name="route",
    )(*(pltpu.with_memory_space_constraint(a, pltpu.HBM) for a in inputs))


def scatter_kernel(cap, code_in, got_ref, out_ref, code_ref, quad, terms, wide, sem):
    fetch = pltpu.make_async_copy(code_in, code_ref, sem)
    fetch.start()
    devices = got_ref.shape[0]
    got = got_ref[...]
    lane = lax.broadcasted_iota(jnp.int32, (devices, LANES), 1)
    slot = jnp.bitwise_and(lane, SPAN - 1)
    codes = jnp.where(lane >= (FIELDS - 1) * SPAN, got, 0.0)
    codes = codes + pltpu.roll(codes, SPAN, 1)
    codes = codes + pltpu.roll(codes, 2 * SPAN, 1)
    total = got
    place_in_group = slot - slot // GROUP * GROUP
    for d in range(1, GROUP):
        same = (codes == pltpu.roll(codes, d, 1)) & (place_in_group >= d)
        total = total + jnp.where(same, pltpu.roll(got, d, 1), 0.0)
    for t in range(FIELDS):
        quad[pl.ds(t, devices, stride=FIELDS), :] = jnp.where(
            (lane >= t * SPAN) & (lane < (t + 1) * SPAN), total, 0.0
        )
    values = quad[...]
    high = values.astype(jnp.bfloat16)
    low = (values - high.astype(jnp.float32)).astype(jnp.bfloat16)
    terms[:, :LANES] = high
    terms[:, LANES:] = low
    row_slot = jnp.bitwise_and(lax.broadcasted_iota(jnp.int32, (2 * LANES, 2 * LANES), 0), SPAN - 1)
    column = lax.broadcasted_iota(jnp.int32, (2 * LANES, 2 * LANES), 1) // LANES
    for i in range(0, cap, 2):
        both = mm(terms[...], (row_slot == column + i).astype(jnp.bfloat16))
        wide[i] = both[:, :LANES]
        wide[i + 1] = both[:, LANES:]
    step = 512

    def clear(n, _):
        out_ref[pl.ds(pl.multiple_of(n * step, step), step), :] = jnp.zeros((step, LANES), jnp.float32)
        return 0

    lax.fori_loop(0, out_ref.shape[0] // step, clear, 0)
    fetch.wait()
    depth = lax.broadcasted_iota(jnp.int32, (FIELDS, LANES), 1)

    def place(q, _):
        for p in range(FIELDS):
            s = q * FIELDS + p
            for start in range(0, cap, GROUP):
                where, news = [], []
                for i in range(start, min(cap, start + GROUP)):
                    word = code_ref[q, p * SPAN + i]
                    row = pl.ds(pl.multiple_of(lax.shift_right_logical(word, 7), FIELDS), FIELDS)
                    news.append(out_ref[row, :] + wide[i, pl.ds(pl.multiple_of(s * FIELDS, FIELDS), FIELDS), :])
                    column = jnp.bitwise_and(jnp.full((FIELDS, LANES), word, jnp.int32), LANES - 1)
                    where.append((row, depth == column))
                for (row, mask), new in zip(where, news):
                    pltpu.store(out_ref.at[row, :], new, mask=mask)
        return 0

    lax.fori_loop(0, devices // FIELDS, place, 0)


def scatter(cap, rows, codes, got):
    devices = got.shape[0]
    return pl.pallas_call(
        functools.partial(scatter_kernel, cap),
        out_shape=jax.ShapeDtypeStruct((rows * FIELDS, LANES), jnp.float32),
        in_specs=[pl.BlockSpec(memory_space=pltpu.VMEM)] * 2,
        out_specs=pl.BlockSpec(memory_space=pltpu.VMEM),
        scratch_shapes=[
            pltpu.SMEM(codes.shape, jnp.int32),
            pltpu.VMEM((devices * FIELDS, LANES), jnp.float32),
            pltpu.VMEM((devices * FIELDS, 2 * LANES), jnp.bfloat16),
            pltpu.VMEM((cap, devices * FIELDS, LANES), jnp.float32),
            pltpu.SemaphoreType.DMA,
        ],
        compiler_params=pltpu.CompilerParams(vmem_limit_bytes=24 * MIB),
        name="scatter",
    )(codes, got)


def share_kernel(
    nx, ny, state, src, fwd, both, grad, h_low, dn_put, up_put, up_got, lo_got, send, recv
):
    place = Place(nx, ny)
    e0, h1, decay, gain = parts_of(state)
    e, src1 = both.at[pl.ds(0, 3)], both.at[pl.ds(3, 3)]
    size_x, size_y, depth = grad.shape
    moves = shifts(size_y + 8, depth)
    barrier = pltpu.get_barrier_semaphore()
    others = greet(place, barrier, AROUND)

    def own(x):
        p = x + 2
        fade, rise = decay[p, :size_y], gain[p, :size_y]
        for c, curl in enumerate(curl_h(h1, p, moves)):
            source = src[c, x, pl.ds(0, size_y, stride=FIELDS), :]
            new = fade * e0[c, p, :size_y] + rise * (curl[:size_y] - source)
            e[c, p, :size_y] = new
            source = src[c, x, pl.ds(1, size_y, stride=FIELDS), :]
            src1[c, p, :size_y] = source
            for n, (array, comp, r) in enumerate(SHARE_DOWN):
                if comp == c:
                    dn_put[n, x] = (new, source)[array][r : r + 1]
            for n, (array, comp, r) in enumerate(SHARE_UP):
                if comp == c:
                    up_put[n, x] = (new, source)[array][size_y - 2 + r : size_y - 1 + r]

    sweep(0, size_x, own, 8)
    pl.semaphore_wait(barrier, others)
    halos = Exchange(
        place,
        row_copies(dn_put, up_put, up_got, lo_got, size_x)
        + plane_copies(both, 2, size_x, size_y),
        send,
        recv,
    )

    def product(x):
        total = fwd[0, 0, x].astype(jnp.float32) * e[0, x + 2, :size_y]
        for c in (1, 2):
            total = total + fwd[0, c, x].astype(jnp.float32) * e[c, x + 2, :size_y]
        grad[x] = total

    sweep(0, size_x, product, 4)

    low = h_low.shape[2]
    up_z, _, up_y, _ = shifts(size_y, depth)

    def h_second(x):
        new = h_rows(e, h1, x + 2, slice(0, size_y), time_step, up_z, lambda c, f: up_y(f))
        for c in range(3):
            h_low[c, x] = new[c][:low]

    sweep(0, size_x - 2, h_second, 6)
    halos.wait()
    for p in (0, 1, size_x + 2, size_x + 3):
        keep = place.plane(p, size_x)
        for c in range(3):
            e[c, p, :size_y] = jnp.where(keep, e[c, p, :size_y], 0.0)
            src1[c, p, :size_y] = jnp.where(keep, src1[c, p, :size_y], 0.0)

    def unstage(p):
        keep = place.plane(p, size_x)
        above, below = jnp.logical_and(keep, place.has(0, 1)), jnp.logical_and(keep, place.has(0, -1))
        gap = jnp.zeros((1, depth), jnp.float32)
        for array, field in enumerate((e, src1)):
            for c in range(3):
                field[c, p, size_y:] = halo_rows(
                    array, c, p, SHARE_DOWN, SHARE_UP, up_got, lo_got, above, below, gap
                )

    sweep(0, size_x + 4, unstage, 4)


def share(nx, ny, state, src, fwd):
    size_x, size_y, depth = fwd.shape[2:]
    wide, tall = size_x + 4, size_y + 8
    return pl.pallas_call(
        functools.partial(share_kernel, nx, ny),
        out_shape=[
            f32(6, wide, tall, depth),
            f32(size_x, size_y, depth),
            f32(3, size_x - 2, size_y - 8, depth),
        ],
        in_specs=in_vmem(3),
        out_specs=in_vmem(3),
        scratch_shapes=[
            *halo_scratch(SHARE_DOWN, SHARE_UP, size_x, depth),
            pltpu.SemaphoreType.DMA((8,)),
            pltpu.SemaphoreType.DMA((8,)),
        ],
        compiler_params=pltpu.CompilerParams(
            collective_id=1, has_side_effects=True, vmem_limit_bytes=6 * MIB
        ),
        name="share",
    )(state, src, fwd)


def finish_kernel(
    nx, ny, both, state, src, fwd, grad1, h_low, e_out, h_out, grad_out, e, h, grad, sem
):
    place = Place(nx, ny)
    e1, src1 = both.at[pl.ds(0, 3)], both.at[pl.ds(3, 3)]
    _, h1, decay, gain = parts_of(state)
    size_x, size_y, depth = grad1.shape
    rows = size_y + 8
    moves = shifts(rows, depth)
    factor = h_factor(place, size_y, rows, depth)

    low = h_low.shape[2]
    up_z = shifts(rows - low, depth)[0]
    last = lax.broadcasted_iota(jnp.int32, (rows - low, depth), 0) == rows - low - 1

    def h_second(x):
        p = x + 2

        def up_y(c, f):
            return jnp.where(last, e1[c, p, 0:1], pltpu.roll(f, rows - low - 1, 0))

        new = h_rows(e1, h1, p, slice(low, rows), factor[low:], up_z, up_y)
        for c in range(3):
            h[c, p, :low] = h_low[c, x]
            h[c, p, low:] = new[c]

    for p in (0, 1, size_x, size_x + 1, size_x + 2):
        h_plane(e1, h1, h, p, factor * jnp.where(place.plane(p, size_x), 1.0, 0.0), moves)
    sweep(0, size_x - 2, h_second, 6)

    def e_second(p, inner):
        fade, rise = decay[p], gain[p]
        total = None
        for c, curl in enumerate(curl_h(h, p, moves)):
            new = fade * e1[c, p] + rise * (curl - src1[c, p])
            e[c, p] = new
            if inner:
                term = fwd[1, c, p - 2].astype(jnp.float32) * new[:size_y]
                total = term if total is None else total + term
        if inner:
            grad[p - 2] = grad1[p - 2] + total

    e_second(1, False)

    def e_inner(p):
        e_second(p, True)

    sweep(2, size_x, e_inner, 8)
    e_second(size_x + 2, False)

    def h_third(p):
        h_plane(e, h, h, p, factor * jnp.where(place.plane(p, size_x), 1.0, 0.0), moves)

    sweep(1, size_x + 1, h_third, 11)
    inside = pl.ds(0, size_y)
    h_copy = pltpu.make_async_copy(h.at[:, pl.ds(2, size_x), inside], h_out, sem.at[0])
    h_copy.start()

    def e_third(x):
        p = x + 2
        fade, rise = decay[p, :size_y], gain[p, :size_y]
        total = grad[x]
        for c, curl in enumerate(curl_h(h, p, moves)):
            source = src[c, x, pl.ds(2, size_y, stride=FIELDS), :]
            new = fade * e[c, p, :size_y] + rise * (curl[:size_y] - source)
            e[c, p, :size_y] = new
            total = total + fwd[2, c, x].astype(jnp.float32) * new
        grad[x] = total

    each = size_x // PARTS

    def results(k):
        here = pl.ds(k * each, each)
        return (
            pltpu.make_async_copy(e.at[:, pl.ds(2 + k * each, each), inside], e_out.at[:, here], sem.at[1 + 2 * k]),
            pltpu.make_async_copy(grad.at[here], grad_out.at[here], sem.at[2 + 2 * k]),
        )

    def part(k, _):
        for x in range(each):
            e_third(k * each + x)
        for copy in results(k):
            copy.start()
        return 0

    lax.fori_loop(0, PARTS, part, 0)
    h_copy.wait()
    for k in range(PARTS):
        for copy in results(k):
            copy.wait()


def finish(nx, ny, both, state, src, fwd, grad1, h_low):
    size_x, size_y, depth = grad1.shape
    field = f32(3, size_x, size_y, depth)
    return pl.pallas_call(
        functools.partial(finish_kernel, nx, ny),
        out_shape=[field, field, f32(size_x, size_y, depth)],
        in_specs=in_vmem(6),
        out_specs=[pl.BlockSpec(memory_space=pltpu.HBM)] * 3,
        scratch_shapes=[
            pltpu.VMEM((3, *both.shape[1:]), jnp.float32),
            pltpu.VMEM((3, *both.shape[1:]), jnp.float32),
            pltpu.VMEM(grad1.shape, jnp.float32),
            pltpu.SemaphoreType.DMA((1 + 2 * PARTS,)),
        ],
        compiler_params=pltpu.CompilerParams(vmem_limit_bytes=10 * MIB),
        name="finish",
    )(both, state, src, fwd, grad1, h_low)


def per_device(
    e_adjoint,
    h_adjoint,
    conductivity,
    permittivity,
    forward_e,
    receiver_data,
    receiver_tile,
    receiver_cell,
    receiver_comp,
):
    _, size_x, size_y, depth = e_adjoint.shape
    nx, ny = lax.axis_size("gx"), lax.axis_size("gy")
    receivers = receiver_data.shape[0]
    cap = 3 * receivers // (nx * ny)
    by_lane = lambda a: a.reshape(receivers // LANES, LANES)
    got, codes, state = route(
        nx,
        ny,
        receiver_data,
        by_lane(receiver_tile),
        by_lane(receiver_cell),
        by_lane(receiver_comp),
        e_adjoint,
        h_adjoint,
        conductivity,
        permittivity,
    )
    placed = scatter(cap, 3 * size_x * size_y, codes, got)
    placed = placed.reshape(3, size_x, size_y * FIELDS, depth)
    both, grad1, h_low = share(nx, ny, state, placed, forward_e)
    return tuple(finish(nx, ny, both, state, placed, forward_e, grad1, h_low))


def solution(mesh):
    placed = (
        P(None, "gx", "gy", None),
        P(None, "gx", "gy", None),
        P("gx", "gy", None),
        P("gx", "gy", None),
        P(None, None, "gx", "gy", None),
        P(("gx", "gy"), None),
        P(("gx", "gy"), None),
        P(("gx", "gy")),
        P(("gx", "gy")),
    )
    return jax.shard_map(
        per_device,
        mesh=mesh,
        in_specs=placed,
        out_specs=(P(None, "gx", "gy", None), P(None, "gx", "gy", None), P("gx", "gy", None)),
        check_vma=False,
    )
```

```python
import functools

import jax
import jax.numpy as jnp
from jax import lax
from jax.experimental import pallas as pl
from jax.experimental.pallas import tpu as pltpu
from jax.sharding import PartitionSpec as P

STEPS = 3
SAMPLES = 128
LANES = 128
FIELDS = 4
SPAN = LANES // FIELDS
MESH = pl.DeviceIdType.MESH
GROUP = 8
PARTS = 2
MIB = 1 << 20

time_step = 0.55


def split3(x):
    a = x.astype(jnp.bfloat16)
    rest = x - a.astype(jnp.float32)
    b = rest.astype(jnp.bfloat16)
    c = (rest - b.astype(jnp.float32)).astype(jnp.bfloat16)
    return a, b, c


def mm(a, b, contract=((1,), (0,))):
    return lax.dot_general(a, b, (contract, ((), ())), preferred_element_type=jnp.float32)


def time_kernel():
    shape = (SAMPLES, LANES)
    sample = lax.broadcasted_iota(jnp.int32, shape, 0).astype(jnp.float32)
    field = lax.broadcasted_iota(jnp.int32, shape, 1) // SPAN
    centre = (field.astype(jnp.float32) + 0.5) * (SAMPLES / STEPS)
    spread = SAMPLES / (4.0 * STEPS)
    kernel = jnp.exp(-jnp.square((sample - centre) / spread))
    norm = jnp.sum(kernel * kernel, axis=0, keepdims=True)
    return jnp.where(field < STEPS, kernel / jnp.sqrt(norm), 0.0)


def pack(devices, cells, data_ref, tile_ref, cell_ref, comp_ref):
    blocks, width = tile_ref.shape
    kernel = time_kernel()
    at, to = (lax.broadcasted_iota(jnp.int32, (width, width), n) for n in (0, 1))
    before = (at < to).astype(jnp.bfloat16)
    every = jnp.ones((width, width), jnp.bfloat16)
    diagonal = at == to
    destination = lax.broadcasted_iota(jnp.int32, (devices, width), 0)
    lane = lax.broadcasted_iota(jnp.int32, (width, LANES), 1)
    slot = jnp.bitwise_and(lane, SPAN - 1).astype(jnp.float32)
    is_code = lane >= STEPS * SPAN
    down = jnp.ones((width, LANES), jnp.bfloat16)
    seen = jnp.zeros((devices, width), jnp.float32)
    packed = jnp.zeros((devices, LANES), jnp.float32)

    def column(row):
        return jnp.where(diagonal, row.astype(jnp.float32), 0.0).astype(jnp.bfloat16)

    for b in range(blocks):
        onehot = (destination == tile_ref[b : b + 1, :]).astype(jnp.float32)
        hot = onehot.astype(jnp.bfloat16)
        rank = jnp.sum(onehot * (seen + mm(hot, before)), axis=0, keepdims=True)
        seen = seen + mm(hot, every)
        amplitude = lax.dot_general(
            data_ref[b * width : (b + 1) * width, :],
            kernel,
            (((1,), (0,)), ((), ())),
            precision=lax.Precision.HIGHEST,
            preferred_element_type=jnp.float32,
        )
        code = comp_ref[b : b + 1, :] * cells + cell_ref[b : b + 1, :]
        low = jnp.bitwise_and(code, 255)
        middle = jnp.bitwise_and(code, 255 << 8)
        high = code - low - middle
        codes = mm(column(low), down) + mm(column(middle), down) + mm(column(high), down)
        spread = jnp.where(
            slot == mm(column(rank), down), jnp.where(is_code, codes, amplitude), 0.0
        )
        for term in split3(spread):
            packed = packed + mm(hot, term)
    return packed


def sweep(start, count, body, width):
    def several(n, _):
        for k in range(width):
            body(start + n * width + k)
        return 0

    turns = count // width
    lax.fori_loop(0, turns, several, 0)
    for p in range(turns * width, count):
        body(start + p)


class Place:
    def __init__(self, nx, ny):
        self.nx, self.ny = nx, ny
        self.ix, self.iy = lax.axis_index("gx"), lax.axis_index("gy")
        self.inside_x = {-1: self.ix > 0, 0: None, 1: self.ix < nx - 1}
        self.inside_y = {-1: self.iy > 0, 0: None, 1: self.iy < ny - 1}

    def other(self, dx, dy):
        return lax.rem(self.ix + dx + self.nx, self.nx), lax.rem(self.iy + dy + self.ny, self.ny)

    def has(self, dx, dy):
        x, y = self.inside_x[dx], self.inside_y[dy]
        if x is None or y is None:
            return y if x is None else x
        return jnp.logical_and(x, y)

    def plane(self, p, size_x):
        low, high = jnp.logical_or(p >= 2, self.ix > 0), jnp.logical_or(p < size_x + 2, self.ix < self.nx - 1)
        return jnp.logical_and(low, high)


AROUND = tuple((dx, dy) for dx in (-1, 0, 1) for dy in (-1, 0, 1) if (dx, dy) != (0, 0))


def greet(place, barrier, offsets):
    count = jnp.int32(0)
    for dx, dy in offsets:
        here = place.has(dx, dy)
        count = count + here.astype(jnp.int32)

        @pl.when(here)
        def _(dx=dx, dy=dy):
            pl.semaphore_signal(barrier, inc=1, device_id=place.other(dx, dy), device_id_type=MESH)

    return count


def shifts(rows, depth):
    lane = lax.broadcasted_iota(jnp.int32, (rows, depth), 1)

    def up_z(f):
        return jnp.where(lane == depth - 1, 0.0, pltpu.roll(f, depth - 1, 1))

    def down_z(f):
        return jnp.where(lane == 0, 0.0, pltpu.roll(f, 1, 1))

    def up_y(f):
        return pltpu.roll(f, rows - 1, 0)

    def down_y(f):
        return pltpu.roll(f, 1, 0)

    return up_z, down_z, up_y, down_y


def h_plane(e, h_from, h_to, p, factor, moves):
    up_z, _, up_y, _ = moves
    ex, ey, ez = e[0, p], e[1, p], e[2, p]
    curl_x = (up_y(ez) - ez) - (up_z(ey) - ey)
    curl_y = (up_z(ex) - ex) - (e[2, p + 1] - ez)
    curl_z = (e[1, p + 1] - ey) - (up_y(ex) - ex)
    for c, curl in enumerate((curl_x, curl_y, curl_z)):
        h_to[c, p] = h_from[c, p] - factor * curl


def h_rows(e, h, p, rows, factor, up_z, up_y):
    ex, ey, ez = (e[c, p, rows] for c in range(3))
    curl_x = (up_y(2, ez) - ez) - (up_z(ey) - ey)
    curl_y = (up_z(ex) - ex) - (e[2, p + 1, rows] - ez)
    curl_z = (e[1, p + 1, rows] - ey) - (up_y(0, ex) - ex)
    return [h[c, p, rows] - factor * curl for c, curl in enumerate((curl_x, curl_y, curl_z))]


def curl_h(h, p, moves):
    _, down_z, _, down_y = moves
    hx, hy, hz = h[0, p], h[1, p], h[2, p]
    curl_x = (hz - down_y(hz)) - (hy - down_z(hy))
    curl_y = (hx - down_z(hx)) - (hz - h[2, p - 1])
    curl_z = (hy - h[1, p - 1]) - (hx - down_y(hx))
    return curl_x, curl_y, curl_z


def h_factor(place, size_y, rows, depth):
    row = lax.broadcasted_iota(jnp.int32, (rows, depth), 0)
    above, below = jnp.where(place.has(0, 1), 1.0, 0.0), jnp.where(place.has(0, -1), 1.0, 0.0)
    return time_step * jnp.where(row < size_y, 1.0, jnp.where(row < size_y + 4, above, below))


def row_copies(dn_put, up_put, up_got, lo_got, size_x):
    first, last, low, high = pl.ds(0, 2), pl.ds(size_x - 2, 2), pl.ds(0, 2), pl.ds(size_x + 2, 2)
    whole = pl.ds(2, size_x)
    return [
        (dn_put.at[:, first], up_got.at[:, high], -1, -1),
        (dn_put.at[:, last], up_got.at[:, low], 1, -1),
        (up_put.at[:, first], lo_got.at[:, high], -1, 1),
        (up_put.at[:, last], lo_got.at[:, low], 1, 1),
        (dn_put, up_got.at[:, whole], 0, -1),
        (up_put, lo_got.at[:, whole], 0, 1),
    ]


def plane_copies(array, count, size_x, size_y):
    lead = (slice(None),) * (len(array.shape) - 3)
    rows = pl.ds(0, size_y)

    def part(start):
        return array.at[(*lead, pl.ds(start, count), rows)]

    return [
        (part(2), part(size_x + 2), -1, 0),
        (part(size_x + 2 - count), part(2 - count), 1, 0),
    ]


FIELD_DOWN = ((0, 0, 0), (0, 1, 0), (0, 2, 0), (0, 0, 1), (0, 2, 1))
FIELD_UP = tuple((0, c, r) for c in range(3) for r in range(2))
ROUTE_DOWN = (*FIELD_DOWN, (1, 0, 0), (1, 1, 0), (1, 2, 0), (2, 0, 0), (3, 0, 0))
ROUTE_UP = (*FIELD_UP, (1, 0, 0), (1, 2, 0), (1, 0, 1), (1, 1, 1), (1, 2, 1), (2, 0, 1), (3, 0, 1))
SHARE_DOWN = (*FIELD_DOWN, (1, 0, 0), (1, 2, 0))
SHARE_UP = (*FIELD_UP, (1, 0, 1), (1, 1, 1), (1, 2, 1))


def halo_scratch(down, up, size_x, depth):
    shapes = [(len(down), size_x), (len(up), size_x), (len(down), size_x + 4), (len(up), size_x + 4)]
    return [pltpu.VMEM((*shape, 1, depth), jnp.float32) for shape in shapes]


def halo_rows(array, c, p, down, up, up_got, lo_got, above, below, fill):
    def one(names, got, r, keep):
        if (array, c, r) not in names:
            return fill
        return jnp.where(keep, got[names.index((array, c, r)), p], fill)

    return jnp.concatenate(
        [one(down, up_got, 0, above), one(down, up_got, 1, above)]
        + [fill] * 4
        + [one(up, lo_got, 0, below), one(up, lo_got, 1, below)],
        axis=0,
    )


class Exchange:
    def __init__(self, place, parts, send, recv):
        self.parts = []
        for n, (a, b, dx, dy) in enumerate(parts):
            copy = pltpu.make_async_remote_copy(
                src_ref=a,
                dst_ref=b,
                send_sem=send.at[n],
                recv_sem=recv.at[n],
                device_id=place.other(dx, dy),
                device_id_type=MESH,
            )
            self.parts.append((copy, place.has(dx, dy), place.has(-dx, -dy)))
            pl.when(self.parts[-1][1])(copy.start)

    def wait(self):
        for copy, goes, comes in self.parts:
            pl.when(comes)(copy.wait_recv)
            pl.when(goes)(copy.wait_send)


def parts_of(state):
    return state.at[pl.ds(0, 3)], state.at[pl.ds(3, 3)], state.at[6], state.at[7]


def route_kernel(
    nx,
    ny,
    cells,
    data_in,
    tile_in,
    cell_in,
    comp_in,
    e_in,
    h_in,
    cond_in,
    perm_in,
    got_ref,
    code_ref,
    state,
    data_ref,
    tile_ref,
    cell_ref,
    comp_ref,
    first,
    mid,
    second,
    last,
    dn_put,
    up_put,
    up_got,
    lo_got,
    load,
    send_y,
    recv_y,
    send_x,
    recv_x,
    send,
    recv,
):
    place = Place(nx, ny)
    ix, iy = place.ix, place.iy
    e, h, decay, gain = parts_of(state)
    size_x, size_y, depth = cond_in.shape
    rows = size_y + 8
    inner = (pl.ds(2, size_x), pl.ds(0, size_y))
    pairs = (
        (tile_in, tile_ref),
        (cell_in, cell_ref),
        (comp_in, comp_ref),
        (data_in, data_ref),
        (e_in, e.at[:, inner[0], inner[1]]),
        (h_in, h.at[:, inner[0], inner[1]]),
        (cond_in, decay.at[inner[0], inner[1]]),
        (perm_in, gain.at[inner[0], inner[1]]),
    )
    loads = [pltpu.make_async_copy(a, b, load.at[n]) for n, (a, b) in enumerate(pairs)]
    for copy in loads:
        copy.start()
    barrier = pltpu.get_barrier_semaphore()
    for k in range(1, nx):
        pl.semaphore_signal(barrier, inc=1, device_id=(lax.rem(ix + k, nx), iy), device_id_type=MESH)
    for k in range(1, ny):
        pl.semaphore_signal(barrier, inc=1, device_id=(ix, lax.rem(iy + k, ny)), device_id_type=MESH)
    corners = greet(place, barrier, [o for o in AROUND if 0 not in o])
    for copy in loads[:4]:
        copy.wait()
    first[...] = pack(nx * ny, cells, data_ref, tile_ref, cell_ref, comp_ref)
    for copy in loads[4:]:
        copy.wait()

    def stage(x):
        p = x + 2
        arrays = ((e.at[0], e.at[1], e.at[2]), (h.at[0], h.at[1], h.at[2]), (decay,), (gain,))
        for n, (array, c, r) in enumerate(ROUTE_DOWN):
            dn_put[n, x] = arrays[array][c][p, r : r + 1, :]
        for n, (array, c, r) in enumerate(ROUTE_UP):
            up_put[n, x] = arrays[array][c][p, size_y - 2 + r : size_y - 1 + r, :]

    sweep(0, size_x, stage, 4)
    pl.semaphore_wait(barrier, corners + (nx + ny - 2))
    by_row = Exchange(
        place, row_copies(dn_put, up_put, up_got, lo_got, size_x), send.at[0], recv.at[0]
    )
    copies = []
    for k in range(1, nx):
        to = lax.rem(ix + k, nx)
        copy = pltpu.make_async_remote_copy(
            src_ref=first.at[pl.ds(pl.multiple_of(to * ny, ny), ny), :],
            dst_ref=mid.at[pl.ds(pl.multiple_of(ix * ny, ny), ny), :],
            send_sem=send_x.at[k - 1],
            recv_sem=recv_x.at[k - 1],
            device_id=(to, iy),
            device_id_type=MESH,
        )
        copy.start()
        copies.append(copy)
    by_plane = Exchange(
        place, plane_copies(state, 2, size_x, size_y), send.at[1], recv.at[1]
    )
    own = pl.ds(pl.multiple_of(ix * ny, ny), ny)
    mid[own, :] = first[own, :]
    for copy in copies:
        copy.wait_recv()
    for j in range(ny):
        second[j * nx : (j + 1) * nx, :] = mid[pl.ds(j, nx, stride=ny), :]
    later = []
    for k in range(1, ny):
        to = lax.rem(iy + k, ny)
        copy = pltpu.make_async_remote_copy(
            src_ref=second.at[pl.ds(pl.multiple_of(to * nx, nx), nx), :],
            dst_ref=last.at[pl.ds(pl.multiple_of(iy * nx, nx), nx), :],
            send_sem=send_y.at[k - 1],
            recv_sem=recv_y.at[k - 1],
            device_id=(ix, to),
            device_id_type=MESH,
        )
        copy.start()
        later.append(copy)
    own = pl.ds(pl.multiple_of(iy * nx, nx), nx)
    last[own, :] = second[own, :]
    for copy in copies:
        copy.wait_send()

    by_plane.wait()
    by_row.wait()
    for p in (0, 1, size_x + 2, size_x + 3):
        keep = place.plane(p, size_x)
        for c in range(3):
            for array in (e, h):
                array[c, p, :size_y] = jnp.where(keep, array[c, p, :size_y], 0.0)

    def unstage(p):
        keep = place.plane(p, size_x)
        above, below = jnp.logical_and(keep, place.has(0, 1)), jnp.logical_and(keep, place.has(0, -1))
        gap = jnp.zeros((1, depth), jnp.float32)
        for array, field in enumerate((e, h)):
            for c in range(3):
                field[c, p, size_y:] = halo_rows(
                    array, c, p, ROUTE_DOWN, ROUTE_UP, up_got, lo_got, above, below, gap
                )

    sweep(0, size_x + 4, unstage, 4)
    row = lax.broadcasted_iota(jnp.int32, (rows, depth), 0)
    inside = jnp.where(
        row < size_y,
        1.0,
        jnp.where(
            row == size_y,
            jnp.where(place.has(0, 1), 1.0, 0.0),
            jnp.where(row == rows - 1, jnp.where(place.has(0, -1), 1.0, 0.0), 0.0),
        ),
    )
    ones = jnp.ones((1, depth), jnp.float32)

    def coefficients(p):
        for array, field in ((2, decay), (3, gain)):
            field[p, size_y:] = halo_rows(array, 0, p, ROUTE_DOWN, ROUTE_UP, up_got, lo_got, True, True, ones)
        half_loss = decay[p] * (0.5 * time_step)
        eps = gain[p]
        inverse = 1.0 / (eps + half_loss)
        keep = inside > jnp.where(place.plane(p, size_x), 0.5, 1.5)
        decay[p] = jnp.where(keep, (eps - half_loss) * inverse, 0.0)
        gain[p] = jnp.where(keep, time_step * inverse, 0.0)

    sweep(1, size_x + 2, coefficients, 2)
    moves = shifts(rows, depth)
    factor = h_factor(place, size_y, rows, depth)

    def h_step(p):
        h_plane(e, h, h, p, factor * jnp.where(place.plane(p, size_x), 1.0, 0.0), moves)

    sweep(0, size_x + 3, h_step, 7)

    for copy in later:
        copy.wait()
    got_ref[...] = last[...]
    quarter = nx * ny // FIELDS
    lane = lax.broadcasted_iota(jnp.int32, (quarter, LANES), 1) // SPAN
    codes = jnp.zeros((quarter, LANES), jnp.int32)
    for k in range(FIELDS):
        code = last[pl.ds(k, quarter, stride=FIELDS), :].astype(jnp.int32)
        word = jnp.bitwise_and(code, LANES - 1) + jnp.bitwise_and(code, -LANES) * FIELDS
        codes = jnp.where(lane == k, pltpu.roll(word, (k + 1) * SPAN % LANES, 1), codes)
    code_ref[...] = codes


def in_vmem(count):
    return [pl.BlockSpec(memory_space=pltpu.VMEM)] * count


def f32(*shape):
    return jax.ShapeDtypeStruct(shape, jnp.float32)


def route(nx, ny, data, tile, cell, comp, e, h, cond, perm):
    devices = nx * ny
    size_x, size_y, depth = cond.shape
    wide, tall = size_x + 4, size_y + 8
    inputs = (data, tile, cell, comp, e, h, cond, perm)
    rows = lambda: pltpu.VMEM((devices, LANES), jnp.float32)
    return pl.pallas_call(
        functools.partial(route_kernel, nx, ny, size_x * size_y * depth),
        out_shape=[
            f32(devices, LANES),
            jax.ShapeDtypeStruct((devices // FIELDS, LANES), jnp.int32),
            f32(8, wide, tall, depth),
        ],
        in_specs=[pl.BlockSpec(memory_space=pltpu.HBM)] * 8,
        out_specs=in_vmem(3),
        scratch_shapes=[
            *(pltpu.VMEM(a.shape, a.dtype) for a in (data, tile, cell, comp)),
            rows(),
            rows(),
            rows(),
            rows(),
            *halo_scratch(ROUTE_DOWN, ROUTE_UP, size_x, depth),
            pltpu.SemaphoreType.DMA((8,)),
            pltpu.SemaphoreType.DMA((ny - 1,)),
            pltpu.SemaphoreType.DMA((ny - 1,)),
            pltpu.SemaphoreType.DMA((nx - 1,)),
            pltpu.SemaphoreType.DMA((nx - 1,)),
            pltpu.SemaphoreType.DMA((2, 8)),
            pltpu.SemaphoreType.DMA((2, 8)),
        ],
        compiler_params=pltpu.CompilerParams(
            collective_id=0, has_side_effects=True, vmem_limit_bytes=16 * MIB
        ),
        name="route",
    )(*(pltpu.with_memory_space_constraint(a, pltpu.HBM) for a in inputs))


def scatter_kernel(cap, code_in, got_ref, out_ref, code_ref, quad, terms, wide, sem):
    fetch = pltpu.make_async_copy(code_in, code_ref, sem)
    fetch.start()
    devices = got_ref.shape[0]
    got = got_ref[...]
    lane = lax.broadcasted_iota(jnp.int32, (devices, LANES), 1)
    slot = jnp.bitwise_and(lane, SPAN - 1)
    codes = jnp.where(lane >= (FIELDS - 1) * SPAN, got, 0.0)
    codes = codes + pltpu.roll(codes, SPAN, 1)
    codes = codes + pltpu.roll(codes, 2 * SPAN, 1)
    total = got
    place_in_group = slot - slot // GROUP * GROUP
    for d in range(1, GROUP):
        same = (codes == pltpu.roll(codes, d, 1)) & (place_in_group >= d)
        total = total + jnp.where(same, pltpu.roll(got, d, 1), 0.0)
    for t in range(FIELDS):
        quad[pl.ds(t, devices, stride=FIELDS), :] = jnp.where(
            (lane >= t * SPAN) & (lane < (t + 1) * SPAN), total, 0.0
        )
    values = quad[...]
    high = values.astype(jnp.bfloat16)
    low = (values - high.astype(jnp.float32)).astype(jnp.bfloat16)
    terms[:, :LANES] = high
    terms[:, LANES:] = low
    row_slot = jnp.bitwise_and(lax.broadcasted_iota(jnp.int32, (2 * LANES, 2 * LANES), 0), SPAN - 1)
    column = lax.broadcasted_iota(jnp.int32, (2 * LANES, 2 * LANES), 1) // LANES
    for i in range(0, cap, 2):
        both = mm(terms[...], (row_slot == column + i).astype(jnp.bfloat16))
        wide[i] = both[:, :LANES]
        wide[i + 1] = both[:, LANES:]
    step = 512

    def clear(n, _):
        out_ref[pl.ds(pl.multiple_of(n * step, step), step), :] = jnp.zeros((step, LANES), jnp.float32)
        return 0

    lax.fori_loop(0, out_ref.shape[0] // step, clear, 0)
    fetch.wait()
    depth = lax.broadcasted_iota(jnp.int32, (FIELDS, LANES), 1)

    def place(q, _):
        for p in range(FIELDS):
            s = q * FIELDS + p
            for start in range(0, cap, GROUP):
                where, news = [], []
                for i in range(start, min(cap, start + GROUP)):
                    word = code_ref[q, p * SPAN + i]
                    row = pl.ds(pl.multiple_of(lax.shift_right_logical(word, 7), FIELDS), FIELDS)
                    news.append(out_ref[row, :] + wide[i, pl.ds(pl.multiple_of(s * FIELDS, FIELDS), FIELDS), :])
                    column = jnp.bitwise_and(jnp.full((FIELDS, LANES), word, jnp.int32), LANES - 1)
                    where.append((row, depth == column))
                for (row, mask), new in zip(where, news):
                    pltpu.store(out_ref.at[row, :], new, mask=mask)
        return 0

    lax.fori_loop(0, devices // FIELDS, place, 0)


def scatter(cap, rows, codes, got):
    devices = got.shape[0]
    return pl.pallas_call(
        functools.partial(scatter_kernel, cap),
        out_shape=jax.ShapeDtypeStruct((rows * FIELDS, LANES), jnp.float32),
        in_specs=[pl.BlockSpec(memory_space=pltpu.VMEM)] * 2,
        out_specs=pl.BlockSpec(memory_space=pltpu.VMEM),
        scratch_shapes=[
            pltpu.SMEM(codes.shape, jnp.int32),
            pltpu.VMEM((devices * FIELDS, LANES), jnp.float32),
            pltpu.VMEM((devices * FIELDS, 2 * LANES), jnp.bfloat16),
            pltpu.VMEM((cap, devices * FIELDS, LANES), jnp.float32),
            pltpu.SemaphoreType.DMA,
        ],
        compiler_params=pltpu.CompilerParams(vmem_limit_bytes=24 * MIB),
        name="scatter",
    )(codes, got)


def share_kernel(
    nx, ny, state, src, fwd, both, grad, h_low, dn_put, up_put, up_got, lo_got, send, recv
):
    place = Place(nx, ny)
    e0, h1, decay, gain = parts_of(state)
    e, src1 = both.at[pl.ds(0, 3)], both.at[pl.ds(3, 3)]
    size_x, size_y, depth = grad.shape
    moves = shifts(size_y + 8, depth)
    barrier = pltpu.get_barrier_semaphore()
    others = greet(place, barrier, AROUND)

    def own(x):
        p = x + 2
        fade, rise = decay[p, :size_y], gain[p, :size_y]
        for c, curl in enumerate(curl_h(h1, p, moves)):
            source = src[c, x, pl.ds(0, size_y, stride=FIELDS), :]
            new = fade * e0[c, p, :size_y] + rise * (curl[:size_y] - source)
            e[c, p, :size_y] = new
            source = src[c, x, pl.ds(1, size_y, stride=FIELDS), :]
            src1[c, p, :size_y] = source
            for n, (array, comp, r) in enumerate(SHARE_DOWN):
                if comp == c:
                    dn_put[n, x] = (new, source)[array][r : r + 1]
            for n, (array, comp, r) in enumerate(SHARE_UP):
                if comp == c:
                    up_put[n, x] = (new, source)[array][size_y - 2 + r : size_y - 1 + r]

    sweep(0, size_x, own, 8)
    pl.semaphore_wait(barrier, others)
    halos = Exchange(
        place,
        row_copies(dn_put, up_put, up_got, lo_got, size_x)
        + plane_copies(both, 2, size_x, size_y),
        send,
        recv,
    )

    def product(x):
        total = fwd[0, 0, x].astype(jnp.float32) * e[0, x + 2, :size_y]
        for c in (1, 2):
            total = total + fwd[0, c, x].astype(jnp.float32) * e[c, x + 2, :size_y]
        grad[x] = total

    sweep(0, size_x, product, 4)

    low = h_low.shape[2]
    up_z, _, up_y, _ = shifts(size_y, depth)

    def h_second(x):
        new = h_rows(e, h1, x + 2, slice(0, size_y), time_step, up_z, lambda c, f: up_y(f))
        for c in range(3):
            h_low[c, x] = new[c][:low]

    sweep(0, size_x - 2, h_second, 6)
    halos.wait()
    for p in (0, 1, size_x + 2, size_x + 3):
        keep = place.plane(p, size_x)
        for c in range(3):
            e[c, p, :size_y] = jnp.where(keep, e[c, p, :size_y], 0.0)
            src1[c, p, :size_y] = jnp.where(keep, src1[c, p, :size_y], 0.0)

    def unstage(p):
        keep = place.plane(p, size_x)
        above, below = jnp.logical_and(keep, place.has(0, 1)), jnp.logical_and(keep, place.has(0, -1))
        gap = jnp.zeros((1, depth), jnp.float32)
        for array, field in enumerate((e, src1)):
            for c in range(3):
                field[c, p, size_y:] = halo_rows(
                    array, c, p, SHARE_DOWN, SHARE_UP, up_got, lo_got, above, below, gap
                )

    sweep(0, size_x + 4, unstage, 4)


def share(nx, ny, state, src, fwd):
    size_x, size_y, depth = fwd.shape[2:]
    wide, tall = size_x + 4, size_y + 8
    return pl.pallas_call(
        functools.partial(share_kernel, nx, ny),
        out_shape=[
            f32(6, wide, tall, depth),
            f32(size_x, size_y, depth),
            f32(3, size_x - 2, size_y - 8, depth),
        ],
        in_specs=in_vmem(3),
        out_specs=in_vmem(3),
        scratch_shapes=[
            *halo_scratch(SHARE_DOWN, SHARE_UP, size_x, depth),
            pltpu.SemaphoreType.DMA((8,)),
            pltpu.SemaphoreType.DMA((8,)),
        ],
        compiler_params=pltpu.CompilerParams(
            collective_id=1, has_side_effects=True, vmem_limit_bytes=6 * MIB
        ),
        name="share",
    )(state, src, fwd)


def finish_kernel(
    nx, ny, both, state, src, fwd, grad1, h_low, e_out, h_out, grad_out, e, h, grad, sem
):
    place = Place(nx, ny)
    e1, src1 = both.at[pl.ds(0, 3)], both.at[pl.ds(3, 3)]
    _, h1, decay, gain = parts_of(state)
    size_x, size_y, depth = grad1.shape
    rows = size_y + 8
    moves = shifts(rows, depth)
    factor = h_factor(place, size_y, rows, depth)

    low = h_low.shape[2]
    up_z = shifts(rows - low, depth)[0]
    last = lax.broadcasted_iota(jnp.int32, (rows - low, depth), 0) == rows - low - 1

    def h_second(x):
        p = x + 2

        def up_y(c, f):
            return jnp.where(last, e1[c, p, 0:1], pltpu.roll(f, rows - low - 1, 0))

        new = h_rows(e1, h1, p, slice(low, rows), factor[low:], up_z, up_y)
        for c in range(3):
            h[c, p, :low] = h_low[c, x]
            h[c, p, low:] = new[c]

    for p in (0, 1, size_x, size_x + 1, size_x + 2):
        h_plane(e1, h1, h, p, factor * jnp.where(place.plane(p, size_x), 1.0, 0.0), moves)
    sweep(0, size_x - 2, h_second, 10)

    def e_second(p, inner):
        fade, rise = decay[p], gain[p]
        total = None
        for c, curl in enumerate(curl_h(h, p, moves)):
            new = fade * e1[c, p] + rise * (curl - src1[c, p])
            e[c, p] = new
            if inner:
                term = fwd[1, c, p - 2].astype(jnp.float32) * new[:size_y]
                total = term if total is None else total + term
        if inner:
            grad[p - 2] = grad1[p - 2] + total

    e_second(1, False)

    def e_inner(p):
        e_second(p, True)

    sweep(2, size_x, e_inner, 16)
    e_second(size_x + 2, False)

    def h_third(p):
        h_plane(e, h, h, p, factor * jnp.where(place.plane(p, size_x), 1.0, 0.0), moves)

    sweep(1, size_x + 1, h_third, 11)
    inside = pl.ds(0, size_y)
    h_copy = pltpu.make_async_copy(h.at[:, pl.ds(2, size_x), inside], h_out, sem.at[0])
    h_copy.start()

    def e_third(x):
        p = x + 2
        fade, rise = decay[p, :size_y], gain[p, :size_y]
        total = grad[x]
        for c, curl in enumerate(curl_h(h, p, moves)):
            source = src[c, x, pl.ds(2, size_y, stride=FIELDS), :]
            new = fade * e[c, p, :size_y] + rise * (curl[:size_y] - source)
            e[c, p, :size_y] = new
            total = total + fwd[2, c, x].astype(jnp.float32) * new
        grad[x] = total

    each = size_x // PARTS

    def results(k):
        here = pl.ds(k * each, each)
        return (
            pltpu.make_async_copy(e.at[:, pl.ds(2 + k * each, each), inside], e_out.at[:, here], sem.at[1 + 2 * k]),
            pltpu.make_async_copy(grad.at[here], grad_out.at[here], sem.at[2 + 2 * k]),
        )

    def part(k, _):
        for x in range(each):
            e_third(k * each + x)
        for copy in results(k):
            copy.start()
        return 0

    lax.fori_loop(0, PARTS, part, 0)
    h_copy.wait()
    for k in range(PARTS):
        for copy in results(k):
            copy.wait()


def finish(nx, ny, both, state, src, fwd, grad1, h_low):
    size_x, size_y, depth = grad1.shape
    field = f32(3, size_x, size_y, depth)
    return pl.pallas_call(
        functools.partial(finish_kernel, nx, ny),
        out_shape=[field, field, f32(size_x, size_y, depth)],
        in_specs=in_vmem(6),
        out_specs=[pl.BlockSpec(memory_space=pltpu.HBM)] * 3,
        scratch_shapes=[
            pltpu.VMEM((3, *both.shape[1:]), jnp.float32),
            pltpu.VMEM((3, *both.shape[1:]), jnp.float32),
            pltpu.VMEM(grad1.shape, jnp.float32),
            pltpu.SemaphoreType.DMA((1 + 2 * PARTS,)),
        ],
        compiler_params=pltpu.CompilerParams(vmem_limit_bytes=10 * MIB),
        name="finish",
    )(both, state, src, fwd, grad1, h_low)


def per_device(
    e_adjoint,
    h_adjoint,
    conductivity,
    permittivity,
    forward_e,
    receiver_data,
    receiver_tile,
    receiver_cell,
    receiver_comp,
):
    _, size_x, size_y, depth = e_adjoint.shape
    nx, ny = lax.axis_size("gx"), lax.axis_size("gy")
    receivers = receiver_data.shape[0]
    cap = 3 * receivers // (nx * ny)
    by_lane = lambda a: a.reshape(receivers // LANES, LANES)
    got, codes, state = route(
        nx,
        ny,
        receiver_data,
        by_lane(receiver_tile),
        by_lane(receiver_cell),
        by_lane(receiver_comp),
        e_adjoint,
        h_adjoint,
        conductivity,
        permittivity,
    )
    placed = scatter(cap, 3 * size_x * size_y, codes, got)
    placed = placed.reshape(3, size_x, size_y * FIELDS, depth)
    both, grad1, h_low = share(nx, ny, state, placed, forward_e)
    return tuple(finish(nx, ny, both, state, placed, forward_e, grad1, h_low))


def solution(mesh):
    placed = (
        P(None, "gx", "gy", None),
        P(None, "gx", "gy", None),
        P("gx", "gy", None),
        P("gx", "gy", None),
        P(None, None, "gx", "gy", None),
        P(("gx", "gy"), None),
        P(("gx", "gy"), None),
        P(("gx", "gy")),
        P(("gx", "gy")),
    )
    return jax.shard_map(
        per_device,
        mesh=mesh,
        in_specs=placed,
        out_specs=(P(None, "gx", "gy", None), P(None, "gx", "gy", None), P("gx", "gy", None)),
        check_vma=False,
    )
```

```python
import functools

import jax
import jax.numpy as jnp
from jax import lax
from jax.experimental import pallas as pl
from jax.experimental.pallas import tpu as pltpu
from jax.sharding import PartitionSpec as P

STEPS = 3
SAMPLES = 128
LANES = 128
FIELDS = 4
SPAN = LANES // FIELDS
MESH = pl.DeviceIdType.MESH
GROUP = 8
PARTS = 2
MIB = 1 << 20

time_step = 0.55


def split3(x):
    a = x.astype(jnp.bfloat16)
    rest = x - a.astype(jnp.float32)
    b = rest.astype(jnp.bfloat16)
    c = (rest - b.astype(jnp.float32)).astype(jnp.bfloat16)
    return a, b, c


def mm(a, b, contract=((1,), (0,))):
    return lax.dot_general(a, b, (contract, ((), ())), preferred_element_type=jnp.float32)


def time_kernel():
    shape = (SAMPLES, LANES)
    sample = lax.broadcasted_iota(jnp.int32, shape, 0).astype(jnp.float32)
    field = lax.broadcasted_iota(jnp.int32, shape, 1) // SPAN
    centre = (field.astype(jnp.float32) + 0.5) * (SAMPLES / STEPS)
    spread = SAMPLES / (4.0 * STEPS)
    kernel = jnp.exp(-jnp.square((sample - centre) / spread))
    norm = jnp.sum(kernel * kernel, axis=0, keepdims=True)
    return jnp.where(field < STEPS, kernel / jnp.sqrt(norm), 0.0)


def pack(devices, cells, data_ref, tile_ref, cell_ref, comp_ref):
    blocks, width = tile_ref.shape
    kernel = time_kernel()
    at, to = (lax.broadcasted_iota(jnp.int32, (width, width), n) for n in (0, 1))
    before = (at < to).astype(jnp.bfloat16)
    every = jnp.ones((width, width), jnp.bfloat16)
    diagonal = at == to
    destination = lax.broadcasted_iota(jnp.int32, (devices, width), 0)
    lane = lax.broadcasted_iota(jnp.int32, (width, LANES), 1)
    slot = jnp.bitwise_and(lane, SPAN - 1).astype(jnp.float32)
    is_code = lane >= STEPS * SPAN
    down = jnp.ones((width, LANES), jnp.bfloat16)
    seen = jnp.zeros((devices, width), jnp.float32)
    packed = jnp.zeros((devices, LANES), jnp.float32)

    def column(row):
        return jnp.where(diagonal, row.astype(jnp.float32), 0.0).astype(jnp.bfloat16)

    for b in range(blocks):
        onehot = (destination == tile_ref[b : b + 1, :]).astype(jnp.float32)
        hot = onehot.astype(jnp.bfloat16)
        rank = jnp.sum(onehot * (seen + mm(hot, before)), axis=0, keepdims=True)
        seen = seen + mm(hot, every)
        amplitude = lax.dot_general(
            data_ref[b * width : (b + 1) * width, :],
            kernel,
            (((1,), (0,)), ((), ())),
            precision=lax.Precision.HIGHEST,
            preferred_element_type=jnp.float32,
        )
        code = comp_ref[b : b + 1, :] * cells + cell_ref[b : b + 1, :]
        low = jnp.bitwise_and(code, 255)
        middle = jnp.bitwise_and(code, 255 << 8)
        high = code - low - middle
        codes = mm(column(low), down) + mm(column(middle), down) + mm(column(high), down)
        spread = jnp.where(
            slot == mm(column(rank), down), jnp.where(is_code, codes, amplitude), 0.0
        )
        for term in split3(spread):
            packed = packed + mm(hot, term)
    return packed


def sweep(start, count, body, width):
    def several(n, _):
        for k in range(width):
            body(start + n * width + k)
        return 0

    turns = count // width
    lax.fori_loop(0, turns, several, 0)
    for p in range(turns * width, count):
        body(start + p)


class Place:
    def __init__(self, nx, ny):
        self.nx, self.ny = nx, ny
        self.ix, self.iy = lax.axis_index("gx"), lax.axis_index("gy")
        self.inside_x = {-1: self.ix > 0, 0: None, 1: self.ix < nx - 1}
        self.inside_y = {-1: self.iy > 0, 0: None, 1: self.iy < ny - 1}

    def other(self, dx, dy):
        return lax.rem(self.ix + dx + self.nx, self.nx), lax.rem(self.iy + dy + self.ny, self.ny)

    def has(self, dx, dy):
        x, y = self.inside_x[dx], self.inside_y[dy]
        if x is None or y is None:
            return y if x is None else x
        return jnp.logical_and(x, y)

    def plane(self, p, size_x):
        low, high = jnp.logical_or(p >= 2, self.ix > 0), jnp.logical_or(p < size_x + 2, self.ix < self.nx - 1)
        return jnp.logical_and(low, high)


AROUND = tuple((dx, dy) for dx in (-1, 0, 1) for dy in (-1, 0, 1) if (dx, dy) != (0, 0))


def greet(place, barrier, offsets):
    count = jnp.int32(0)
    for dx, dy in offsets:
        here = place.has(dx, dy)
        count = count + here.astype(jnp.int32)

        @pl.when(here)
        def _(dx=dx, dy=dy):
            pl.semaphore_signal(barrier, inc=1, device_id=place.other(dx, dy), device_id_type=MESH)

    return count


def shifts(rows, depth):
    lane = lax.broadcasted_iota(jnp.int32, (rows, depth), 1)

    def up_z(f):
        return jnp.where(lane == depth - 1, 0.0, pltpu.roll(f, depth - 1, 1))

    def down_z(f):
        return jnp.where(lane == 0, 0.0, pltpu.roll(f, 1, 1))

    def up_y(f):
        return pltpu.roll(f, rows - 1, 0)

    def down_y(f):
        return pltpu.roll(f, 1, 0)

    return up_z, down_z, up_y, down_y


def h_plane(e, h_from, h_to, p, factor, moves):
    up_z, _, up_y, _ = moves
    ex, ey, ez = e[0, p], e[1, p], e[2, p]
    curl_x = (up_y(ez) - ez) - (up_z(ey) - ey)
    curl_y = (up_z(ex) - ex) - (e[2, p + 1] - ez)
    curl_z = (e[1, p + 1] - ey) - (up_y(ex) - ex)
    for c, curl in enumerate((curl_x, curl_y, curl_z)):
        h_to[c, p] = h_from[c, p] - factor * curl


def h_rows(e, h, p, rows, factor, up_z, up_y):
    ex, ey, ez = (e[c, p, rows] for c in range(3))
    curl_x = (up_y(2, ez) - ez) - (up_z(ey) - ey)
    curl_y = (up_z(ex) - ex) - (e[2, p + 1, rows] - ez)
    curl_z = (e[1, p + 1, rows] - ey) - (up_y(0, ex) - ex)
    return [h[c, p, rows] - factor * curl for c, curl in enumerate((curl_x, curl_y, curl_z))]


def curl_h(h, p, moves):
    _, down_z, _, down_y = moves
    hx, hy, hz = h[0, p], h[1, p], h[2, p]
    curl_x = (hz - down_y(hz)) - (hy - down_z(hy))
    curl_y = (hx - down_z(hx)) - (hz - h[2, p - 1])
    curl_z = (hy - h[1, p - 1]) - (hx - down_y(hx))
    return curl_x, curl_y, curl_z


def h_factor(place, size_y, rows, depth):
    row = lax.broadcasted_iota(jnp.int32, (rows, depth), 0)
    above, below = jnp.where(place.has(0, 1), 1.0, 0.0), jnp.where(place.has(0, -1), 1.0, 0.0)
    return time_step * jnp.where(row < size_y, 1.0, jnp.where(row < size_y + 4, above, below))


def row_copies(dn_put, up_put, up_got, lo_got, size_x):
    first, last, low, high = pl.ds(0, 2), pl.ds(size_x - 2, 2), pl.ds(0, 2), pl.ds(size_x + 2, 2)
    whole = pl.ds(2, size_x)
    return [
        (dn_put.at[:, first], up_got.at[:, high], -1, -1),
        (dn_put.at[:, last], up_got.at[:, low], 1, -1),
        (up_put.at[:, first], lo_got.at[:, high], -1, 1),
        (up_put.at[:, last], lo_got.at[:, low], 1, 1),
        (dn_put, up_got.at[:, whole], 0, -1),
        (up_put, lo_got.at[:, whole], 0, 1),
    ]


def plane_copies(array, count, size_x, size_y):
    lead = (slice(None),) * (len(array.shape) - 3)
    rows = pl.ds(0, size_y)

    def part(start):
        return array.at[(*lead, pl.ds(start, count), rows)]

    return [
        (part(2), part(size_x + 2), -1, 0),
        (part(size_x + 2 - count), part(2 - count), 1, 0),
    ]


FIELD_DOWN = ((0, 0, 0), (0, 1, 0), (0, 2, 0), (0, 0, 1), (0, 2, 1))
FIELD_UP = tuple((0, c, r) for c in range(3) for r in range(2))
ROUTE_DOWN = (*FIELD_DOWN, (1, 0, 0), (1, 1, 0), (1, 2, 0), (2, 0, 0), (3, 0, 0))
ROUTE_UP = (*FIELD_UP, (1, 0, 0), (1, 2, 0), (1, 0, 1), (1, 1, 1), (1, 2, 1), (2, 0, 1), (3, 0, 1))
SHARE_DOWN = (*FIELD_DOWN, (1, 0, 0), (1, 2, 0))
SHARE_UP = (*FIELD_UP, (1, 0, 1), (1, 1, 1), (1, 2, 1))


def halo_scratch(down, up, size_x, depth):
    shapes = [(len(down), size_x), (len(up), size_x), (len(down), size_x + 4), (len(up), size_x + 4)]
    return [pltpu.VMEM((*shape, 1, depth), jnp.float32) for shape in shapes]


def halo_rows(array, c, p, down, up, up_got, lo_got, above, below, fill):
    def one(names, got, r, keep):
        if (array, c, r) not in names:
            return fill
        return jnp.where(keep, got[names.index((array, c, r)), p], fill)

    return jnp.concatenate(
        [one(down, up_got, 0, above), one(down, up_got, 1, above)]
        + [fill] * 4
        + [one(up, lo_got, 0, below), one(up, lo_got, 1, below)],
        axis=0,
    )


class Exchange:
    def __init__(self, place, parts, send, recv):
        self.parts = []
        for n, (a, b, dx, dy) in enumerate(parts):
            copy = pltpu.make_async_remote_copy(
                src_ref=a,
                dst_ref=b,
                send_sem=send.at[n],
                recv_sem=recv.at[n],
                device_id=place.other(dx, dy),
                device_id_type=MESH,
            )
            self.parts.append((copy, place.has(dx, dy), place.has(-dx, -dy)))
            pl.when(self.parts[-1][1])(copy.start)

    def wait(self):
        for copy, goes, comes in self.parts:
            pl.when(comes)(copy.wait_recv)
            pl.when(goes)(copy.wait_send)


def parts_of(state):
    return state.at[pl.ds(0, 3)], state.at[pl.ds(3, 3)], state.at[6], state.at[7]


def route_kernel(
    nx,
    ny,
    cells,
    data_in,
    tile_in,
    cell_in,
    comp_in,
    e_in,
    h_in,
    cond_in,
    perm_in,
    got_ref,
    code_ref,
    state,
    data_ref,
    tile_ref,
    cell_ref,
    comp_ref,
    first,
    mid,
    second,
    last,
    dn_put,
    up_put,
    up_got,
    lo_got,
    load,
    send_y,
    recv_y,
    send_x,
    recv_x,
    send,
    recv,
):
    place = Place(nx, ny)
    ix, iy = place.ix, place.iy
    e, h, decay, gain = parts_of(state)
    size_x, size_y, depth = cond_in.shape
    rows = size_y + 8
    inner = (pl.ds(2, size_x), pl.ds(0, size_y))
    pairs = (
        (tile_in, tile_ref),
        (cell_in, cell_ref),
        (comp_in, comp_ref),
        (data_in, data_ref),
        (e_in, e.at[:, inner[0], inner[1]]),
        (h_in, h.at[:, inner[0], inner[1]]),
        (cond_in, decay.at[inner[0], inner[1]]),
        (perm_in, gain.at[inner[0], inner[1]]),
    )
    loads = [pltpu.make_async_copy(a, b, load.at[n]) for n, (a, b) in enumerate(pairs)]
    for copy in loads:
        copy.start()
    barrier = pltpu.get_barrier_semaphore()
    for k in range(1, nx):
        pl.semaphore_signal(barrier, inc=1, device_id=(lax.rem(ix + k, nx), iy), device_id_type=MESH)
    for k in range(1, ny):
        pl.semaphore_signal(barrier, inc=1, device_id=(ix, lax.rem(iy + k, ny)), device_id_type=MESH)
    corners = greet(place, barrier, [o for o in AROUND if 0 not in o])
    for copy in loads[:4]:
        copy.wait()
    first[...] = pack(nx * ny, cells, data_ref, tile_ref, cell_ref, comp_ref)
    for copy in loads[4:]:
        copy.wait()

    def stage(x):
        p = x + 2
        arrays = ((e.at[0], e.at[1], e.at[2]), (h.at[0], h.at[1], h.at[2]), (decay,), (gain,))
        for n, (array, c, r) in enumerate(ROUTE_DOWN):
            dn_put[n, x] = arrays[array][c][p, r : r + 1, :]
        for n, (array, c, r) in enumerate(ROUTE_UP):
            up_put[n, x] = arrays[array][c][p, size_y - 2 + r : size_y - 1 + r, :]

    sweep(0, size_x, stage, 4)
    pl.semaphore_wait(barrier, corners + (nx + ny - 2))
    by_row = Exchange(
        place, row_copies(dn_put, up_put, up_got, lo_got, size_x), send.at[0], recv.at[0]
    )
    copies = []
    for k in range(1, nx):
        to = lax.rem(ix + k, nx)
        copy = pltpu.make_async_remote_copy(
            src_ref=first.at[pl.ds(pl.multiple_of(to * ny, ny), ny), :],
            dst_ref=mid.at[pl.ds(pl.multiple_of(ix * ny, ny), ny), :],
            send_sem=send_x.at[k - 1],
            recv_sem=recv_x.at[k - 1],
            device_id=(to, iy),
            device_id_type=MESH,
        )
        copy.start()
        copies.append(copy)
    by_plane = Exchange(
        place, plane_copies(state, 2, size_x, size_y), send.at[1], recv.at[1]
    )
    own = pl.ds(pl.multiple_of(ix * ny, ny), ny)
    mid[own, :] = first[own, :]
    for copy in copies:
        copy.wait_recv()
    for j in range(ny):
        second[j * nx : (j + 1) * nx, :] = mid[pl.ds(j, nx, stride=ny), :]
    later = []
    for k in range(1, ny):
        to = lax.rem(iy + k, ny)
        copy = pltpu.make_async_remote_copy(
            src_ref=second.at[pl.ds(pl.multiple_of(to * nx, nx), nx), :],
            dst_ref=last.at[pl.ds(pl.multiple_of(iy * nx, nx), nx), :],
            send_sem=send_y.at[k - 1],
            recv_sem=recv_y.at[k - 1],
            device_id=(ix, to),
            device_id_type=MESH,
        )
        copy.start()
        later.append(copy)
    own = pl.ds(pl.multiple_of(iy * nx, nx), nx)
    last[own, :] = second[own, :]
    for copy in copies:
        copy.wait_send()

    by_plane.wait()
    by_row.wait()
    for p in (0, 1, size_x + 2, size_x + 3):
        keep = place.plane(p, size_x)
        for c in range(3):
            for array in (e, h):
                array[c, p, :size_y] = jnp.where(keep, array[c, p, :size_y], 0.0)

    def unstage(p):
        keep = place.plane(p, size_x)
        above, below = jnp.logical_and(keep, place.has(0, 1)), jnp.logical_and(keep, place.has(0, -1))
        gap = jnp.zeros((1, depth), jnp.float32)
        for array, field in enumerate((e, h)):
            for c in range(3):
                field[c, p, size_y:] = halo_rows(
                    array, c, p, ROUTE_DOWN, ROUTE_UP, up_got, lo_got, above, below, gap
                )

    sweep(0, size_x + 4, unstage, 12)
    row = lax.broadcasted_iota(jnp.int32, (rows, depth), 0)
    inside = jnp.where(
        row < size_y,
        1.0,
        jnp.where(
            row == size_y,
            jnp.where(place.has(0, 1), 1.0, 0.0),
            jnp.where(row == rows - 1, jnp.where(place.has(0, -1), 1.0, 0.0), 0.0),
        ),
    )
    ones = jnp.ones((1, depth), jnp.float32)

    def coefficients(p):
        for array, field in ((2, decay), (3, gain)):
            field[p, size_y:] = halo_rows(array, 0, p, ROUTE_DOWN, ROUTE_UP, up_got, lo_got, True, True, ones)
        half_loss = decay[p] * (0.5 * time_step)
        eps = gain[p]
        inverse = 1.0 / (eps + half_loss)
        keep = inside > jnp.where(place.plane(p, size_x), 0.5, 1.5)
        decay[p] = jnp.where(keep, (eps - half_loss) * inverse, 0.0)
        gain[p] = jnp.where(keep, time_step * inverse, 0.0)

    sweep(1, size_x + 2, coefficients, 17)
    moves = shifts(rows, depth)
    factor = h_factor(place, size_y, rows, depth)

    def h_step(p):
        h_plane(e, h, h, p, factor * jnp.where(place.plane(p, size_x), 1.0, 0.0), moves)

    sweep(0, size_x + 3, h_step, 7)

    for copy in later:
        copy.wait()
    got_ref[...] = last[...]
    quarter = nx * ny // FIELDS
    lane = lax.broadcasted_iota(jnp.int32, (quarter, LANES), 1) // SPAN
    codes = jnp.zeros((quarter, LANES), jnp.int32)
    for k in range(FIELDS):
        code = last[pl.ds(k, quarter, stride=FIELDS), :].astype(jnp.int32)
        word = jnp.bitwise_and(code, LANES - 1) + jnp.bitwise_and(code, -LANES) * FIELDS
        codes = jnp.where(lane == k, pltpu.roll(word, (k + 1) * SPAN % LANES, 1), codes)
    code_ref[...] = codes


def in_vmem(count):
    return [pl.BlockSpec(memory_space=pltpu.VMEM)] * count


def f32(*shape):
    return jax.ShapeDtypeStruct(shape, jnp.float32)


def route(nx, ny, data, tile, cell, comp, e, h, cond, perm):
    devices = nx * ny
    size_x, size_y, depth = cond.shape
    wide, tall = size_x + 4, size_y + 8
    inputs = (data, tile, cell, comp, e, h, cond, perm)
    rows = lambda: pltpu.VMEM((devices, LANES), jnp.float32)
    return pl.pallas_call(
        functools.partial(route_kernel, nx, ny, size_x * size_y * depth),
        out_shape=[
            f32(devices, LANES),
            jax.ShapeDtypeStruct((devices // FIELDS, LANES), jnp.int32),
            f32(8, wide, tall, depth),
        ],
        in_specs=[pl.BlockSpec(memory_space=pltpu.HBM)] * 8,
        out_specs=in_vmem(3),
        scratch_shapes=[
            *(pltpu.VMEM(a.shape, a.dtype) for a in (data, tile, cell, comp)),
            rows(),
            rows(),
            rows(),
            rows(),
            *halo_scratch(ROUTE_DOWN, ROUTE_UP, size_x, depth),
            pltpu.SemaphoreType.DMA((8,)),
            pltpu.SemaphoreType.DMA((ny - 1,)),
            pltpu.SemaphoreType.DMA((ny - 1,)),
            pltpu.SemaphoreType.DMA((nx - 1,)),
            pltpu.SemaphoreType.DMA((nx - 1,)),
            pltpu.SemaphoreType.DMA((2, 8)),
            pltpu.SemaphoreType.DMA((2, 8)),
        ],
        compiler_params=pltpu.CompilerParams(
            collective_id=0, has_side_effects=True, vmem_limit_bytes=16 * MIB
        ),
        name="route",
    )(*(pltpu.with_memory_space_constraint(a, pltpu.HBM) for a in inputs))


def scatter_kernel(cap, code_in, got_ref, out_ref, code_ref, quad, terms, wide, sem):
    fetch = pltpu.make_async_copy(code_in, code_ref, sem)
    fetch.start()
    devices = got_ref.shape[0]
    got = got_ref[...]
    lane = lax.broadcasted_iota(jnp.int32, (devices, LANES), 1)
    slot = jnp.bitwise_and(lane, SPAN - 1)
    codes = jnp.where(lane >= (FIELDS - 1) * SPAN, got, 0.0)
    codes = codes + pltpu.roll(codes, SPAN, 1)
    codes = codes + pltpu.roll(codes, 2 * SPAN, 1)
    total = got
    place_in_group = slot - slot // GROUP * GROUP
    for d in range(1, GROUP):
        same = (codes == pltpu.roll(codes, d, 1)) & (place_in_group >= d)
        total = total + jnp.where(same, pltpu.roll(got, d, 1), 0.0)
    for t in range(FIELDS):
        quad[pl.ds(t, devices, stride=FIELDS), :] = jnp.where(
            (lane >= t * SPAN) & (lane < (t + 1) * SPAN), total, 0.0
        )
    values = quad[...]
    high = values.astype(jnp.bfloat16)
    low = (values - high.astype(jnp.float32)).astype(jnp.bfloat16)
    terms[:, :LANES] = high
    terms[:, LANES:] = low
    row_slot = jnp.bitwise_and(lax.broadcasted_iota(jnp.int32, (2 * LANES, 2 * LANES), 0), SPAN - 1)
    column = lax.broadcasted_iota(jnp.int32, (2 * LANES, 2 * LANES), 1) // LANES
    for i in range(0, cap, 2):
        both = mm(terms[...], (row_slot == column + i).astype(jnp.bfloat16))
        wide[i] = both[:, :LANES]
        wide[i + 1] = both[:, LANES:]
    step = 512

    def clear(n, _):
        out_ref[pl.ds(pl.multiple_of(n * step, step), step), :] = jnp.zeros((step, LANES), jnp.float32)
        return 0

    lax.fori_loop(0, out_ref.shape[0] // step, clear, 0)
    fetch.wait()
    depth = lax.broadcasted_iota(jnp.int32, (FIELDS, LANES), 1)

    def place(q, _):
        for p in range(FIELDS):
            s = q * FIELDS + p
            for start in range(0, cap, GROUP):
                where, news = [], []
                for i in range(start, min(cap, start + GROUP)):
                    word = code_ref[q, p * SPAN + i]
                    row = pl.ds(pl.multiple_of(lax.shift_right_logical(word, 7), FIELDS), FIELDS)
                    news.append(out_ref[row, :] + wide[i, pl.ds(pl.multiple_of(s * FIELDS, FIELDS), FIELDS), :])
                    column = jnp.bitwise_and(jnp.full((FIELDS, LANES), word, jnp.int32), LANES - 1)
                    where.append((row, depth == column))
                for (row, mask), new in zip(where, news):
                    pltpu.store(out_ref.at[row, :], new, mask=mask)
        return 0

    lax.fori_loop(0, devices // FIELDS, place, 0)


def scatter(cap, rows, codes, got):
    devices = got.shape[0]
    return pl.pallas_call(
        functools.partial(scatter_kernel, cap),
        out_shape=jax.ShapeDtypeStruct((rows * FIELDS, LANES), jnp.float32),
        in_specs=[pl.BlockSpec(memory_space=pltpu.VMEM)] * 2,
        out_specs=pl.BlockSpec(memory_space=pltpu.VMEM),
        scratch_shapes=[
            pltpu.SMEM(codes.shape, jnp.int32),
            pltpu.VMEM((devices * FIELDS, LANES), jnp.float32),
            pltpu.VMEM((devices * FIELDS, 2 * LANES), jnp.bfloat16),
            pltpu.VMEM((cap, devices * FIELDS, LANES), jnp.float32),
            pltpu.SemaphoreType.DMA,
        ],
        compiler_params=pltpu.CompilerParams(vmem_limit_bytes=24 * MIB),
        name="scatter",
    )(codes, got)


def share_kernel(
    nx, ny, state, src, fwd, both, grad, h_low, dn_put, up_put, up_got, lo_got, send, recv
):
    place = Place(nx, ny)
    e0, h1, decay, gain = parts_of(state)
    e, src1 = both.at[pl.ds(0, 3)], both.at[pl.ds(3, 3)]
    size_x, size_y, depth = grad.shape
    moves = shifts(size_y + 8, depth)
    barrier = pltpu.get_barrier_semaphore()
    others = greet(place, barrier, AROUND)

    def own(x):
        p = x + 2
        fade, rise = decay[p, :size_y], gain[p, :size_y]
        for c, curl in enumerate(curl_h(h1, p, moves)):
            source = src[c, x, pl.ds(0, size_y, stride=FIELDS), :]
            new = fade * e0[c, p, :size_y] + rise * (curl[:size_y] - source)
            e[c, p, :size_y] = new
            source = src[c, x, pl.ds(1, size_y, stride=FIELDS), :]
            src1[c, p, :size_y] = source
            for n, (array, comp, r) in enumerate(SHARE_DOWN):
                if comp == c:
                    dn_put[n, x] = (new, source)[array][r : r + 1]
            for n, (array, comp, r) in enumerate(SHARE_UP):
                if comp == c:
                    up_put[n, x] = (new, source)[array][size_y - 2 + r : size_y - 1 + r]

    sweep(0, size_x, own, 8)
    pl.semaphore_wait(barrier, others)
    halos = Exchange(
        place,
        row_copies(dn_put, up_put, up_got, lo_got, size_x)
        + plane_copies(both, 2, size_x, size_y),
        send,
        recv,
    )

    def product(x):
        total = fwd[0, 0, x].astype(jnp.float32) * e[0, x + 2, :size_y]
        for c in (1, 2):
            total = total + fwd[0, c, x].astype(jnp.float32) * e[c, x + 2, :size_y]
        grad[x] = total

    sweep(0, size_x, product, 4)

    low = h_low.shape[2]
    up_z, _, up_y, _ = shifts(size_y, depth)

    def h_second(x):
        new = h_rows(e, h1, x + 2, slice(0, size_y), time_step, up_z, lambda c, f: up_y(f))
        for c in range(3):
            h_low[c, x] = new[c][:low]

    sweep(0, size_x - 2, h_second, 6)
    halos.wait()
    for p in (0, 1, size_x + 2, size_x + 3):
        keep = place.plane(p, size_x)
        for c in range(3):
            e[c, p, :size_y] = jnp.where(keep, e[c, p, :size_y], 0.0)
            src1[c, p, :size_y] = jnp.where(keep, src1[c, p, :size_y], 0.0)

    def unstage(p):
        keep = place.plane(p, size_x)
        above, below = jnp.logical_and(keep, place.has(0, 1)), jnp.logical_and(keep, place.has(0, -1))
        gap = jnp.zeros((1, depth), jnp.float32)
        for array, field in enumerate((e, src1)):
            for c in range(3):
                field[c, p, size_y:] = halo_rows(
                    array, c, p, SHARE_DOWN, SHARE_UP, up_got, lo_got, above, below, gap
                )

    sweep(0, size_x + 4, unstage, 12)


def share(nx, ny, state, src, fwd):
    size_x, size_y, depth = fwd.shape[2:]
    wide, tall = size_x + 4, size_y + 8
    return pl.pallas_call(
        functools.partial(share_kernel, nx, ny),
        out_shape=[
            f32(6, wide, tall, depth),
            f32(size_x, size_y, depth),
            f32(3, size_x - 2, size_y - 8, depth),
        ],
        in_specs=in_vmem(3),
        out_specs=in_vmem(3),
        scratch_shapes=[
            *halo_scratch(SHARE_DOWN, SHARE_UP, size_x, depth),
            pltpu.SemaphoreType.DMA((8,)),
            pltpu.SemaphoreType.DMA((8,)),
        ],
        compiler_params=pltpu.CompilerParams(
            collective_id=1, has_side_effects=True, vmem_limit_bytes=6 * MIB
        ),
        name="share",
    )(state, src, fwd)


def finish_kernel(
    nx, ny, both, state, src, fwd, grad1, h_low, e_out, h_out, grad_out, e, h, grad, sem
):
    place = Place(nx, ny)
    e1, src1 = both.at[pl.ds(0, 3)], both.at[pl.ds(3, 3)]
    _, h1, decay, gain = parts_of(state)
    size_x, size_y, depth = grad1.shape
    rows = size_y + 8
    moves = shifts(rows, depth)
    factor = h_factor(place, size_y, rows, depth)

    low = h_low.shape[2]
    up_z = shifts(rows - low, depth)[0]
    last = lax.broadcasted_iota(jnp.int32, (rows - low, depth), 0) == rows - low - 1

    def h_second(x):
        p = x + 2

        def up_y(c, f):
            return jnp.where(last, e1[c, p, 0:1], pltpu.roll(f, rows - low - 1, 0))

        new = h_rows(e1, h1, p, slice(low, rows), factor[low:], up_z, up_y)
        for c in range(3):
            h[c, p, :low] = h_low[c, x]
            h[c, p, low:] = new[c]

    for p in (0, 1, size_x, size_x + 1, size_x + 2):
        h_plane(e1, h1, h, p, factor * jnp.where(place.plane(p, size_x), 1.0, 0.0), moves)
    sweep(0, size_x - 2, h_second, 10)

    def e_second(p, inner):
        fade, rise = decay[p], gain[p]
        total = None
        for c, curl in enumerate(curl_h(h, p, moves)):
            new = fade * e1[c, p] + rise * (curl - src1[c, p])
            e[c, p] = new
            if inner:
                term = fwd[1, c, p - 2].astype(jnp.float32) * new[:size_y]
                total = term if total is None else total + term
        if inner:
            grad[p - 2] = grad1[p - 2] + total

    e_second(1, False)

    def e_inner(p):
        e_second(p, True)

    sweep(2, size_x, e_inner, 16)
    e_second(size_x + 2, False)

    def h_third(p):
        h_plane(e, h, h, p, factor * jnp.where(place.plane(p, size_x), 1.0, 0.0), moves)

    sweep(1, size_x + 1, h_third, 11)
    inside = pl.ds(0, size_y)
    h_copy = pltpu.make_async_copy(h.at[:, pl.ds(2, size_x), inside], h_out, sem.at[0])
    h_copy.start()

    def e_third(x):
        p = x + 2
        fade, rise = decay[p, :size_y], gain[p, :size_y]
        total = grad[x]
        for c, curl in enumerate(curl_h(h, p, moves)):
            source = src[c, x, pl.ds(2, size_y, stride=FIELDS), :]
            new = fade * e[c, p, :size_y] + rise * (curl[:size_y] - source)
            e[c, p, :size_y] = new
            total = total + fwd[2, c, x].astype(jnp.float32) * new
        grad[x] = total

    each = size_x // PARTS

    def results(k):
        here = pl.ds(k * each, each)
        return (
            pltpu.make_async_copy(e.at[:, pl.ds(2 + k * each, each), inside], e_out.at[:, here], sem.at[1 + 2 * k]),
            pltpu.make_async_copy(grad.at[here], grad_out.at[here], sem.at[2 + 2 * k]),
        )

    def part(k, _):
        for x in range(each):
            e_third(k * each + x)
        for copy in results(k):
            copy.start()
        return 0

    lax.fori_loop(0, PARTS, part, 0)
    h_copy.wait()
    for k in range(PARTS):
        for copy in results(k):
            copy.wait()


def finish(nx, ny, both, state, src, fwd, grad1, h_low):
    size_x, size_y, depth = grad1.shape
    field = f32(3, size_x, size_y, depth)
    return pl.pallas_call(
        functools.partial(finish_kernel, nx, ny),
        out_shape=[field, field, f32(size_x, size_y, depth)],
        in_specs=in_vmem(6),
        out_specs=[pl.BlockSpec(memory_space=pltpu.HBM)] * 3,
        scratch_shapes=[
            pltpu.VMEM((3, *both.shape[1:]), jnp.float32),
            pltpu.VMEM((3, *both.shape[1:]), jnp.float32),
            pltpu.VMEM(grad1.shape, jnp.float32),
            pltpu.SemaphoreType.DMA((1 + 2 * PARTS,)),
        ],
        compiler_params=pltpu.CompilerParams(vmem_limit_bytes=10 * MIB),
        name="finish",
    )(both, state, src, fwd, grad1, h_low)


def per_device(
    e_adjoint,
    h_adjoint,
    conductivity,
    permittivity,
    forward_e,
    receiver_data,
    receiver_tile,
    receiver_cell,
    receiver_comp,
):
    _, size_x, size_y, depth = e_adjoint.shape
    nx, ny = lax.axis_size("gx"), lax.axis_size("gy")
    receivers = receiver_data.shape[0]
    cap = 3 * receivers // (nx * ny)
    by_lane = lambda a: a.reshape(receivers // LANES, LANES)
    got, codes, state = route(
        nx,
        ny,
        receiver_data,
        by_lane(receiver_tile),
        by_lane(receiver_cell),
        by_lane(receiver_comp),
        e_adjoint,
        h_adjoint,
        conductivity,
        permittivity,
    )
    placed = scatter(cap, 3 * size_x * size_y, codes, got)
    placed = placed.reshape(3, size_x, size_y * FIELDS, depth)
    both, grad1, h_low = share(nx, ny, state, placed, forward_e)
    return tuple(finish(nx, ny, both, state, placed, forward_e, grad1, h_low))


def solution(mesh):
    placed = (
        P(None, "gx", "gy", None),
        P(None, "gx", "gy", None),
        P("gx", "gy", None),
        P("gx", "gy", None),
        P(None, None, "gx", "gy", None),
        P(("gx", "gy"), None),
        P(("gx", "gy"), None),
        P(("gx", "gy")),
        P(("gx", "gy")),
    )
    return jax.shard_map(
        per_device,
        mesh=mesh,
        in_specs=placed,
        out_specs=(P(None, "gx", "gy", None), P(None, "gx", "gy", None), P("gx", "gy", None)),
        check_vma=False,
    )
```
